32 devices in a mesh: dp: 8 (over z, x), tensor: 4 (over y, core).
Axes of the slice: x: 2, y: 2, z: 4, core: 2. Of those that a mesh axis runs over, the one named last changes fastest.
Arguments:
- residual: bfloat16 [8, 2048, 1024], P('dp', 'tensor')
- teacher: bfloat16 [8, 2048, 1024], P('dp', 'tensor'), may hold values from -6 to 6
- valid_mask: int32 [8, 2048], P('dp', 'tensor'), may hold values from 0 to 1, as said below
- gain_in: float32 [1024], replicated, may hold values from 0.1 to 1.9
- w_z: bfloat16 [1024, 2048], P('dp', 'tensor'), may hold values from -0.1875 to 0.1875
- w_x: bfloat16 [1024, 2048], P('dp', 'tensor')
- w_bc: bfloat16 [1024, 256], P('dp'), may hold values from -0.1875 to 0.1875
- w_dt: bfloat16 [1024, 32], P('dp', 'tensor'), may hold values from -0.1875 to 0.1875
- conv_x: float32 [4, 2048], P(None, 'tensor'), may hold values from -3 to 3
- conv_bc: float32 [4, 256], replicated, may hold values from -3 to 3
- dt_bias: float32 [32], P('tensor'), may hold values from -6 to -2
- a_log: float32 [32], P('tensor'), may hold values from 0 to 2.77
- d_skip: float32 [32], P('tensor'), may hold values from 0.5 to 1.5
- gain_gate: float32 [2048], P('tensor'), may hold values from 0.1 to 1.9
- w_out: bfloat16 [1024, 2048], P('dp', 'tensor'), may hold values from -0.125 to 0.125
Outputs:
- mixed: bfloat16 [8, 2048, 1024], P('dp', 'tensor')
- loss: float32 [], replicated
- grad_residual: bfloat16 [8, 2048, 1024], P('dp', 'tensor')
- grad_gain_in: float32 [1024], replicated
- grad_w_z: float32 [1024, 2048], P('dp', 'tensor')
- grad_w_x: float32 [1024, 2048], P('dp', 'tensor')
- grad_w_bc: float32 [1024, 256], P('dp')
- grad_w_dt: float32 [1024, 32], P('dp', 'tensor')
- grad_conv_x: float32 [4, 2048], P(None, 'tensor')
- grad_conv_bc: float32 [4, 256], replicated
- grad_dt_bias: float32 [32], P('tensor')
- grad_a_log: float32 [32], P('tensor')
- grad_d_skip: float32 [32], P('tensor')
- grad_gain_gate: float32 [2048], P('tensor')
- grad_w_out: float32 [1024, 2048], P('dp', 'tensor')
The draws below stay inside these ranges and needn't reach their ends.
Inputs may be any that keep to these rules, and one draw needn't show every extreme that they name: `valid_mask`: 1 marks a token that counts in the loss; the first token of every sequence counts.
All inputs are finite; a program needn't handle non-finite values.
Results may differ from the reference program's by a relative error of at most 0.011.
Values may be sent and summed in bfloat16 or wider, within the bound.
No kernel may reach another device: no remote copies, remote signals or barrier semaphores. Data moves between devices by JAX's collectives and lax.ppermute only.
A program may use at most 192 MiB of HBM per device.

```python
import jax
import jax.numpy as jnp
from jax import lax

D = 1024
H = 32
HP = 64
NS = 128
KW = 4
BLOCK = 256
LEN = 2048
DI = 2048
SEQS = 8
TOKENS = 16384


def draw_residual(key, part):
    key = jax.random.fold_in(key, 11)
    sub_keys = jax.random.split(key, 3)
    row_scale = 10.0 ** jax.random.uniform(sub_keys[0], (SEQS, LEN, 1), jnp.float32, -0.5, 0.5)
    col_scale = 10.0 ** jax.random.uniform(sub_keys[1], (D,), jnp.float32, -0.5, 0.5)
    base_vals = jnp.clip(jax.random.normal(sub_keys[2], (SEQS, LEN, D), jnp.float32), -4.0, 4.0)
    return (base_vals * row_scale * col_scale).astype(jnp.bfloat16)


def draw_w_x(key, part):
    key = jax.random.fold_in(key, 23)
    sub_keys = jax.random.split(key, 1)
    col_pos = jnp.arange(DI, dtype=jnp.float32) / (DI - 1)
    col_scale = 10.0 ** (col_pos - 0.5)
    base_vals = jnp.clip(jax.random.normal(sub_keys[0], (D, DI), jnp.float32), -4.0, 4.0)
    return (base_vals * col_scale * D ** (-0.5)).astype(jnp.bfloat16)


def draw_valid_mask(key, part):
    key = jax.random.fold_in(key, 37)
    position = jnp.arange(SEQS * LEN, dtype=jnp.int32).reshape(SEQS, LEN)
    threshold = 250 + 700 * position // (SEQS * LEN)
    rolled = jax.random.randint(key, (SEQS, LEN), 0, 1000)
    chosen = jnp.where(rolled < threshold, 1, 0)
    first_pos = jnp.arange(LEN, dtype=jnp.int32)[None, :] == 0
    return jnp.where(first_pos, 1, chosen).astype(jnp.int32)


def shard_levels(stream_key, dims, cuts, smallest, largest):
    gain, own = 1.0, jax.random.fold_in(stream_key, 6)
    for dim, shards_of in cuts:
        draws = jnp.exp(jax.random.uniform(jax.random.fold_in(own, dim), (shards_of,), jnp.float32, smallest / len(cuts), largest / len(cuts)))
        gain = gain * jnp.repeat(draws, dims[dim] // shards_of).reshape([-1 if axis == dim else 1 for axis in range(len(dims))])
    return gain


def scatter_about(stream_key, shape, spread, limit, cuts=(), held_as=jnp.bfloat16):
    level = shard_levels(stream_key, shape, cuts, -0.22, 0.18) if cuts else 1.0
    drawn = jax.random.normal(stream_key, shape, jnp.float32) * spread * level
    return jnp.minimum(jnp.maximum(drawn, -limit), limit).astype(held_as)


def setup_inputs(seed: int = 0) -> dict:
    key_of = jax.random.split(jax.random.key(seed), 16)
    residual = draw_residual(jax.random.fold_in(key_of[15], 71), 0)
    teacher = scatter_about(key_of[1], (SEQS, LEN, D), 1.0, 6.0, ((0, 8), (1, 4)))
    valid_mask = draw_valid_mask(jax.random.fold_in(key_of[15], 71), 0)
    gain_in = jnp.clip(1.0 + 0.18 * jax.random.normal(key_of[3], (D,), jnp.float32), 0.1, 1.9)
    w_z = scatter_about(key_of[4], (D, DI), D ** -0.5, 0.1875, ((0, 8), (1, 4)))
    w_x = draw_w_x(jax.random.fold_in(key_of[15], 71), 0)
    w_bc = scatter_about(key_of[6], (D, 2 * NS), D ** -0.5, 0.1875, ((0, 8),))
    w_dt = scatter_about(key_of[7], (D, H), D ** -0.5, 0.1875, ((0, 8), (1, 4)))
    conv_x = scatter_about(key_of[8], (KW, DI), KW ** -0.5, 3.0, ((1, 4),), jnp.float32)
    conv_bc = scatter_about(key_of[9], (KW, 2 * NS), KW ** -0.5, 3.0, (), jnp.float32)
    dt_bias = jnp.clip(-6.0 + 4.0 * jax.random.uniform(key_of[10], (H,), jnp.float32) ** shard_levels(key_of[10], (H,), ((0, 4),), -0.2, 0.2), -6.0, -2.0)
    a_log = jnp.clip(2.77 * jax.random.uniform(key_of[11], (H,), jnp.float32) ** shard_levels(key_of[11], (H,), ((0, 4),), -0.2, 0.2), 0.0, 2.77)
    d_skip = jnp.clip(0.5 + 1.0 * jax.random.uniform(key_of[12], (H,), jnp.float32) ** shard_levels(key_of[12], (H,), ((0, 4),), -0.2, 0.2), 0.5, 1.5)
    gain_gate = jnp.clip(1.0 + 0.18 * jax.random.normal(key_of[13], (DI,), jnp.float32), 0.1, 1.9)
    w_out = scatter_about(key_of[14], (D, DI), DI ** -0.5, 0.125, ((0, 8), (1, 4)))
    return {"residual": residual, "teacher": teacher, "valid_mask": valid_mask, "gain_in": gain_in, "w_z": w_z, "w_x": w_x, "w_bc": w_bc, "w_dt": w_dt, "conv_x": conv_x, "conv_bc": conv_bc, "dt_bias": dt_bias, "a_log": a_log, "d_skip": d_skip, "gain_gate": gain_gate, "w_out": w_out}


EPSILON = 1e-05
HIGH = lax.Precision.HIGHEST

@jax.custom_vjp
def low(v):
    return lax.optimization_barrier(v.astype(jnp.bfloat16)).astype(jnp.float32)

@jax.custom_vjp
def low_back(v):
    return v

def low_keep(v):
    return (low(v), None)

def low_pass(kept, grad):
    return (grad,)

def back_keep(v):
    return (v, None)

def back_low(kept, grad):
    return (low(grad),)
low.defvjp(low_keep, low_pass)
low_back.defvjp(back_keep, back_low)

def hi_dot(left_mat, right_mat):
    return jnp.dot(left_mat, right_mat, precision=HIGH, preferred_element_type=jnp.float32)

def prenorm(values, gain_vec):
    return values * lax.rsqrt(lax.optimization_barrier(jnp.mean(values * values, axis=-1, keepdims=True)) + EPSILON) * gain_vec

def convolve(values, kernel):
    taps = kernel.shape[0]
    length = values.shape[1]
    padded = jnp.pad(values, ((0, 0), (taps - 1, 0), (0, 0)))
    summed = padded[:, 0:length] * kernel[0]
    for offset in range(1, taps):
        summed = summed + padded[:, offset:offset + length] * kernel[offset]
    return jax.nn.silu(summed)

def scan_heads(inputs, steps_dt, rates, b_proj, c_proj, block):
    length, n_heads, head_dim = inputs.shape
    n_blocks = length // block
    x_blocks = inputs.reshape(n_blocks, block, n_heads, head_dim)
    dt_blocks = steps_dt.reshape(n_blocks, block, n_heads)
    b_blocks = b_proj.reshape(n_blocks, block, b_proj.shape[-1])
    c_blocks = c_proj.reshape(n_blocks, block, c_proj.shape[-1])
    lower_tri = (jnp.arange(block)[:, None] >= jnp.arange(block)[None, :])[None]

    def advance(carried, pieces):
        x_now, dt_now, b_now, c_now = pieces
        cum_rate = jnp.cumsum(dt_now * rates, axis=0).T
        spread_ts = cum_rate[:, :, None] - cum_rate[:, None, :]
        weights = jnp.where(lower_tri, jnp.exp(jnp.where(lower_tri, spread_ts, 0.0)), 0.0)
        scores = jnp.dot(c_now, b_now.T, precision=HIGH)
        mixing = weights * scores[None] * dt_now.T[:, None, :]
        inner_part = jnp.einsum('hts,shp->thp', mixing, x_now, precision=HIGH)
        carried_part = jnp.einsum('tn,hpn->thp', c_now, carried, precision=HIGH) * jnp.exp(cum_rate).T[:, :, None]
        tail_w = jnp.exp(cum_rate[:, -1:] - cum_rate).T * dt_now
        fresh_state = jnp.einsum('shp,sn->hpn', x_now * tail_w[:, :, None], b_now, precision=HIGH)
        carried = carried * jnp.exp(cum_rate[:, -1])[:, None, None] + fresh_state
        return (carried, inner_part + carried_part)
    start_state = jnp.zeros((n_heads, head_dim, b_proj.shape[-1]), jnp.float32)
    _, outputs = lax.scan(jax.checkpoint(advance), start_state, (x_blocks, dt_blocks, b_blocks, c_blocks))
    return outputs.reshape(length, n_heads, head_dim)

def ssd_mixer(conv_x_out, conv_bc_out, gate_in, dt_in, dt_bias, a_log, d_skip):
    n_seqs, length, chans = conv_x_out.shape
    n_heads = chans // HP
    n_state = conv_bc_out.shape[-1] // 2
    steps_dt = jax.nn.softplus(dt_in + dt_bias)
    rates = -jnp.exp(a_log)
    heads_in = conv_x_out.reshape(n_seqs, length, n_heads, HP)

    def one_seq(seq_x, seq_dt, seq_b, seq_c):
        return scan_heads(seq_x, seq_dt, rates, seq_b, seq_c, BLOCK)
    scanned = jax.vmap(one_seq)(heads_in, steps_dt, conv_bc_out[..., :n_state], conv_bc_out[..., n_state:])
    scanned = scanned + d_skip[:, None] * heads_in
    return scanned.reshape(n_seqs, length, chans) * jax.nn.silu(gate_in)

def forward(upper, target, valid, count, params):
    gain_in, w_z, w_x, w_bc, w_dt, conv_x, conv_bc, dt_bias, a_log, d_skip, gain_gate, w_out = params
    n_seqs, length, width = upper.shape
    normed = low(prenorm(upper, gain_in))
    tok_rows = normed.reshape(n_seqs * length, width)
    gate_in = low_back(hi_dot(tok_rows, w_z)).reshape(n_seqs, length, -1)
    inner_in = low_back(hi_dot(tok_rows, w_x)).reshape(n_seqs, length, -1)
    dt_in = low_back(hi_dot(tok_rows, w_dt)).reshape(n_seqs, length, -1)
    bc_in = hi_dot(tok_rows, w_bc).reshape(n_seqs, length, -1)
    conv_x_out = low(convolve(inner_in, conv_x))
    conv_bc_out = low(convolve(bc_in, conv_bc))
    gated = ssd_mixer(conv_x_out, conv_bc_out, gate_in, dt_in, dt_bias, a_log, d_skip)
    normed_gate = low(gated * lax.rsqrt(lax.optimization_barrier(jnp.mean(gated * gated, axis=-1, keepdims=True)) + EPSILON) * gain_gate)
    branch = low_back(hi_dot(normed_gate.reshape(n_seqs * length, -1), w_out.T)).reshape(n_seqs, length, width)
    result = upper + branch
    error = result - target
    loss_term = jnp.sum(valid[..., None] * error * error) / (count * width)
    return (result, loss_term)

def reference(residual, teacher, valid_mask, gain_in, w_z, w_x, w_bc, w_dt, conv_x, conv_bc, dt_bias, a_log, d_skip, gain_gate, w_out):
    params = (gain_in.astype(jnp.float32), w_z.astype(jnp.float32), w_x.astype(jnp.float32), w_bc.astype(jnp.float32), w_dt.astype(jnp.float32), conv_x.astype(jnp.float32), conv_bc.astype(jnp.float32), dt_bias.astype(jnp.float32), a_log.astype(jnp.float32), d_skip.astype(jnp.float32), gain_gate.astype(jnp.float32), w_out.astype(jnp.float32))
    valid_all = valid_mask.astype(jnp.float32)
    count = jnp.sum(valid_all)
    loss_scale = jnp.asarray(TOKENS * D / 2.0, jnp.float32)

    def one_step(carry, item):
        upper, target, valid = item

        def run(upper_in, params_in):
            return forward(upper_in[None], target[None], valid[None], count, params_in)
        (result, loss_term), pull = jax.vjp(run, upper, params)
        grad_upper, grad_params = pull((jnp.zeros_like(result), loss_scale))
        loss_acc, grad_acc = carry
        grad_acc = jax.tree.map(lambda first_g, second_g: first_g + second_g, grad_acc, grad_params)
        return ((loss_acc + loss_term, grad_acc), (result[0].astype(jnp.bfloat16), grad_upper.astype(jnp.bfloat16)))
    start_carry = (jnp.zeros((), jnp.float32), jax.tree.map(jnp.zeros_like, params))
    (loss, grads), (mixed, grad_residual) = lax.scan(one_step, start_carry, (residual.astype(jnp.float32), teacher.astype(jnp.float32), valid_all))
    return (mixed, loss, grad_residual, grads[0], grads[1], grads[2], grads[3], grads[4], grads[5], grads[6], grads[7], grads[8], grads[9], grads[10], grads[11])
```

```python
import functools

import jax
import jax.numpy as jnp
from jax import lax
from jax.experimental import pallas as pl
from jax.experimental.pallas import tpu as pltpu
from jax.sharding import PartitionSpec as P

HP = 64
BLOCK = 256
EPSILON = 1e-05
HEADS_PAD = 128
HALO = 16
BF = jnp.bfloat16
F32 = jnp.float32
HIGH = lax.Precision.HIGHEST
VMEM_LIMIT = 56 * 1024 * 1024
AXES = ("dp", "tensor")


def dot_nn(left, right):
    return lax.dot_general(left, right, (((1,), (0,)), ((), ())), preferred_element_type=F32)


def dot_nt(left, right):
    return lax.dot_general(left, right, (((1,), (1,)), ((), ())), preferred_element_type=F32)


def dot_tn(left, right):
    return lax.dot_general(left, right, (((0,), (0,)), ((), ())), preferred_element_type=F32)


def split_low(values):
    high = values.astype(BF)
    return high, (values - high.astype(F32)).astype(BF)


def by_expansion(values, spread_mat):
    high, rest = split_low(values)
    return dot_nn(high, spread_mat) + dot_nn(rest, spread_mat)


def per_head(values, spread_mat):
    high, rest = split_low(values)
    return dot_nt(high, spread_mat) + dot_nt(rest, spread_mat)


def sigmoid(values):
    return 1.0 / (1.0 + jnp.exp(-values))


def call(kernel, grid, in_specs, out_specs, out_shape, scratch=(), prefetch=0, flops=0, nbytes=0):
    return pl.pallas_call(
        kernel,
        grid_spec=pltpu.PrefetchScalarGridSpec(
            num_scalar_prefetch=prefetch,
            grid=grid,
            in_specs=in_specs,
            out_specs=out_specs,
            scratch_shapes=list(scratch),
        ),
        out_shape=out_shape,
        compiler_params=pltpu.CompilerParams(
            dimension_semantics=("arbitrary",) * len(grid), vmem_limit_bytes=VMEM_LIMIT
        ),
        cost_estimate=pl.CostEstimate(flops=flops, bytes_accessed=nbytes, transcendentals=0),
    )


def whole(shape):
    rank = len(shape)
    return pl.BlockSpec(shape, lambda *_: (0,) * rank, pipeline_mode=pl.Buffered(1))


def rows(block, width):
    return pl.BlockSpec((block, width), lambda i, *_: (i, 0))


def out(shape, dtype):
    return jax.ShapeDtypeStruct(shape, dtype)


def front_kernel(
    n_ref, halo_ref, wx_ref, wbc_ref, wdt_ref, cx_ref, cbc_ref, bias_ref, rate_ref, spread_ref,
    xin_ref, xc_ref, bcin_ref, bcc_ref, dt_ref, a_ref, ag_ref, sig_ref, at_ref, state_ref,
    xs, bs, before,
):
    step = pl.program_id(0)
    block = n_ref.shape[0]
    chans = wx_ref.shape[1]
    bcw = wbc_ref.shape[1]
    n_state = bcw // 2

    @pl.when(step == 0)
    def _():
        halo_x = dot_nn(halo_ref[...], wx_ref[...])
        halo_bc = dot_nn(halo_ref[...], wbc_ref[...])
        xs[0:8, :] = halo_x[8:16]
        bs[0:8, :] = halo_bc[8:16]
        before[...] = jnp.zeros_like(before)
        state_ref[...] = jnp.zeros_like(state_ref)

    @pl.when(step > 0)
    def _():
        xs[0:8, :] = xs[block : block + 8, :]
        bs[0:8, :] = bs[block : block + 8, :]

    n_now = n_ref[...]
    xs[8 : block + 8, :] = dot_nn(n_now, wx_ref[...])
    bs[8 : block + 8, :] = dot_nn(n_now, wbc_ref[...])
    xin_ref[...] = xs[8 : block + 8, :].astype(BF)
    bcin_ref[...] = bs[8 : block + 8, :].astype(BF)
    dt_raw = dot_nt(wdt_ref[...], n_now) + bias_ref[...]
    tail = jnp.exp(-jnp.abs(dt_raw))
    log_part = jnp.where(
        tail < 0.01, tail * (1.0 - tail * (0.5 - tail * (1.0 / 3.0))), jnp.log(1.0 + tail)
    )
    dt_t = jnp.maximum(dt_raw, 0.0) + log_part
    row_i = lax.broadcasted_iota(jnp.int32, (block, block), 0)
    col_i = lax.broadcasted_iota(jnp.int32, (block, block), 1)
    upto = jnp.where(row_i <= col_i, 1.0, 0.0).astype(F32)
    a_t = jnp.dot(dt_t * rate_ref[...], upto, precision=HIGH, preferred_element_type=F32)
    at_ref[...] = a_t[0 : at_ref.shape[0]]
    a_now = a_t.T
    dt_now = dt_t.T
    a_ref[...] = a_now
    dt_ref[...] = dt_now
    sig_ref[...] = sigmoid(dt_raw.T)
    ag_ref[...] = a_now + before[0:1]
    a_last = a_now[block - 1 : block]
    before[...] = before[...] + a_last
    for col in range(0, bcw, 128):
        pre = bs[5 : block + 5, col : col + 128] * cbc_ref[0:1, col : col + 128]
        for k in range(1, 4):
            pre += bs[5 + k : block + 5 + k, col : col + 128] * cbc_ref[k : k + 1, col : col + 128]
        bcc_ref[:, col : col + 128] = (pre * sigmoid(pre)).astype(BF)
    for col in range(0, chans, 128):
        pre = xs[5 : block + 5, col : col + 128] * cx_ref[0:1, col : col + 128]
        for k in range(1, 4):
            pre += xs[5 + k : block + 5 + k, col : col + 128] * cx_ref[k : k + 1, col : col + 128]
        xc_ref[:, col : col + 128] = (pre * sigmoid(pre)).astype(BF)
    spread = spread_ref[...]
    weight = by_expansion(dt_now * jnp.exp(a_last - a_now), spread)
    weighted = (xc_ref[...].astype(F32) * weight).astype(BF)
    decay = by_expansion(jnp.broadcast_to(jnp.exp(a_last), (8, HEADS_PAD)), spread)
    state_ref[...] = state_ref[...] * decay[0:1] + dot_tn(bcc_ref[:, 0:n_state], weighted)


def front(n_full, halo, wx, wbc, wdt, conv_x, conv_bc, bias, rate, spread):
    toks, width = n_full.shape
    chans = wx.shape[1]
    bcw = wbc.shape[1]
    n_state = bcw // 2
    heads = chans // HP
    nb = toks // BLOCK
    return call(
        front_kernel,
        (nb,),
        [
            rows(BLOCK, width), whole(halo.shape), whole(wx.shape), whole(wbc.shape),
            whole(wdt.shape), whole(conv_x.shape), whole(conv_bc.shape), whole(bias.shape),
            whole(rate.shape), whole(spread.shape),
        ],
        [
            rows(BLOCK, chans), rows(BLOCK, chans), rows(BLOCK, bcw), rows(BLOCK, bcw),
            rows(BLOCK, HEADS_PAD), rows(BLOCK, HEADS_PAD), rows(BLOCK, HEADS_PAD),
            rows(BLOCK, HEADS_PAD), pl.BlockSpec((heads, BLOCK), lambda i: (0, i)),
            whole((n_state, chans)),
        ],
        [
            out((toks, chans), BF), out((toks, chans), BF), out((toks, bcw), BF),
            out((toks, bcw), BF), out((toks, HEADS_PAD), F32), out((toks, HEADS_PAD), F32),
            out((toks, HEADS_PAD), F32), out((toks, HEADS_PAD), F32), out((heads, toks), F32),
            out((n_state, chans), F32),
        ],
        [
            pltpu.VMEM((BLOCK + 8, chans), F32), pltpu.VMEM((BLOCK + 8, bcw), F32),
            pltpu.VMEM((8, HEADS_PAD), F32),
        ],
        flops=2 * toks * width * (chans + bcw), nbytes=8 * toks * chans,
    )(n_full, halo, wx, wbc, wdt, conv_x, conv_bc, bias, rate, spread)


def scan_kernel(
    xc_ref, bcc_ref, dt_ref, a_ref, at_ref, start_ref, spread_ref, y_ref, saved_ref, xt, state
):
    step = pl.program_id(0)
    block, chans = xc_ref.shape
    n_state = bcc_ref.shape[1] // 2
    half = block // 2

    @pl.when(step == 0)
    def _():
        state[...] = start_ref[...].astype(F32)

    spread = spread_ref[...]
    b_now = bcc_ref[:, 0:n_state]
    c_now = bcc_ref[:, n_state:]
    a_now = a_ref[...]
    a_last = a_now[block - 1 : block]
    state_low = state[...].astype(BF)
    saved_ref[0] = state_low
    xt[...] = (xc_ref[...].astype(F32) * by_expansion(dt_ref[...], spread)).astype(BF)
    y_ref[...] = dot_nn(c_now, state_low) * by_expansion(jnp.exp(a_now), spread)
    scores = dot_nt(c_now, b_now)
    row_i = lax.broadcasted_iota(jnp.int32, (half, half), 0)
    col_i = lax.broadcasted_iota(jnp.int32, (half, half), 1)
    shut = jnp.where(row_i >= col_i, 0.0, -1e30).astype(F32)
    lane = lax.broadcasted_iota(jnp.int32, (half, 128), 1)
    for pair in range(chans // 128):
        cols = slice(pair * 128, pair * 128 + 128)
        x_pair = xt[:, cols]
        tops, lows = [], []
        for sub in range(2):
            h = pair * 2 + sub
            a_row = at_ref[h : h + 1, :]
            a_top = a_now[0:half, h : h + 1]
            a_low = a_now[half:block, h : h + 1]
            m_top = jnp.exp(a_top - a_row[:, 0:half] + shut) * scores[0:half, 0:half]
            m_left = jnp.exp(a_low - a_row[:, 0:half]) * scores[half:block, 0:half]
            m_low = jnp.exp(a_low - a_row[:, half:block] + shut) * scores[half:block, half:block]
            tops.append(dot_nn(m_top.astype(BF), x_pair[0:half]))
            lows.append(
                dot_nn(jnp.concatenate([m_left.astype(BF), m_low.astype(BF)], axis=1), x_pair)
            )
        y_ref[0:half, cols] += jnp.where(lane < HP, tops[0], tops[1])
        y_ref[half:block, cols] += jnp.where(lane < HP, lows[0], lows[1])
    tail = by_expansion(jnp.exp(a_last - a_now), spread)
    decay = by_expansion(jnp.broadcast_to(jnp.exp(a_last), (8, HEADS_PAD)), spread)
    state[...] = state[...] * decay[0:1] + dot_tn(
        b_now, (xt[...].astype(F32) * tail).astype(BF)
    )
    saved_ref[1] = state[...].astype(BF)


def scan_forward(xc, bcc, dt, a_cols, a_rows, start, spread):
    toks, chans = xc.shape
    bcw = bcc.shape[1]
    n_state = bcw // 2
    heads = chans // HP
    nb = toks // BLOCK
    return call(
        scan_kernel,
        (nb,),
        [
            rows(BLOCK, chans), rows(BLOCK, bcw), rows(BLOCK, HEADS_PAD), rows(BLOCK, HEADS_PAD),
            pl.BlockSpec((heads, BLOCK), lambda i: (0, i)), whole(start.shape),
            whole(spread.shape),
        ],
        [rows(BLOCK, chans), pl.BlockSpec((2, n_state, chans), lambda i: (i, 0, 0))],
        [out((toks, chans), F32), out((2 * nb, n_state, chans), BF)],
        [pltpu.VMEM((BLOCK, chans), BF), pltpu.VMEM((n_state, chans), F32)],
        flops=2 * toks * BLOCK * chans * 2, nbytes=10 * toks * chans,
    )(xc, bcc, dt, a_cols, a_rows, start, spread)


def gate_kernel(
    where_ref, n_ref, y_ref, xc_ref, wz_ref, wo_ref, skip_ref, gain_ref,
    gate_out, u_ref, far_ref, near_ref, sq_ref,
):
    step = pl.program_id(0)
    chans = y_ref.shape[1]
    n_now = n_ref[...]
    squares = jnp.zeros((n_now.shape[0], 128), F32)
    for col in range(0, chans, 256):
        cols = slice(col, col + 256)
        gate = dot_nn(n_now, wz_ref[:, cols])
        gated = (y_ref[:, cols] + skip_ref[:, cols] * xc_ref[:, cols].astype(F32)) * (
            gate * sigmoid(gate)
        )
        gate_out[:, cols] = gate.astype(BF)
        u_ref[:, cols] = (gated * gain_ref[:, cols]).astype(BF)
        sq = gated * gated
        squares += sq[:, 0:128] + sq[:, 128:256]
    sq_ref[...] = jnp.broadcast_to(jnp.sum(squares, axis=1, keepdims=True), squares.shape)
    part = dot_nt(u_ref[...], wo_ref[...])

    @pl.when(step < 2)
    def _():
        far_ref[...] = part.astype(BF)

    @pl.when(step >= 2)
    def _():
        near_ref[...] = part


def gate_out_proj(place, n_full, y, xc, wz, wo, skip_row, gain_row):
    toks, width = n_full.shape
    chans = wz.shape[1]
    nb = toks // BLOCK

    def spot(i, where):
        return (((i // 2) + 1 - where[3]) % 2) * 2 + i % 2

    def moved(w):
        return pl.BlockSpec((BLOCK, w), lambda i, where: (spot(i, where), 0))

    return call(
        gate_kernel,
        (nb,),
        [
            moved(width), moved(chans), moved(chans), whole(wz.shape), whole(wo.shape),
            whole(skip_row.shape), whole(gain_row.shape),
        ],
        [
            moved(chans), moved(chans),
            pl.BlockSpec((BLOCK, width), lambda i, where: (jnp.minimum(i, 1), 0)),
            pl.BlockSpec((BLOCK, width), lambda i, where: (jnp.maximum(i - 2, 0), 0)),
            pl.BlockSpec((BLOCK, 128), lambda i, where: (i, 0)),
        ],
        [
            out((toks, chans), BF), out((toks, chans), BF), out((toks // 2, width), BF),
            out((toks // 2, width), F32), out((toks, 128), F32),
        ],
        prefetch=1, flops=4 * toks * width * chans, nbytes=14 * toks * chans,
    )(place, n_full, y, xc, wz, wo, skip_row, gain_row)


def loss_kernel(
    near_ref, got_ref, sq_ref, sqgot_ref, res_ref, teach_ref, valid_ref, scale_ref,
    mixed_ref, gres_ref, gs_ref, q_ref, loss_ref, *, inner,
):
    @pl.when(pl.program_id(0) == 0)
    def _():
        loss_ref[...] = jnp.zeros_like(loss_ref)

    total = sq_ref[:, 0:1] + sqgot_ref[:, 0:1]
    factor = lax.rsqrt(total / inner + EPSILON)
    branch = near_ref[...] + got_ref[...].astype(F32)
    result = res_ref[...].astype(F32) + factor * branch
    mixed_ref[...] = result.astype(BF)
    error = result - teach_ref[...].astype(F32)
    valid = valid_ref[...]
    terms = jnp.sum((valid * error * error).reshape(-1, 8, error.shape[1]), axis=0)
    for col in range(0, error.shape[1], 128):
        loss_ref[...] += terms[:, col : col + 128]
    grad = (valid * scale_ref[0:1, 0:1]) * error
    gres_ref[...] = grad
    gs = (grad * factor).astype(BF)
    gs_ref[...] = gs
    prods = jnp.sum(gs.astype(F32) * branch, axis=1, keepdims=True)
    q_ref[...] = jnp.broadcast_to(prods * factor * factor / inner, q_ref.shape)


def loss_step(near, got, sq, sqgot, residual, teacher, valid_col, scale, inner):
    toks, width = near.shape
    nb = toks // BLOCK
    return call(
        functools.partial(loss_kernel, inner=inner),
        (nb,),
        [
            rows(BLOCK, width), rows(BLOCK, width), rows(BLOCK, 128), rows(BLOCK, 128),
            rows(BLOCK, width), rows(BLOCK, width), rows(BLOCK, 1), whole(scale.shape),
        ],
        [
            rows(BLOCK, width), rows(BLOCK, width), rows(BLOCK, width), rows(BLOCK, 128),
            whole((8, 128)),
        ],
        [
            out((toks, width), BF), out((toks, width), F32), out((toks, width), BF),
            out((toks, 128), F32), out((8, 128), F32),
        ],
        nbytes=20 * toks * width,
    )(near, got, sq, sqgot, residual, teacher, valid_col, scale)


def gate_back_kernel(
    gs_ref, q_ref, wo_ref, y_ref, xc_ref, gate_ref, ag_ref, c_ref, skip_ref, gain_ref, spread_ref,
    dz_ref, dy_ref, rowdot_ref, dstart_ref, dgain_ref, dskip_ref, dyf,
):
    @pl.when(pl.program_id(0) == 0)
    def _():
        dstart_ref[...] = jnp.zeros_like(dstart_ref)
        dgain_ref[...] = jnp.zeros_like(dgain_ref)
        dskip_ref[...] = jnp.zeros_like(dskip_ref)

    chans = y_ref.shape[1]
    n_state = c_ref.shape[1]
    q_now = q_ref[:, 0:1]
    gs = gs_ref[...]
    for col in range(0, chans, 256):
        cols = slice(col, col + 256)
        grad = dot_nn(gs, wo_ref[:, cols])
        gate = gate_ref[:, cols].astype(F32)
        sig = sigmoid(gate)
        silu = gate * sig
        x_now = xc_ref[:, cols].astype(F32)
        y_now = y_ref[:, cols]
        mixed = y_now + skip_ref[:, cols] * x_now
        gated = mixed * silu
        dgain_ref[:, cols] += jnp.sum((grad * gated).reshape(-1, 8, 256), axis=0)
        dgated = grad * gain_ref[:, cols] - gated * q_now
        dz_ref[:, cols] = (dgated * mixed * (sig * (1.0 + gate * (1.0 - sig)))).astype(BF)
        dy = (dgated * silu).astype(BF)
        dy_ref[:, cols] = dy
        dy32 = dy.astype(F32)
        dskip_ref[:, cols] += jnp.sum((dy32 * x_now).reshape(-1, 8, 256), axis=0)
        dyf[:, cols] = dy32 * y_now
    spread = spread_ref[...]
    rowdot_ref[...] = per_head(dyf[...], spread)
    scaled = (dy_ref[...].astype(F32) * by_expansion(jnp.exp(ag_ref[...]), spread)).astype(BF)
    dstart_ref[...] += dot_tn(c_ref[...], scaled)


def gate_backward(gs, q, wo, y, xc, gate, ag, bcc, skip_row, gain_row, spread):
    toks, width = gs.shape
    chans = wo.shape[1]
    n_state = bcc.shape[1] // 2
    nb = toks // BLOCK
    return call(
        gate_back_kernel,
        (nb,),
        [
            rows(BLOCK, width), rows(BLOCK, 128), whole(wo.shape), rows(BLOCK, chans),
            rows(BLOCK, chans), rows(BLOCK, chans), rows(BLOCK, HEADS_PAD),
            pl.BlockSpec((BLOCK, n_state), lambda i: (i, 1)), whole(skip_row.shape),
            whole(gain_row.shape), whole(spread.shape),
        ],
        [
            rows(BLOCK, chans), rows(BLOCK, chans), rows(BLOCK, HEADS_PAD),
            whole((n_state, chans)), whole((8, chans)), whole((8, chans)),
        ],
        [
            out((toks, chans), BF), out((toks, chans), BF), out((toks, HEADS_PAD), F32),
            out((n_state, chans), F32), out((8, chans), F32), out((8, chans), F32),
        ],
        [pltpu.VMEM((BLOCK, chans), F32)],
        flops=2 * toks * width * chans, nbytes=14 * toks * chans,
    )(gs, q, wo, y, xc, gate, ag, bcc, skip_row, gain_row, spread)


def scan_back_kernel(
    xc_ref, bcc_ref, dt_ref, a_ref, at_ref, sig_ref, dy_ref, rowdot_ref, saved_ref, xin_ref,
    bcin_ref, dend_ref, cx_ref, cbc_ref, skip_ref, rate_ref, spread_ref,
    dxin_ref, dbc_ref, ddt_ref, dxh_ref, dbch_ref, dcx_ref, dcbc_ref, dhead_ref,
    xt, dstate, dxt, xs, bs, dxp, dbp, dbco,
):
    step = pl.program_id(0)
    block, chans = xc_ref.shape
    bcw = bcc_ref.shape[1]
    n_state = bcw // 2
    half = block // 2
    toks = bcin_ref.shape[0] - HALO

    @pl.when(step == 0)
    def _():
        dstate[...] = dend_ref[...].astype(F32)
        dxp[block : block + 8, :] = jnp.zeros((8, chans), F32)
        dbp[block : block + 8, :] = jnp.zeros((8, bcw), F32)
        dcx_ref[...] = jnp.zeros_like(dcx_ref)
        dcbc_ref[...] = jnp.zeros_like(dcbc_ref)
        dhead_ref[...] = jnp.zeros_like(dhead_ref)

    @pl.when(step > 0)
    def _():
        dxp[block : block + 8, :] = dxp[0:8, :]
        dbp[block : block + 8, :] = dbp[0:8, :]

    spread = spread_ref[...]
    b_now = bcc_ref[:, 0:n_state]
    c_now = bcc_ref[:, n_state:]
    a_now = a_ref[...]
    dt_now = dt_ref[...]
    a_last = a_now[block - 1 : block]
    dt_wide = by_expansion(dt_now, spread)
    xt[...] = (xc_ref[...].astype(F32) * dt_wide).astype(BF)
    tail = by_expansion(jnp.exp(a_last - a_now), spread)
    dstate_low = dstate[...].astype(BF)
    dxt[...] = dot_nn(b_now, dstate_low) * tail
    scores = dot_nt(b_now, c_now)
    row_i = lax.broadcasted_iota(jnp.int32, (half, half), 0)
    col_i = lax.broadcasted_iota(jnp.int32, (half, half), 1)
    shut = jnp.where(row_i <= col_i, 0.0, -1e30).astype(F32)
    lane = lax.broadcasted_iota(jnp.int32, (half, 128), 1)
    lane_full = lax.broadcasted_iota(jnp.int32, (block, 128), 1)
    g_top = jnp.zeros((half, block), F32)
    g_low = jnp.zeros((half, half), F32)
    for pair in range(chans // 128):
        cols = slice(pair * 128, pair * 128 + 128)
        x_pair = xt[:, cols]
        dy_pair = dy_ref[:, cols]
        tops, lows = [], []
        for sub in range(2):
            h = pair * 2 + sub
            mine = (lane_full < HP) if sub == 0 else (lane_full >= HP)
            x_mine = jnp.where(mine, x_pair, jnp.zeros_like(x_pair))
            a_row = at_ref[h : h + 1, :]
            a_top = a_now[0:half, h : h + 1]
            a_low = a_now[half:block, h : h + 1]
            w_top = jnp.exp(a_row[:, 0:half] - a_top + shut)
            w_right = jnp.exp(a_row[:, half:block] - a_top)
            w_low = jnp.exp(a_row[:, half:block] - a_low + shut)
            w_upper = jnp.concatenate([w_top, w_right], axis=1)
            m_upper = (w_upper * scores[0:half]).astype(BF)
            m_low = (w_low * scores[half:block, half:block]).astype(BF)
            tops.append(dot_nn(m_upper, dy_pair))
            lows.append(dot_nn(m_low, dy_pair[half:block]))
            g_top += w_upper * dot_nt(x_mine[0:half], dy_pair)
            g_low += w_low * dot_nt(x_mine[half:block], dy_pair[half:block])
        dxt[0:half, cols] += jnp.where(lane < HP, tops[0], tops[1])
        dxt[half:block, cols] += jnp.where(lane < HP, lows[0], lows[1])
    g_top = g_top.astype(BF)
    g_low = g_low.astype(BF)
    dy_wide = (dy_ref[...].astype(F32) * by_expansion(jnp.exp(a_now), spread)).astype(BF)
    x_tail = (xt[...].astype(F32) * tail).astype(BF)
    d_b = dot_nt(x_tail, dstate_low)
    d_c = dot_nt(dy_wide, saved_ref[0])
    dbco[0:half, 0:n_state] = d_b[0:half] + dot_nn(g_top, c_now)
    dbco[half:block, 0:n_state] = d_b[half:block] + dot_nn(g_low, c_now[half:block])
    d_c_top = dot_tn(g_top, b_now[0:half])
    dbco[0:half, n_state:] = d_c[0:half] + d_c_top[0:half]
    dbco[half:block, n_state:] = (
        d_c[half:block] + d_c_top[half:block] + dot_tn(g_low, b_now[half:block])
    )
    coldot = per_head(dxt[...] * xt[...].astype(F32), spread)
    direct = per_head(dxt[...] * xc_ref[...].astype(F32), spread)
    ends = jnp.sum(dstate[...] * saved_ref[1].astype(F32), axis=0, keepdims=True)
    ends = per_head(jnp.broadcast_to(ends, (8, chans)), spread)
    row_k = lax.broadcasted_iota(jnp.int32, (block, HEADS_PAD), 0)
    d_a = rowdot_ref[...] - coldot + jnp.where(row_k == block - 1, ends[0:1], 0.0)
    row_b = lax.broadcasted_iota(jnp.int32, (block, block), 0)
    col_b = lax.broadcasted_iota(jnp.int32, (block, block), 1)
    onward = jnp.where(row_b <= col_b, 1.0, 0.0).astype(F32)
    d_step = jnp.dot(onward, d_a, precision=HIGH, preferred_element_type=F32)
    rate = rate_ref[0:1, :]
    d_raw = (direct + rate * d_step) * sig_ref[...]
    ddt_ref[...] = d_raw.astype(BF)
    dhead_ref[0:8, :] += jnp.sum(d_raw.reshape(-1, 8, HEADS_PAD), axis=0)
    dhead_ref[8:16, :] += jnp.sum((dt_now * d_step * rate).reshape(-1, 8, HEADS_PAD), axis=0)
    decay = by_expansion(jnp.broadcast_to(jnp.exp(a_last), (8, HEADS_PAD)), spread)
    dstate[...] = dstate[...] * decay[0:1] + dot_tn(c_now, dy_wide)
    first = pl.multiple_of(toks - (step + 1) * block, block)
    last = step == pl.num_programs(0) - 1
    bs[...] = bcin_ref[pl.ds(first, block + HALO), :].astype(F32)
    off = HALO - 3
    for col in range(0, bcw, 128):
        cols = slice(col, col + 128)
        pre = bs[off : off + block, cols] * cbc_ref[0:1, cols]
        for k in range(1, 4):
            pre += bs[off + k : off + k + block, cols] * cbc_ref[k : k + 1, cols]
        sig = sigmoid(pre)
        dpre = dbco[:, cols] * (sig * (1.0 + pre * (1.0 - sig)))
        dbp[0:block, cols] = dpre
        for k in range(4):
            dcbc_ref[8 * k : 8 * k + 8, cols] += jnp.sum(
                (dpre * bs[off + k : off + k + block, cols]).reshape(-1, 8, 128), axis=0
            )
        back = dbp[3 : 3 + block, cols] * cbc_ref[0:1, cols]
        for k in range(1, 4):
            back += dbp[3 - k : 3 - k + block, cols] * cbc_ref[k : k + 1, cols]
        dbc_ref[:, cols] = back.astype(BF)
    for col in range(0, chans, 128):
        cols = slice(col, col + 128)
        xs[...] = xin_ref[pl.ds(first, block + HALO), cols].astype(F32)
        pre = xs[off : off + block] * cx_ref[0:1, cols]
        for k in range(1, 4):
            pre += xs[off + k : off + k + block] * cx_ref[k : k + 1, cols]
        sig = sigmoid(pre)
        grad = dxt[:, cols] * dt_wide[:, cols] + skip_ref[:, cols] * dy_ref[:, cols].astype(F32)
        dpre = grad * (sig * (1.0 + pre * (1.0 - sig)))
        dxp[0:block, cols] = dpre
        for k in range(4):
            dcx_ref[8 * k : 8 * k + 8, cols] += jnp.sum(
                (dpre * xs[off + k : off + k + block]).reshape(-1, 8, 128), axis=0
            )
        back = dxp[3 : 3 + block, cols] * cx_ref[0:1, cols]
        for k in range(1, 4):
            back += dxp[3 - k : 3 - k + block, cols] * cx_ref[k : k + 1, cols]
        dxin_ref[:, cols] = back.astype(BF)

    @pl.when(last)
    def _():
        row_h = lax.broadcasted_iota(jnp.int32, (HALO, 1), 0)
        for src, taps, dest in ((dxp, cx_ref, dxh_ref), (dbp, cbc_ref, dbch_ref)):
            head = src[0:8, :]
            acc = jnp.zeros((HALO, src.shape[1]), F32)
            for t in range(3):
                total = taps[0:1, :] * head[t : t + 1]
                for k in range(1, t + 1):
                    total = total + taps[k : k + 1, :] * head[t - k : t - k + 1]
                acc = acc + jnp.where(row_h == HALO - 3 + t, total, 0.0)
            dest[...] = acc.astype(BF)


def scan_backward(
    xc, bcc, dt, a_cols, a_rows, sig, dy, rowdot, saved, xin_ext, bcin_ext, dend, conv_x, conv_bc,
    skip_row, rate_row, spread,
):
    toks, chans = xc.shape
    bcw = bcc.shape[1]
    n_state = bcw // 2
    heads = chans // HP
    nb = toks // BLOCK

    def back(width):
        return pl.BlockSpec((BLOCK, width), lambda i: (nb - 1 - i, 0))

    return call(
        scan_back_kernel,
        (nb,),
        [
            back(chans), back(bcw), back(HEADS_PAD), back(HEADS_PAD),
            pl.BlockSpec((heads, BLOCK), lambda i: (0, nb - 1 - i)), back(HEADS_PAD),
            back(chans), back(HEADS_PAD),
            pl.BlockSpec((2, n_state, chans), lambda i: (nb - 1 - i, 0, 0)),
            whole(xin_ext.shape), whole(bcin_ext.shape), whole(dend.shape),
            whole(conv_x.shape), whole(conv_bc.shape), whole(skip_row.shape),
            whole(rate_row.shape), whole(spread.shape),
        ],
        [
            back(chans), back(bcw), back(HEADS_PAD), whole((HALO, chans)), whole((HALO, bcw)),
            whole((32, chans)), whole((32, bcw)), whole((16, HEADS_PAD)),
        ],
        [
            out((toks, chans), BF), out((toks, bcw), BF), out((toks, HEADS_PAD), BF),
            out((HALO, chans), BF), out((HALO, bcw), BF), out((32, chans), F32),
            out((32, bcw), F32), out((16, HEADS_PAD), F32),
        ],
        [
            pltpu.VMEM((BLOCK, chans), BF), pltpu.VMEM((n_state, chans), F32),
            pltpu.VMEM((BLOCK, chans), F32), pltpu.VMEM((BLOCK + HALO, 128), F32),
            pltpu.VMEM((BLOCK + HALO, bcw), F32), pltpu.VMEM((BLOCK + 8, chans), F32),
            pltpu.VMEM((BLOCK + 8, bcw), F32), pltpu.VMEM((BLOCK, bcw), F32),
        ],
        flops=2 * toks * BLOCK * chans * 4, nbytes=16 * toks * chans,
    )(
        xc, bcc, dt, a_cols, a_rows, sig, dy, rowdot, saved, xin_ext, bcin_ext, dend, conv_x,
        conv_bc, skip_row, rate_row, spread,
    )


def input_grad_kernel(
    where_ref, dz_ref, dx_ref, dbc_ref, ddt_ref, add_ref, wz_ref, wx_ref, wbc_ref, wdt_ref,
    far_ref, near_ref,
):
    step = pl.program_id(0)
    part = dot_nt(dz_ref[...], wz_ref[...])
    part += dot_nt(dx_ref[...], wx_ref[...])
    part += dot_nt(dbc_ref[...], wbc_ref[...])
    part += dot_nn(ddt_ref[...], wdt_ref[...])
    add = jnp.where(step % 2 == 1, add_ref[...].astype(F32), 0.0)
    core = where_ref[3]

    @pl.when(step < 2)
    def _():
        far_ref[...] = part.astype(BF)

        @pl.when(core == 0)
        def _():
            block = part.shape[0]
            far_ref[block - HALO :, :] = (part[block - HALO :] + add).astype(BF)

    @pl.when(step >= 2)
    def _():
        near_ref[...] = part

        @pl.when(core == 1)
        def _():
            block = part.shape[0]
            near_ref[block - HALO :, :] = part[block - HALO :] + add


def input_grad(place, dz, dxin, dbc, ddt, add, wz, wx, wbc, wdt):
    toks, chans = dz.shape
    width = wz.shape[0]
    nb = toks // BLOCK

    def moved(w):
        return pl.BlockSpec(
            (BLOCK, w), lambda i, where: ((((i // 2) + 1 - where[3]) % 2) * 2 + i % 2, 0)
        )

    return call(
        input_grad_kernel,
        (nb,),
        [
            moved(chans), moved(chans), moved(dbc.shape[1]), moved(HEADS_PAD), whole(add.shape),
            whole(wz.shape), whole(wx.shape), whole(wbc.shape), whole(wdt.shape),
        ],
        [
            pl.BlockSpec((BLOCK, width), lambda i, where: (jnp.minimum(i, 1), 0)),
            pl.BlockSpec((BLOCK, width), lambda i, where: (jnp.maximum(i - 2, 0), 0)),
        ],
        [out((toks // 2, width), BF), out((toks // 2, width), F32)],
        prefetch=1, flops=4 * toks * width * chans, nbytes=8 * toks * chans,
    )(place, dz, dxin, dbc, ddt, add, wz, wx, wbc, wdt)


class Moves:
    def __init__(self, n_dp, n_tensor):
        self.n_dp = n_dp
        self.n_all = n_dp * n_tensor
        self.n_tensor = n_tensor
        dp = lax.axis_index("dp")
        tensor = lax.axis_index("tensor")
        self.dp = dp
        self.row = tensor // 2
        self.core = tensor % 2
        self.z = dp // 2
        self.x = dp % 2
        self.place = jnp.stack([self.z, self.x, self.row, self.core]).astype(jnp.int32)

    def swap(self, value, z=0, x=0, y=0, c=0):
        mask = (z * 2 + x) * self.n_tensor + y * 2 + c
        return lax.ppermute(value, AXES, [(i, i ^ mask) for i in range(self.n_all)])

    def up(self, value):
        pairs = [(i, i + 2) for i in range(self.n_all) if i % self.n_tensor < 2]
        return lax.ppermute(value, AXES, pairs)

    def down(self, value):
        pairs = [(i + 2, i) for i in range(self.n_all) if i % self.n_tensor < 2]
        return lax.ppermute(value, AXES, pairs)


def gather_blocks(moves, block):
    others = [moves.swap(block, z=k) for k in (1, 2, 3)]
    first = jnp.stack([block, others[0]])
    second = jnp.stack([others[1], others[2]])
    first = jnp.stack([first, moves.swap(first, x=1)])
    second = jnp.stack([second, moves.swap(second, y=1)])
    return first, moves.swap(first, y=1), second, moves.swap(second, x=1)


def spots(z, x):
    for kx in range(2):
        for kz in range(2):
            slab = (z ^ kz) * 2 + (x ^ kx)
            yield 0, kx, kz, slab, 0
            yield 1, kx, kz, slab, 1
    for ky in range(2):
        for kz in range(2):
            yield 2, ky, kz, (z ^ (2 + kz)) * 2 + x, ky
            yield 3, ky, kz, (z ^ (2 + kz)) * 2 + (x ^ 1), ky


def place_first_kernel(where_ref, p0, p1, p2, p3, wx_ref, wbc_ref, wdt_ref, count_ref, dts, *, slab):
    pieces = (p0, p1, p2, p3)
    cols = p0.shape[-1]
    z, x, y = where_ref[0], where_ref[1], where_ref[2]
    bc_rows = slab // 4
    total = jnp.zeros((8, 128), F32)
    for arr, i, j, dp, ky in spots(z, x):
        piece = pieces[arr]
        row0 = pl.multiple_of(dp * slab, slab)
        wx_ref[pl.ds(row0, slab), ky * cols : ky * cols + cols] = piece[i, j, 0:slab, :]
        bc0 = pl.multiple_of(dp * slab + (y ^ ky) * 2 * bc_rows, bc_rows)
        bc1 = pl.multiple_of(dp * slab + (y ^ ky) * 2 * bc_rows + bc_rows, bc_rows)
        wbc_ref[pl.ds(bc0, bc_rows), :] = piece[i, j, slab : slab + bc_rows, 0 : cols // 2]
        wbc_ref[pl.ds(bc1, bc_rows), :] = piece[i, j, slab : slab + bc_rows, cols // 2 : cols]
        extra = piece[i, j, slab + bc_rows : slab + bc_rows + 16, 0:slab].astype(F32)
        dts[ky * 8 : ky * 8 + 8, pl.ds(row0, slab)] = extra[0:8]
        total = total + extra[8:16]
    wdt_ref[...] = jnp.zeros_like(wdt_ref)
    wdt_ref[0:16, :] = dts[...].astype(BF)
    count_ref[...] = jnp.broadcast_to(jnp.sum(total[0:1], axis=1, keepdims=True), (8, 128))


def place_second_kernel(where_ref, p0, p1, p2, p3, wz_ref, wo_ref, *, slab):
    pieces = (p0, p1, p2, p3)
    cols = p0.shape[-1]
    for arr, i, j, dp, ky in spots(where_ref[0], where_ref[1]):
        row0 = pl.multiple_of(dp * slab, slab)
        piece = pieces[arr]
        wz_ref[pl.ds(row0, slab), ky * cols : ky * cols + cols] = piece[i, j, 0:slab, :]
        wo_ref[pl.ds(row0, slab), ky * cols : ky * cols + cols] = piece[i, j, slab : 2 * slab, :]


def gather_first(moves, w_x, w_bc, w_dt, counts):
    slab, cols = w_x.shape
    n_dp = moves.n_dp
    width = slab * n_dp
    bcw = w_bc.shape[1]
    if n_dp != 8:
        own = lax.all_gather(w_x, "dp", axis=0, tiled=True)
        wx = jnp.concatenate([own, moves.swap(own, y=1)], axis=1)
        wbc = lax.all_gather(w_bc, "dp", axis=0, tiled=True)
        own = lax.all_gather(w_dt, "dp", axis=0, tiled=True).T
        both = jnp.concatenate([own, moves.swap(own, y=1)], axis=0)
        wdt = jnp.zeros((HEADS_PAD, width), BF).at[0 : both.shape[0]].set(both)
        count = lax.psum(jnp.sum(counts), AXES) / 2.0
        return wx, wbc, wdt, jnp.full((8, 128), count, F32)
    bc_rows = slab // 4
    half = lax.dynamic_slice_in_dim(w_bc, moves.row * 2 * bc_rows, 2 * bc_rows, 0)
    extra = jnp.zeros((16, cols), BF)
    extra = extra.at[0:8, 0:slab].set(w_dt.T)
    extra = extra.at[8, 0:4].set(counts.astype(BF))
    block = jnp.concatenate(
        [w_x, jnp.concatenate([half[0:bc_rows], half[bc_rows:]], axis=1), extra], axis=0
    )
    pieces = gather_blocks(moves, block)
    return call(
        functools.partial(place_first_kernel, slab=slab),
        (1,),
        [whole(p.shape) for p in pieces],
        [
            whole((width, 2 * cols)), whole((width, bcw)), whole((HEADS_PAD, width)),
            whole((8, 128)),
        ],
        [
            out((width, 2 * cols), BF), out((width, bcw), BF), out((HEADS_PAD, width), BF),
            out((8, 128), F32),
        ],
        [pltpu.VMEM((16, width), F32)],
        prefetch=1, nbytes=8 * width * cols,
    )(moves.place, *pieces)


def gather_second(moves, w_z, w_out):
    slab, cols = w_z.shape
    n_dp = moves.n_dp
    width = slab * n_dp
    if n_dp != 8:
        both = []
        for weight in (w_z, w_out):
            own = lax.all_gather(weight, "dp", axis=0, tiled=True)
            both.append(jnp.concatenate([own, moves.swap(own, y=1)], axis=1))
        return tuple(both)
    pieces = gather_blocks(moves, jnp.concatenate([w_z, w_out], axis=0))
    return call(
        functools.partial(place_second_kernel, slab=slab),
        (1,),
        [whole(p.shape) for p in pieces],
        [whole((width, 2 * cols)), whole((width, 2 * cols))],
        [out((width, 2 * cols), BF), out((width, 2 * cols), BF)],
        prefetch=1, nbytes=16 * width * cols,
    )(moves.place, *pieces)


def split_rows(result, hold, x, cols, a_own, a_other, b_own, b_other, step, slab, at):
    hold[...] = result
    near = pl.multiple_of(x * slab, slab)
    far = pl.multiple_of((1 - x) * slab, slab)
    rows_at = slice(at, at + slab)

    @pl.when(step < 2)
    def _():
        a_own[0, 0, rows_at, :] = hold[pl.ds(near, slab), 0:cols].astype(BF)
        a_own[0, 1, rows_at, :] = hold[pl.ds(far, slab), 0:cols].astype(BF)
        a_other[0, 0, rows_at, :] = hold[pl.ds(near, slab), cols:].astype(BF)
        a_other[0, 1, rows_at, :] = hold[pl.ds(far, slab), cols:].astype(BF)

    @pl.when(step >= 2)
    def _():
        b_own[0, 0, rows_at, :] = hold[pl.ds(near, slab), 0:cols].astype(BF)
        b_own[0, 1, rows_at, :] = hold[pl.ds(near, slab), cols:].astype(BF)
        b_other[0, 0, rows_at, :] = hold[pl.ds(far, slab), 0:cols].astype(BF)
        b_other[0, 1, rows_at, :] = hold[pl.ds(far, slab), cols:].astype(BF)


def row_sums(weight, grad):
    ones = jnp.ones((8, weight.shape[1]), BF)
    high, rest = split_low(weight.astype(F32) * grad)
    return (dot_nt(ones, high) + dot_nt(ones, rest))[0:1]


def two_grads_kernel(
    where_ref, n_ref, dz_ref, gs_ref, u_ref, wz_ref, a_own, a_other, b_own, b_other, gain_ref, hold,
    *, slab,
):
    step = pl.program_id(0)
    cols = a_own.shape[-1]
    x = where_ref[1]
    slab_z = where_ref[0] ^ step
    outs = (a_own, a_other, b_own, b_other)
    grad = dot_tn(n_ref[...], dz_ref[...])
    gain_ref[pl.ds(slab_z, 1), :] = row_sums(wz_ref[...], grad)
    split_rows(grad, hold, x, cols, *outs, step, slab, 0)
    split_rows(dot_tn(gs_ref[...], u_ref[...]), hold, x, cols, *outs, step, slab, slab)


def quad_specs(slab_rows, cols):
    first = pl.BlockSpec((1, 2, slab_rows, cols), lambda i, where: (jnp.minimum(i, 1), 0, 0, 0))
    second = pl.BlockSpec((1, 2, slab_rows, cols), lambda i, where: (jnp.maximum(i - 2, 0), 0, 0, 0))
    return [first, first, second, second], [out((2, 2, slab_rows, cols), BF)] * 4


def two_grads(moves, n_full, dz, gs, u, wz):
    toks, width = n_full.shape
    chans = dz.shape[1]
    cols = chans // 2
    slab = width // 8
    specs, shapes = quad_specs(2 * slab, cols)
    lane_block = pl.BlockSpec((toks, 2 * slab), lambda i, where: (0, where[0] ^ i))
    return call(
        functools.partial(two_grads_kernel, slab=slab),
        (4,),
        [
            lane_block, whole(dz.shape), lane_block, whole(u.shape),
            pl.BlockSpec((2 * slab, chans), lambda i, where: (where[0] ^ i, 0)),
        ],
        specs + [whole((4, 2 * slab))],
        shapes + [out((4, 2 * slab), F32)],
        [pltpu.VMEM((2 * slab, chans), F32)],
        prefetch=1, flops=4 * toks * width * chans, nbytes=16 * toks * chans,
    )(moves.place, n_full, dz, gs, u, wz)


def last_grads_kernel(
    where_ref, n_ref, halo_ref, dx_ref, dxh_ref, dbc_ref, dbch_ref, ddt_ref, wx_ref, wbc_ref,
    wdt_ref, a_own, a_other, b_own, b_other, gain_ref, dwdt_ref, hold, hold_bc, *, slab,
):
    step = pl.program_id(0)
    cols = a_own.shape[-1]
    z, x, y, core = where_ref[0], where_ref[1], where_ref[2], where_ref[3]
    slab_z = z ^ step
    n_now = n_ref[...]
    grad = dot_tn(n_now, dx_ref[...]) + dot_tn(halo_ref[...], dxh_ref[...])
    grad_bc = dot_tn(n_now, dbc_ref[...]) + dot_tn(halo_ref[...], dbch_ref[...])
    grad_dt = dot_tn(ddt_ref[...], n_now)
    dwdt_ref[...] = grad_dt[0:16]
    sums = row_sums(wx_ref[...], grad) + 0.5 * row_sums(wbc_ref[...], grad_bc)
    sums += jnp.sum(grad_dt * wdt_ref[...].astype(F32), axis=0, keepdims=True)
    gain_ref[pl.ds(slab_z, 1), :] = sums
    split_rows(grad, hold, x, cols, a_own, a_other, b_own, b_other, step, slab, 0)
    hold_bc[...] = grad_bc
    quarter = slab // 4
    eighth = quarter // 2
    rows_at = slice(slab, slab + eighth)

    def bc_block(kx, ky):
        start = pl.multiple_of((x ^ kx) * slab + ((y ^ ky) * 2 + core) * quarter, quarter)
        block = hold_bc[pl.ds(start, quarter), :].astype(BF)
        return jnp.concatenate([block[0:eighth], block[eighth:]], axis=1)

    @pl.when(step < 2)
    def _():
        a_own[0, 0, rows_at, :] = bc_block(0, 0)
        a_own[0, 1, rows_at, :] = bc_block(1, 0)
        a_other[0, 0, rows_at, :] = bc_block(0, 1)
        a_other[0, 1, rows_at, :] = bc_block(1, 1)

    @pl.when(step >= 2)
    def _():
        b_own[0, 0, rows_at, :] = bc_block(0, 0)
        b_own[0, 1, rows_at, :] = bc_block(0, 1)
        b_other[0, 0, rows_at, :] = bc_block(1, 0)
        b_other[0, 1, rows_at, :] = bc_block(1, 1)


def last_grads(moves, n_full, halo, dxin, dxh, dbc, dbch, ddt, wx, wbc, wdt):
    toks, width = n_full.shape
    chans = dxin.shape[1]
    bcw = dbc.shape[1]
    cols = chans // 2
    slab = width // 8
    specs, shapes = quad_specs(slab + slab // 8, cols)
    lane_block = pl.BlockSpec((toks, 2 * slab), lambda i, where: (0, where[0] ^ i))
    return call(
        functools.partial(last_grads_kernel, slab=slab),
        (4,),
        [
            lane_block, pl.BlockSpec((HALO, 2 * slab), lambda i, where: (0, where[0] ^ i)),
            whole(dxin.shape), whole(dxh.shape), whole(dbc.shape), whole(dbch.shape),
            whole(ddt.shape), pl.BlockSpec((2 * slab, chans), lambda i, where: (where[0] ^ i, 0)),
            pl.BlockSpec((2 * slab, bcw), lambda i, where: (where[0] ^ i, 0)),
            pl.BlockSpec((HEADS_PAD, 2 * slab), lambda i, where: (0, where[0] ^ i)),
        ],
        specs + [
            whole((4, 2 * slab)), pl.BlockSpec((16, 2 * slab), lambda i, where: (0, where[0] ^ i)),
        ],
        shapes + [out((4, 2 * slab), F32), out((16, width), F32)],
        [pltpu.VMEM((2 * slab, chans), F32), pltpu.VMEM((2 * slab, bcw), F32)],
        prefetch=1, flops=2 * toks * width * chans, nbytes=16 * toks * chans,
    )(moves.place, n_full, halo, dxin, dxh, dbc, dbch, ddt, wx, wbc, wdt)


def add_low(first, second):
    return (first.astype(F32) + second.astype(F32)).astype(BF)


def reduce_blocks(moves, a_own, a_other, b_own, b_other, ride=None):
    if ride is None:
        a_sum = add_low(a_own, moves.swap(a_other, y=1))
    else:
        shape = a_other.shape
        sent = jnp.concatenate([a_other.reshape(-1, shape[-1]), ride], axis=0)
        n_main = sent.shape[0] - ride.shape[0]
        got = moves.swap(sent, y=1)
        a_sum = add_low(a_own, got[:n_main].reshape(shape))
        ride = add_pair(ride, got[n_main:])
    b_sum = add_low(b_own, moves.swap(b_other, x=1))
    if ride is None:
        a_sum = add_low(a_sum[:, 0], moves.swap(a_sum[:, 1], x=1))
    else:
        shape = a_sum[:, 1].shape
        sent = jnp.concatenate([a_sum[:, 1].reshape(-1, shape[-1]), ride], axis=0)
        got = moves.swap(sent, x=1)
        a_sum = add_low(a_sum[:, 0], got[:n_main // 2].reshape(shape))
        ride = add_pair(ride, got[n_main // 2 :])
    b_sum = add_low(b_sum[:, 0], moves.swap(b_sum[:, 1], y=1))
    total = a_sum[0].astype(F32)
    sends = (a_sum[1], b_sum[0], b_sum[1])
    if ride is None:
        for k, sent in enumerate(sends):
            total = total + moves.swap(sent, z=k + 1).astype(F32)
        return total, None
    n_main = total.shape[0]
    rides = join_pair(ride)
    for k, sent in enumerate(sends):
        got = moves.swap(jnp.concatenate([sent, ride], axis=0), z=k + 1)
        total = total + got[:n_main].astype(F32)
        rides = rides + join_pair(got[n_main:])
    return total, rides


def make_pair(values):
    high, rest = split_low(values)
    return jnp.concatenate([high, rest], axis=0)


def join_pair(pair):
    n = pair.shape[0] // 2
    return pair[:n].astype(F32) + pair[n:].astype(F32)


def add_pair(first, second):
    return make_pair(join_pair(first) + join_pair(second))


def body(
    residual, teacher, valid_mask, gain_in, w_z, w_x, w_bc, w_dt, conv_x, conv_bc, dt_bias, a_log,
    d_skip, gain_gate, w_out,
):
    _, pos_dev, width = residual.shape
    n_tensor = lax.axis_size("tensor")
    n_dp = lax.axis_size("dp")
    moves = Moves(n_dp, n_tensor)
    tokens_all = pos_dev * n_tensor * n_dp
    cols = w_z.shape[1]
    chans = 2 * cols
    own_heads = w_dt.shape[1]
    heads = 2 * own_heads
    inner = cols * n_tensor
    bcw = w_bc.shape[1]
    slab = w_z.shape[0]
    toks = 2 * pos_dev
    core = moves.core

    valid = valid_mask.reshape(pos_dev).astype(F32)
    counts = jnp.sum(valid.reshape(2, pos_dev // 2), axis=1)
    counts = jnp.concatenate([counts, moves.swap(counts, c=1)])

    pack = jnp.concatenate(
        [
            conv_x, gain_gate[None],
            jnp.concatenate(
                [dt_bias, a_log, d_skip, jnp.zeros((cols - 3 * own_heads,), F32)]
            )[None],
            jnp.zeros((2, cols), F32),
        ],
        axis=0,
    )
    pack_other = moves.swap(pack, y=1)
    conv_x_core = jnp.concatenate([pack[0:4], pack_other[0:4]], axis=1)
    gain_row = jnp.concatenate([pack[4:5], pack_other[4:5]], axis=1)

    def head_param(k):
        at = slice(k * own_heads, (k + 1) * own_heads)
        return jnp.concatenate([pack[5, at], pack_other[5, at]])

    def pad_heads(values):
        return jnp.concatenate([values, jnp.zeros((HEADS_PAD - heads,), F32)])

    bias_col = pad_heads(head_param(0))[:, None]
    rates = pad_heads(-jnp.exp(head_param(1)))
    rate_col = rates[:, None]
    rate_row = rates[None, :]
    skip_row = jnp.repeat(head_param(2), HP)[None]
    spread = (
        jnp.arange(HEADS_PAD)[:, None] == (jnp.arange(chans) // HP)[None, :]
    ).astype(BF)

    upper = residual.reshape(pos_dev, width).astype(F32)
    factor = lax.rsqrt(jnp.mean(upper * upper, axis=-1, keepdims=True) + EPSILON)
    normed = (upper * factor * gain_in).astype(BF)
    normed_other = moves.swap(normed, c=1)
    n_full = jnp.where(
        core == 0,
        jnp.concatenate([normed, normed_other], axis=0),
        jnp.concatenate([normed_other, normed], axis=0),
    )
    halo = moves.up(n_full[toks - HALO :])

    wx, wbc, wdt, count_tile = gather_first(moves, w_x, w_bc, w_dt, counts)
    wz, wo = gather_second(moves, w_z, w_out)
    scale = tokens_all / count_tile

    (
        xin, xc, bcin, bcc, dt, a_cols, a_glob, sig, a_rows, state_end,
    ) = front(n_full, halo, wx, wbc, wdt, conv_x_core, conv_bc, bias_col, rate_col, spread)

    def cross(values):
        return jnp.concatenate([values[:, cols:], values[:, :cols]], axis=1)

    state_start = cross(moves.up(state_end.astype(BF)))
    y, saved = scan_forward(xc, bcc, dt, a_cols, a_rows, state_start, spread)
    gate, u, far, near, squares = gate_out_proj(
        moves.place, n_full, y, xc, wz, wo, skip_row, gain_row
    )
    got = moves.swap(far, c=1)
    sq_got = moves.swap(squares[0:pos_dev], c=1)
    mixed, grad_result, gs, q, loss_part = loss_step(
        near, got, squares[pos_dev:], sq_got, residual.reshape(pos_dev, width),
        teacher.reshape(pos_dev, width), valid[:, None], scale, inner,
    )

    def both(mine):
        other = moves.swap(mine, c=1)
        return jnp.where(
            core == 0,
            jnp.concatenate([mine, other], axis=0),
            jnp.concatenate([other, mine], axis=0),
        )

    gs_full = both(gs)
    q_full = both(q)
    dz, dy, rowdot, dstart, dgain_gate, dskip = gate_backward(
        gs_full, q_full, wo, y, xc, gate, a_glob, bcc, skip_row, gain_row, spread
    )
    dend = cross(moves.down(dstart.astype(BF)))

    if n_dp == 8:
        a_own, a_other, b_own, b_other, gain_z = two_grads(moves, n_full, dz, gs_full, u, wz)
        zo_grad, _ = reduce_blocks(moves, a_own, a_other, b_own, b_other)
        grad_w_z, grad_w_out = zo_grad[:slab], zo_grad[slab:]
    else:
        grad_z = dot_tn(n_full, dz)
        grad_o = dot_tn(gs_full, u)

    xin_halo = dot_nn(halo, wx).astype(BF)
    bcin_halo = dot_nn(halo, wbc).astype(BF)
    (
        dxin, dbc, ddt, dxh, dbch, dconv_x, dconv_bc, dhead,
    ) = scan_backward(
        xc, bcc, dt, a_cols, a_rows, sig, dy, rowdot, saved,
        jnp.concatenate([xin_halo, xin], axis=0), jnp.concatenate([bcin_halo, bcin], axis=0),
        dend, conv_x_core, conv_bc, skip_row, rate_row, spread,
    )

    halo_grad = moves.down((dot_nt(dxh, wx) + dot_nt(dbch, wbc)).astype(BF))
    far, near = input_grad(moves.place, dz, dxin, dbc, ddt, halo_grad, wz, wx, wbc, wdt)
    grad_normed = near + moves.swap(far, c=1).astype(F32)

    def in_order(values):
        half = values.shape[-1] // 2
        turned = jnp.concatenate([values[..., half:], values[..., :half]], axis=-1)
        return jnp.where(moves.row == 0, values, turned)

    def head_sum(at):
        return in_order(dhead[at : at + 8, 0:heads].sum(axis=0))

    small = [
        in_order(dconv_x.reshape(4, 8, chans).sum(axis=1)),
        in_order(dgain_gate.sum(axis=0)),
        head_sum(0),
        head_sum(8),
        in_order(dskip.sum(axis=0).reshape(heads, HP).sum(axis=1)),
    ]
    shared = [dconv_bc.reshape(4, 8, bcw).sum(axis=1), loss_part.sum()]
    if n_dp == 8:
        dbc_sum = add_low(dbc, moves.swap(dbc, c=1))
        dbch_sum = add_low(dbch, moves.swap(dbch, c=1))
        a_own, a_other, b_own, b_other, gain_x, grad_dt = last_grads(
            moves, n_full, halo, dxin, dxh, dbc_sum, dbch_sum, ddt, wx, wbc, wdt
        )
        shared.append((gain_z + gain_x).reshape(-1) / gain_in)
        small.append(in_order(grad_dt.T))
        flat = jnp.concatenate([v.reshape(-1) for v in small + shared])
        n_flat = flat.shape[0]
        per_row = cols * 16
        n_pad = -(-n_flat // per_row) * per_row
        ride = make_pair(
            jnp.concatenate([flat, jnp.zeros((n_pad - n_flat,), F32)]).reshape(-1, cols)
        )
        x_grad, sums = reduce_blocks(moves, a_own, a_other, b_own, b_other, ride)
        sums = sums.reshape(-1)
        grad_w_x = x_grad[:slab]
        bc_own = x_grad[slab:]
        bc_own = jnp.concatenate([bc_own[:, :bcw], bc_own[:, bcw:]], axis=0)
        bc_c = moves.swap(bc_own, c=1)
        bc_two = jnp.where(
            core == 0,
            jnp.concatenate([bc_own, bc_c], axis=0),
            jnp.concatenate([bc_c, bc_own], axis=0),
        )
        bc_y = moves.swap(bc_two, y=1)
        grad_w_bc = jnp.where(
            moves.row == 0,
            jnp.concatenate([bc_two, bc_y], axis=0),
            jnp.concatenate([bc_y, bc_two], axis=0),
        )
    else:
        grad_x = dot_tn(n_full, dxin) + dot_tn(halo, dxh)
        grad_bc = dot_tn(n_full, dbc) + dot_tn(halo, dbch)
        grad_dt = dot_tn(ddt, n_full)[0:heads]
        gain_sum = jnp.sum(wz.astype(F32) * grad_z, axis=1)
        gain_sum += jnp.sum(wx.astype(F32) * grad_x, axis=1)
        gain_sum += jnp.sum(wbc.astype(F32) * grad_bc, axis=1)
        gain_sum += jnp.sum(wdt[0:heads].astype(F32) * grad_dt, axis=0)
        shared.append(gain_sum / gain_in)
        small.append(in_order(grad_dt.T))
        big = jnp.stack([grad_z, grad_o, grad_x])
        big = big[:, :, :cols] + moves.swap(big[:, :, cols:], y=1)
        big = lax.psum_scatter(big, "dp", scatter_dimension=1, tiled=True)
        grad_w_z, grad_w_out, grad_w_x = big[0], big[1], big[2]
        grad_w_bc = lax.psum_scatter(
            lax.psum(grad_bc, "tensor"), "dp", scatter_dimension=0, tiled=True
        )
        sums = lax.psum(jnp.concatenate([v.reshape(-1) for v in small + shared]), "dp")
        sums = sums + moves.swap(sums, y=1)
    done = []
    at = 0
    for value in small + shared:
        done.append(sums[at : at + value.size].reshape(value.shape))
        at += value.size
    n_small = len(small)
    first_shared = sum(v.size for v in small)
    tail = sums[first_shared:at]
    tail = tail + moves.swap(tail, c=1)
    n_conv = 4 * bcw
    grad_conv_bc = tail[:n_conv].reshape(4, bcw)
    loss = tail[n_conv] / (count_tile[0, 0] * width)
    grad_gain_in = tail[n_conv + 1 :]

    def own(value):
        half = value.shape[-1] // 2
        return lax.dynamic_slice_in_dim(value, moves.row * half, half, value.ndim - 1)

    g_conv_x, g_gain_gate, g_bias, g_log, g_skip, g_dt = [own(v) for v in done[:n_small]]
    g_dt = lax.dynamic_slice_in_dim(g_dt, moves.dp * slab, slab, 0)

    hat = upper * factor
    scaled = grad_normed * gain_in
    grad_upper = factor * (scaled - hat * jnp.mean(scaled * hat, axis=-1, keepdims=True))
    grad_residual = (grad_result + grad_upper).astype(BF)
    return (
        mixed[None], loss, grad_residual[None], grad_gain_in, grad_w_z, grad_w_x, grad_w_bc, g_dt,
        g_conv_x, grad_conv_bc, g_bias, g_log, g_skip, g_gain_gate, grad_w_out,
    )


def solution(mesh):
    both = P("dp", "tensor")
    tokens = P("dp", "tensor", None)
    return jax.shard_map(
        body,
        mesh=mesh,
        in_specs=(
            tokens, tokens, both, P(), both, both, P("dp", None), both, P(None, "tensor"), P(),
            P("tensor"), P("tensor"), P("tensor"), P("tensor"), both,
        ),
        out_specs=(
            tokens, P(), tokens, P(), both, both, P("dp", None), both, P(None, "tensor"), P(),
            P("tensor"), P("tensor"), P("tensor"), P("tensor"), both,
        ),
        check_vma=False,
    )
```

```python
import functools

import jax
import jax.numpy as jnp
from jax import lax
from jax.experimental import pallas as pl
from jax.experimental.pallas import tpu as pltpu
from jax.sharding import PartitionSpec as P

HP = 64
BLOCK = 256
EPSILON = 1e-05
HEADS_PAD = 128
HALO = 16
BF = jnp.bfloat16
F32 = jnp.float32
HIGH = lax.Precision.HIGHEST
VMEM_LIMIT = 10 * 1024 * 1024
AXES = ("dp", "tensor")
FRONT_SPLIT = 2
BACK_SPLIT = 3


def dot_nn(left, right):
    return lax.dot_general(left, right, (((1,), (0,)), ((), ())), preferred_element_type=F32)


def dot_nt(left, right):
    return lax.dot_general(left, right, (((1,), (1,)), ((), ())), preferred_element_type=F32)


def dot_tn(left, right):
    return lax.dot_general(left, right, (((0,), (0,)), ((), ())), preferred_element_type=F32)


def split_low(values):
    high = values.astype(BF)
    return high, (values - high.astype(F32)).astype(BF)


def dot_split(dot, left, right):
    high, rest = split_low(left)
    return dot(high, right) + dot(rest, right)


def by_expansion(values, spread_mat):
    rest = values - values.astype(BF).astype(F32)
    lane = lax.broadcasted_iota(jnp.int32, values.shape, 1)
    both = jnp.where(lane < HEADS_PAD // 2, values, pltpu.roll(rest, HEADS_PAD // 2, 1))
    return dot_nn(both.astype(BF), spread_mat)


def per_head(values, sum_mat):
    high, rest = split_low(values)
    return dot_nn(high, sum_mat) + dot_nn(rest, sum_mat)


def sigmoid(values):
    return jax.nn.sigmoid(values)


def call(
    kernel, grid, in_specs, out_specs, out_shape, scratch=(), prefetch=0, flops=0, nbytes=0,
    in_place=(), far_off=(), vmem=VMEM_LIMIT,
):
    n_in, n_out = len(in_specs), len(out_specs)

    def with_operands(*operands, keep=()):
        scalars, arrays = operands[:prefetch], list(operands[prefetch:])
        extra = [v for v in keep if not any(v is w for w in arrays)]
        n_extra, n_keep = len(extra), len(keep)
        every = arrays + extra
        aliases = {prefetch + i: o for i, o in in_place}
        for o, value in enumerate(keep):
            i = [k for k, w in enumerate(every) if w is value][0]
            aliases[prefetch + i] = n_out + o

        def wrapped(*refs):
            first = prefetch + n_in
            second = first + n_extra
            kernel(*refs[:first], *refs[second : second + n_out], *refs[second + n_out + n_keep :])

        anywhere = pl.BlockSpec(memory_space=pl.ANY)
        results = pl.pallas_call(
            wrapped,
            grid_spec=pltpu.PrefetchScalarGridSpec(
                num_scalar_prefetch=prefetch,
                grid=grid,
                in_specs=list(in_specs) + [anywhere] * n_extra,
                out_specs=list(out_specs) + [anywhere] * n_keep,
                scratch_shapes=list(scratch),
            ),
            out_shape=list(out_shape) + [out(v.shape, v.dtype) for v in keep],
            input_output_aliases=aliases,
            compiler_params=pltpu.CompilerParams(
                dimension_semantics=("arbitrary",) * len(grid), vmem_limit_bytes=vmem
            ),
            cost_estimate=pl.CostEstimate(flops=1, bytes_accessed=1, transcendentals=0),
        )(*scalars, *[v if i in far_off else near_core(v) for i, v in enumerate(every)])
        return results[:n_out], results[n_out:]

    return with_operands


class Held:
    def __init__(self, value):
        self.value = value


class Chain:
    def __init__(self):
        self.live = []

    def hold(self, *values):
        held = [Held(value) for value in values]
        self.live += held
        return held if len(held) > 1 else held[0]

    def drop(self, *held):
        self.live = [h for h in self.live if not any(h is d for d in held)]
        values = [h.value for h in held]
        return values if len(values) > 1 else values[0]

    def run(self, prepared):
        runner, operands = prepared
        results, kept = runner(*operands, keep=[h.value for h in self.live])
        for held, value in zip(self.live, kept):
            held.value = value
        return self.hold(*results)


def now(*held):
    return [h.value for h in held]


def whole(shape):
    del shape
    return pl.BlockSpec(memory_space=pltpu.VMEM)


def rows(block, width):
    return pl.BlockSpec((block, width), lambda i, *_: (i, 0))


def out(shape, dtype):
    return pltpu.VMEM(shape, dtype)


def near_core(values):
    return pltpu.with_memory_space_constraint(values, pltpu.VMEM)


def front_kernel(
    n_ref, halo_ref, wx_ref, wbc_ref, wdt_ref, cx_ref, cbc_ref, bias_ref, rate_ref, spread_ref,
    *refs, first,
):
    if first > 0:
        xtail_in, btail_in, before_in, state_in = refs[:4]
        refs = refs[4 + 12 :]
    (
        xin_ref, xc_ref, bcin_ref, bcc_ref, sx_ref, sbc_ref, dt_ref, a_ref, ahead_ref, at_ref,
        y_ref, saved_ref, xtail_ref, btail_ref, before, state, end_ref, xh_ref, bh_ref, xs, bs, xt,
    ) = refs
    step = pl.program_id(0)
    block = n_ref.shape[0]
    chans = wx_ref.shape[1]
    bcw = wbc_ref.shape[1]
    n_state = bcw // 2
    half = block // 2

    @pl.when(step == 0)
    def _():
        if first == 0:
            halo_x = dot_nn(halo_ref[...], wx_ref[...])
            halo_bc = dot_nn(halo_ref[...], wbc_ref[...])
            for j in range(chans // 128):
                xs[j, 0:8, :] = halo_x[8:16, j * 128 : j * 128 + 128]
            for j in range(bcw // 128):
                bs[j, 0:8, :] = halo_bc[8:16, j * 128 : j * 128 + 128]
            xh_ref[...] = halo_x.astype(BF)
            bh_ref[...] = halo_bc.astype(BF)
            before[...] = jnp.zeros_like(before)
            state[...] = jnp.zeros_like(state)
        else:
            xs[:, 0:8, :] = xtail_in[...]
            bs[:, 0:8, :] = btail_in[...]
            before[...] = before_in[...]
            state[...] = state_in[...]
            xh_ref[...] = jnp.zeros_like(xh_ref)
            bh_ref[...] = jnp.zeros_like(bh_ref)

    @pl.when(step > 0)
    def _():
        for j in range(chans // 128):
            xs[j, 0:8, :] = xs[j, block : block + 8, :]
        for j in range(bcw // 128):
            bs[j, 0:8, :] = bs[j, block : block + 8, :]

    n_now = n_ref[...]

    def convolve(held, j, taps):
        cols = slice(j * 128, j * 128 + 128)
        pre = held[j, 5 : block + 5, :] * taps[0:1, cols]
        for k in range(1, 4):
            pre += held[j, 5 + k : block + 5 + k, :] * taps[k : k + 1, cols]
        sig = sigmoid(pre)
        return (pre * sig).astype(BF), sig * (1.0 + pre * (1.0 - sig))

    bc_now = dot_nn(n_now, wbc_ref[...])
    bcin_ref[...] = bc_now
    for j in range(bcw // 128):
        bs[j, 8 : block + 8, :] = bc_now[:, j * 128 : j * 128 + 128]
        cols = slice(j * 128, j * 128 + 128)
        bcc_ref[:, cols], sbc_ref[:, cols] = convolve(bs, j, cbc_ref)
    dt_raw = dot_nt(wdt_ref[...], n_now) + bias_ref[...]
    tail = jnp.exp(-jnp.abs(dt_raw))
    log_part = jnp.where(
        tail < 0.01, tail * (1.0 - tail * (0.5 - tail * (1.0 / 3.0))), jnp.log(1.0 + tail)
    )
    dt_t = jnp.maximum(dt_raw, 0.0) + log_part
    row_i = lax.broadcasted_iota(jnp.int32, (block, block), 0)
    col_i = lax.broadcasted_iota(jnp.int32, (block, block), 1)
    upto = jnp.where(row_i <= col_i, 1.0, 0.0).astype(F32)
    a_t = jnp.dot(dt_t * rate_ref[...], upto, precision=HIGH, preferred_element_type=F32)
    at_ref[...] = a_t[0 : at_ref.shape[0]]
    a_now = a_t.T
    dt_now = dt_t.T
    a_ref[...] = a_now
    dt_ref[...] = dt_now
    ahead_ref[...] = before[...]
    a_last = a_now[block - 1 : block]
    before[...] = before[...] + a_last
    for part in range(0, chans, 256):
        x_now = dot_nn(n_now, wx_ref[:, part : part + 256])
        xin_ref[:, part : part + 256] = x_now.astype(BF)
        for j in (part // 128, part // 128 + 1):
            at = j * 128 - part
            xs[j, 8 : block + 8, :] = x_now[:, at : at + 128]
            cols = slice(j * 128, j * 128 + 128)
            xc_ref[:, cols], slope = convolve(xs, j, cx_ref)
            sx_ref[:, cols] = slope.astype(BF)

    spread = spread_ref[...]
    b_now = bcc_ref[:, 0:n_state]
    c_now = bcc_ref[:, n_state:]
    state_low = state[...].astype(BF)
    saved_ref[0] = state_low
    xt[...] = (xc_ref[...].astype(F32) * by_expansion(dt_now, spread)).astype(BF)
    y_ref[...] = dot_nn(c_now, state_low) * by_expansion(jnp.exp(a_now), spread)
    scores = dot_nt(c_now, b_now)
    row_i = lax.broadcasted_iota(jnp.int32, (half, half), 0)
    col_i = lax.broadcasted_iota(jnp.int32, (half, half), 1)
    shut = jnp.where(row_i >= col_i, 0.0, -1e30).astype(F32)
    lane = lax.broadcasted_iota(jnp.int32, (half, 128), 1)
    for pair in range(chans // 128):
        cols = slice(pair * 128, pair * 128 + 128)
        x_pair = xt[:, cols]
        tops, lows = [], []
        for sub in range(2):
            h = pair * 2 + sub
            a_row = a_t[h : h + 1, :]
            a_top = a_now[0:half, h : h + 1]
            a_low = a_now[half:block, h : h + 1]
            m_top = jnp.exp(a_top - a_row[:, 0:half] + shut) * scores[0:half, 0:half]
            m_left = jnp.exp(a_low - a_row[:, 0:half]) * scores[half:block, 0:half]
            m_low = jnp.exp(a_low - a_row[:, half:block] + shut) * scores[half:block, half:block]
            tops.append(dot_nn(m_top.astype(BF), x_pair[0:half]))
            lows.append(
                dot_nn(jnp.concatenate([m_left.astype(BF), m_low.astype(BF)], axis=1), x_pair)
            )
        y_ref[0:half, cols] += jnp.where(lane < HP, tops[0], tops[1])
        y_ref[half:block, cols] += jnp.where(lane < HP, lows[0], lows[1])
    tail_w = by_expansion(jnp.exp(a_last - a_now), spread)
    decay = by_expansion(jnp.broadcast_to(jnp.exp(a_last), (8, HEADS_PAD)), spread)
    state[...] = state[...] * decay[0:1] + dot_tn(
        b_now, (xt[...].astype(F32) * tail_w).astype(BF)
    )
    end_ref[...] = state[...].astype(BF)
    xtail_ref[...] = xs[:, block : block + 8, :]
    btail_ref[...] = bs[:, block : block + 8, :]


def front(first, count, n_full, halo, wx, wbc, wdt, conv_x, conv_bc, bias, rate, spread, carried):
    toks, width = n_full.shape
    chans = wx.shape[1]
    bcw = wbc.shape[1]
    n_state = bcw // 2
    heads = chans // HP
    nb = toks // BLOCK
    n_x, n_b = chans // 128, bcw // 128

    def at(w):
        return pl.BlockSpec((BLOCK, w), lambda i: (first + i, 0))

    wide = [
        (at(chans), jax.ShapeDtypeStruct((toks, chans), BF)), (at(chans), out((toks, chans), BF)),
        (at(bcw), jax.ShapeDtypeStruct((toks, bcw), F32)), (at(bcw), out((toks, bcw), BF)),
        (at(chans), jax.ShapeDtypeStruct((toks, chans), BF)),
        (at(bcw), jax.ShapeDtypeStruct((toks, bcw), F32)),
        (at(HEADS_PAD), out((toks, HEADS_PAD), F32)), (at(HEADS_PAD), out((toks, HEADS_PAD), F32)),
        (pl.BlockSpec((8, HEADS_PAD), lambda i: (first + i, 0)), out((8 * nb, HEADS_PAD), F32)),
        (pl.BlockSpec((heads, BLOCK), lambda i: (0, first + i)), out((heads, toks), F32)),
        (at(chans), out((toks, chans), F32)),
        (
            pl.BlockSpec((1, n_state, chans), lambda i: (first + i, 0, 0)),
            out((nb, n_state, chans), BF),
        ),
    ]
    passed = [
        out((n_x, 8, 128), F32), out((n_b, 8, 128), F32), out((8, HEADS_PAD), F32),
        out((n_state, chans), F32),
    ]
    last = [out((n_state, chans), BF), out((HALO, chans), BF), out((HALO, bcw), BF)]
    fixed = (halo, wx, wbc, wdt, conv_x, conv_bc, bias, rate, spread)
    anywhere = pl.BlockSpec(memory_space=pl.ANY)
    runner = call(
        functools.partial(front_kernel, first=first),
        (count,),
        [at(width)]
        + [whole(v.shape) for v in fixed]
        + ([whole(v.shape) for v in passed] + [anywhere] * len(wide) if first else []),
        [spec for spec, _ in wide] + [whole(v.shape) for v in passed + last],
        [shape for _, shape in wide] + passed + last,
        [
            pltpu.VMEM((n_x, BLOCK + 8, 128), F32), pltpu.VMEM((n_b, BLOCK + 8, 128), F32),
            pltpu.VMEM((BLOCK, chans), BF),
        ],
        in_place=[(10 + 4 + k, k) for k in range(len(wide))] if first else [],
        far_off=(14, 16, 18, 19) if first else (),
        flops=2 * count * BLOCK * (width * (chans + bcw) + 2 * BLOCK * chans),
        nbytes=20 * count * BLOCK * chans,
    )
    return runner, (n_full, *fixed, *carried)


def gate_kernel(
    where_ref, n_ref, y_ref, xc_ref, c_ref, a_ref, ahead_ref, start_ref, wz_ref, wo_ref, skip_ref,
    gain_ref, spread_ref, *refs,
):
    gate_out, part_ref, sq_ref, u_ref = refs[-4:]
    chans = y_ref.shape[1]
    n_now = n_ref[...]
    squares = jnp.zeros((n_now.shape[0], 128), F32)
    passed = jnp.exp(a_ref[...] + ahead_ref[0:1])
    c_now = c_ref[...]
    for col in range(0, chans, 256):
        cols = slice(col, col + 256)
        gate = dot_nn(n_now, wz_ref[:, cols])
        y_now = y_ref[:, cols] + dot_nn(c_now, start_ref[:, turned(cols, chans)]) * by_expansion(
            passed, spread_ref[:, cols]
        )
        gated = (y_now + skip_ref[:, cols] * xc_ref[:, cols].astype(F32)) * (
            gate * sigmoid(gate)
        )
        gate_out[:, cols] = gate
        u_ref[:, cols] = (gated * gain_ref[:, cols]).astype(BF)
        sq = gated * gated
        squares += sq[:, 0:128] + sq[:, 128:256]
    sq_ref[...] = jnp.broadcast_to(jnp.sum(squares, axis=1, keepdims=True), squares.shape)
    part_ref[...] = dot_nt(u_ref[...], wo_ref[...]).astype(part_ref.dtype)


def turned(cols, chans):
    start = (cols.start + chans // 2) % chans
    return slice(start, start + cols.stop - cols.start)


def gate_out_proj(
    far, place, n_full, y, xc, bcc, a_cols, ahead, start, wz, wo, skip_row, gain_row, spread,
    in_place=(),
):
    toks, width = n_full.shape
    chans = wz.shape[1]
    half = toks // 2 // BLOCK

    def spot(i, where):
        core = 1 - where[3] if far else where[3]
        return core * half + i

    def moved(w):
        return pl.BlockSpec((BLOCK, w), lambda i, where: (spot(i, where), 0))

    plain = pl.BlockSpec((BLOCK, width), lambda i, where: (i, 0))
    anywhere = pl.BlockSpec(memory_space=pl.ANY)
    runner = call(
        gate_kernel,
        (half,),
        [
            moved(width), moved(chans), moved(chans),
            pl.BlockSpec((BLOCK, start.shape[0]), lambda i, where: (spot(i, where), 1)),
            moved(HEADS_PAD),
            pl.BlockSpec((8, HEADS_PAD), lambda i, where: (spot(i, where), 0)),
            whole(start.shape), whole(wz.shape), whole(wo.shape),
            whole(skip_row.shape), whole(gain_row.shape), whole(spread.shape),
        ] + [anywhere] * len(in_place),
        [
            moved(chans), plain,
            pl.BlockSpec((BLOCK, 128), lambda i, where: (i, 0)),
        ],
        [
            out((toks, chans), F32), out((toks // 2, width), BF if far else F32),
            out((toks // 2, 128), F32),
        ],
        [pltpu.VMEM((BLOCK, chans), BF)],
        in_place=[(12 + k, k) for k in range(len(in_place))],
        prefetch=1, flops=2 * toks * width * chans, nbytes=7 * toks * chans,
    )
    return runner, (
        place, n_full, y, xc, bcc, a_cols, ahead, start, wz, wo, skip_row, gain_row, spread,
        *in_place,
    )


def loss_kernel(
    near_ref, got_ref, sq_ref, sqgot_ref, res_ref, teach_ref, valid_ref, count_ref, countgot_ref,
    mixed_ref, gres_ref, gs_ref, q_ref, loss_ref, *, inner, tokens,
):
    @pl.when(pl.program_id(0) == 0)
    def _():
        loss_ref[...] = jnp.zeros_like(loss_ref)

    total = sq_ref[:, 0:1] + sqgot_ref[:, 0:1]
    factor = lax.rsqrt(total / inner + EPSILON)
    branch = near_ref[...] + got_ref[...].astype(F32)
    result = res_ref[...].astype(F32) + factor * branch
    mixed_ref[...] = result.astype(BF)
    error = result - teach_ref[...].astype(F32)
    valid = valid_ref[...]
    terms = jnp.sum((valid * error * error).reshape(-1, 8, error.shape[1]), axis=0)
    for col in range(0, error.shape[1], 128):
        loss_ref[...] += terms[:, col : col + 128]
    count = count_ref[0:1, 0:1] + countgot_ref[0:1, 0:1]
    grad = (valid * (tokens / count)) * error
    gres_ref[...] = grad
    gs = (grad * factor).astype(BF)
    gs_ref[...] = gs
    prods = jnp.sum(gs.astype(F32) * branch, axis=1, keepdims=True)
    q_ref[...] = jnp.broadcast_to(prods * factor * factor / inner, q_ref.shape)


def loss_step(
    near, got, sq, sqgot, residual, teacher, valid_col, count, count_got, inner, tokens
):
    toks, width = near.shape
    nb = toks // BLOCK
    runner = call(
        functools.partial(loss_kernel, inner=inner, tokens=tokens),
        (nb,),
        [
            rows(BLOCK, width), rows(BLOCK, width), rows(BLOCK, 128), rows(BLOCK, 128),
            rows(BLOCK, width), rows(BLOCK, width), rows(BLOCK, 1), whole(count.shape),
            whole(count_got.shape),
        ],
        [
            rows(BLOCK, width), rows(BLOCK, width), rows(BLOCK, width), rows(BLOCK, 128),
            whole((8, 128)),
        ],
        [
            jax.ShapeDtypeStruct((toks, width), BF), jax.ShapeDtypeStruct((toks, width), F32),
            out((toks, width), BF), out((toks, 128), F32), out((8, 128), F32),
        ],
        nbytes=20 * toks * width, far_off=(4, 5),
    )
    return runner, (near, got, sq, sqgot, residual, teacher, valid_col, count, count_got)


def gate_back_kernel(
    where_ref, gs_ref, q_ref, wo_ref, y_ref, xc_ref, gate_ref, a_ref, ahead_ref, c_ref, start_ref,
    skip_ref, gain_ref, spread_ref, sum_ref, *refs, second,
):
    (
        dz_ref, dy_ref, rowdot_ref, u_ref, dstart_ref, dgain_ref, dskip_ref, dlow_ref, dyf,
    ) = refs[-9:]

    @pl.when(pl.program_id(0) == 0)
    def _():
        for place, ref in enumerate((dstart_ref, dgain_ref, dskip_ref)):
            ref[...] = refs[place][...] if second else jnp.zeros_like(ref)

    chans = y_ref.shape[1]
    q_now = q_ref[:, 0:1]
    gs = gs_ref[...]
    passed = jnp.exp(a_ref[...] + ahead_ref[0:1])
    c_now = c_ref[...]
    for col in range(0, chans, 256):
        cols = slice(col, col + 256)
        grad = dot_nn(gs, wo_ref[:, cols])
        gate = gate_ref[:, cols].astype(F32)
        sig = sigmoid(gate)
        silu = gate * sig
        x_now = xc_ref[:, cols].astype(F32)
        wide = by_expansion(passed, spread_ref[:, cols])
        y_now = y_ref[:, cols] + dot_nn(c_now, start_ref[:, turned(cols, chans)]) * wide
        mixed = y_now + skip_ref[:, cols] * x_now
        gated = mixed * silu
        dgain_ref[:, cols] += jnp.sum((grad * gated).reshape(-1, 8, 256), axis=0)
        u_ref[:, cols] = (gated * gain_ref[:, cols]).astype(BF)
        dgated = grad * gain_ref[:, cols] - gated * q_now
        dz_ref[:, cols] = (dgated * mixed * (sig * (1.0 + gate * (1.0 - sig)))).astype(BF)
        dy = (dgated * silu).astype(BF)
        dy_ref[:, cols] = dy
        dy32 = dy.astype(F32)
        dskip_ref[:, cols] += jnp.sum((dy32 * x_now).reshape(-1, 8, 256), axis=0)
        dyf[:, cols] = dy32 * y_now
        dstart_ref[:, cols] += dot_tn(c_now, (dy32 * wide).astype(BF))
    rowdot_ref[...] = per_head(dyf[...], sum_ref[...])
    dlow_ref[...] = dstart_ref[...].astype(BF)


def gate_backward(
    place, gs, q, wo, y, xc, gate, a_cols, ahead, bcc, start, skip_row, gain_row, spread, sum_mat,
    sums=(), in_place=(),
):
    toks, width = y.shape[0], gs.shape[1]
    chans = wo.shape[1]
    n_state = bcc.shape[1] // 2
    half = toks // 2 // BLOCK
    second = len(sums) > 0

    def spot(i, where):
        return (1 - where[3] if second else where[3]) * half + i

    def moved(w):
        return pl.BlockSpec((BLOCK, w), lambda i, where: (spot(i, where), 0))

    def plain(w):
        return pl.BlockSpec((BLOCK, w), lambda i, where: (i, 0))

    anywhere = pl.BlockSpec(memory_space=pl.ANY)
    runner = call(
        functools.partial(gate_back_kernel, second=second),
        (half,),
        [
            plain(width), plain(128), whole(wo.shape), moved(chans), moved(chans), moved(chans),
            moved(HEADS_PAD), pl.BlockSpec((8, HEADS_PAD), lambda i, where: (spot(i, where), 0)),
            pl.BlockSpec((BLOCK, n_state), lambda i, where: (spot(i, where), 1)),
            whole(start.shape), whole(skip_row.shape), whole(gain_row.shape),
            whole(spread.shape), whole(sum_mat.shape),
        ]
        + [whole(v.shape) for v in sums]
        + [anywhere] * len(in_place),
        [
            moved(chans), moved(chans), moved(HEADS_PAD), moved(chans), whole((n_state, chans)),
            whole((8, chans)), whole((8, chans)), whole((n_state, chans)),
        ],
        [
            out((toks, chans), BF), out((toks, chans), BF), out((toks, HEADS_PAD), F32),
            out((toks, chans), BF), out((n_state, chans), F32), out((8, chans), F32),
            out((8, chans), F32), out((n_state, chans), BF),
        ],
        [pltpu.VMEM((BLOCK, chans), F32)],
        in_place=[(14 + len(sums) + k, k) for k in range(len(in_place))],
        prefetch=1, flops=toks * width * chans, nbytes=7 * toks * chans,
    )
    return runner, (
        place, gs, q, wo, y, xc, gate, a_cols, ahead, bcc, start, skip_row, gain_row, spread,
        sum_mat, *sums, *in_place,
    )


def scan_back_kernel(
    xc_ref, bcc_ref, dt_ref, a_ref, ahead_ref, at_ref, dy_ref, rowdot_ref, saved_ref, xin_ref,
    bcin_ref, sx_ref, sbc_ref, xh_ref, bh_ref, start_ref, cx_ref, cbc_ref, skip_ref,
    rate_ref, spread_ref, sum_ref, wx_ref, wbc_ref, dend_ref, *refs, top, final, n_carried,
):
    carried = refs[:n_carried]
    (
        dxin_ref, dbc_ref, ddt_ref, dxh_ref, dbch_ref, hgrad_ref, dcx_ref, dcbc_ref, dhead_ref, dstate,
        dxc_out, dbc_out, xt, dxt, dxp, dbp, dbco,
    ) = refs[-17:]
    step = pl.program_id(0)
    block, chans = xc_ref.shape
    bcw = bcc_ref.shape[1]
    n_state = bcw // 2
    half = block // 2
    n_x = chans // 128
    n_b = bcw // 128

    @pl.when(step == 0)
    def _():
        if n_carried == 0:
            dstate[:, 0 : chans // 2] = dend_ref[:, chans // 2 :].astype(F32)
            dstate[:, chans // 2 :] = dend_ref[:, 0 : chans // 2].astype(F32)
            for ref in (dcx_ref, dcbc_ref, dhead_ref):
                ref[...] = jnp.zeros_like(ref)
            dxp[:, block : block + 8, :] = jnp.zeros((n_x, 8, 128), F32)
            dbp[:, block : block + 8, :] = jnp.zeros((n_b, 8, 128), F32)
        else:
            for ref, given in zip((dcx_ref, dcbc_ref, dhead_ref, dstate), carried):
                ref[...] = given[...]
            for j in range(n_x):
                dxp[j, block : block + 8, :] = carried[4][:, j * 128 : j * 128 + 128]
            for j in range(n_b):
                dbp[j, block : block + 8, :] = carried[5][:, j * 128 : j * 128 + 128]

    @pl.when(step > 0)
    def _():
        for j in range(n_x):
            dxp[j, block : block + 8, :] = dxp[j, 0:8, :]
        for j in range(n_b):
            dbp[j, block : block + 8, :] = dbp[j, 0:8, :]

    spread = spread_ref[...]
    sum_mat = sum_ref[...]
    b_now = bcc_ref[:, 0:n_state]
    c_now = bcc_ref[:, n_state:]
    a_now = a_ref[...]
    dt_now = dt_ref[...]
    a_last = a_now[block - 1 : block]
    dt_wide = by_expansion(dt_now, spread)
    xt[...] = (xc_ref[...].astype(F32) * dt_wide).astype(BF)
    tail = by_expansion(jnp.exp(a_last - a_now), spread)
    dstate_low = dstate[...].astype(BF)
    dxt[...] = dot_nn(b_now, dstate_low) * tail
    scores = dot_nt(b_now, c_now)
    row_i = lax.broadcasted_iota(jnp.int32, (half, half), 0)
    col_i = lax.broadcasted_iota(jnp.int32, (half, half), 1)
    shut = jnp.where(row_i <= col_i, 0.0, -1e30).astype(F32)
    lane = lax.broadcasted_iota(jnp.int32, (half, 128), 1)
    lane_full = lax.broadcasted_iota(jnp.int32, (block, 128), 1)
    g_top = jnp.zeros((half, block), F32)
    g_low = jnp.zeros((half, half), F32)
    for pair in range(n_x):
        cols = slice(pair * 128, pair * 128 + 128)
        x_pair = xt[:, cols]
        dy_pair = dy_ref[:, cols]
        tops, lows = [], []
        for sub in range(2):
            h = pair * 2 + sub
            mine = (lane_full < HP) if sub == 0 else (lane_full >= HP)
            x_mine = jnp.where(mine, x_pair, jnp.zeros_like(x_pair))
            a_row = at_ref[h : h + 1, :]
            a_top = a_now[0:half, h : h + 1]
            a_low = a_now[half:block, h : h + 1]
            w_top = jnp.exp(a_row[:, 0:half] - a_top + shut)
            w_right = jnp.exp(a_row[:, half:block] - a_top)
            w_low = jnp.exp(a_row[:, half:block] - a_low + shut)
            w_upper = jnp.concatenate([w_top, w_right], axis=1)
            m_upper = (w_upper * scores[0:half]).astype(BF)
            m_low = (w_low * scores[half:block, half:block]).astype(BF)
            tops.append(dot_nn(m_upper, dy_pair))
            lows.append(dot_nn(m_low, dy_pair[half:block]))
            g_top += w_upper * dot_nt(x_mine[0:half], dy_pair)
            g_low += w_low * dot_nt(x_mine[half:block], dy_pair[half:block])
        dxt[0:half, cols] += jnp.where(lane < HP, tops[0], tops[1])
        dxt[half:block, cols] += jnp.where(lane < HP, lows[0], lows[1])
    came = by_expansion(jnp.exp(ahead_ref[...]), spread)
    start = jnp.concatenate(
        [start_ref[:, chans // 2 :], start_ref[:, 0 : chans // 2]], axis=1
    ).astype(F32)
    first_state = saved_ref[0].astype(F32) + start * came[0:1]
    dy_wide = (dy_ref[...].astype(F32) * by_expansion(jnp.exp(a_now), spread)).astype(BF)
    x_tail = (xt[...].astype(F32) * tail).astype(BF)
    d_b = dot_nt(x_tail, dstate_low)
    d_c = dot_nt(dy_wide, first_state.astype(BF))
    decay = by_expansion(jnp.broadcast_to(jnp.exp(a_last), (8, HEADS_PAD)), spread)
    last_state = first_state * decay[0:1] + dot_tn(b_now, x_tail)
    dbco[0:half, 0:n_state] = d_b[0:half] + dot_split(dot_nn, g_top, c_now)
    dbco[half:block, 0:n_state] = d_b[half:block] + dot_split(dot_nn, g_low, c_now[half:block])
    d_c_top = dot_split(dot_tn, g_top, b_now[0:half])
    dbco[0:half, n_state:] = d_c[0:half] + d_c_top[0:half]
    dbco[half:block, n_state:] = (
        d_c[half:block] + d_c_top[half:block] + dot_split(dot_tn, g_low, b_now[half:block])
    )
    coldot = per_head(dxt[...] * xt[...].astype(F32), sum_mat)
    direct = dot_nn((dxt[...] * xc_ref[...].astype(F32)).astype(BF), sum_mat)
    ends = jnp.sum(dstate[...] * last_state, axis=0, keepdims=True)
    ends = per_head(jnp.broadcast_to(ends, (8, chans)), sum_mat)
    row_k = lax.broadcasted_iota(jnp.int32, (block, HEADS_PAD), 0)
    d_a = rowdot_ref[...] - coldot + jnp.where(row_k == block - 1, ends[0:1], 0.0)
    row_b = lax.broadcasted_iota(jnp.int32, (block, block), 0)
    col_b = lax.broadcasted_iota(jnp.int32, (block, block), 1)
    onward = jnp.where(row_b <= col_b, 1.0, 0.0).astype(F32)
    d_step = jnp.dot(onward, d_a, precision=HIGH, preferred_element_type=F32)
    rate = rate_ref[0:1, :]
    slope = jnp.where(
        dt_now < 0.01, dt_now * (1.0 - dt_now * (0.5 - dt_now * (1.0 / 6.0))), 1.0 - jnp.exp(-dt_now)
    )
    d_raw = (direct + rate * d_step) * slope
    ddt_ref[...] = d_raw.astype(BF)
    dhead_ref[0:8, :] += jnp.sum(d_raw.reshape(-1, 8, HEADS_PAD), axis=0)
    dhead_ref[8:16, :] += jnp.sum((dt_now * d_step * rate).reshape(-1, 8, HEADS_PAD), axis=0)
    dstate[...] = dstate[...] * decay[0:1] + dot_tn(c_now, dy_wide)
    def conv_back(here, slope, grad_of, passed_on, taps, sums, dest, j):
        cols = slice(j * 128, j * 128 + 128)
        dpre = grad_of(cols) * slope[:, cols].astype(F32)
        passed_on[j, 0:block, :] = dpre
        x_now = here[:, cols].astype(F32)
        back = jnp.zeros_like(dpre)
        for k in range(4):
            later = dpre if k == 3 else passed_on[j, 3 - k : 3 - k + block, :]
            sums[8 * k : 8 * k + 8, cols] += jnp.sum((later * x_now).reshape(-1, 8, 128), axis=0)
            back += later * taps[k : k + 1, cols]
        dest[:, cols] = back.astype(dest.dtype)

    for j in range(n_b):
        conv_back(
            bcin_ref, sbc_ref, lambda cols: dbco[:, cols], dbp, cbc_ref, dcbc_ref, dbc_ref, j
        )
    for j in range(n_x):
        conv_back(
            xin_ref, sx_ref,
            lambda cols: dxt[:, cols] * dt_wide[:, cols]
            + skip_ref[:, cols] * dy_ref[:, cols].astype(F32),
            dxp, cx_ref, dcx_ref, dxin_ref, j,
        )

    @pl.when(step == pl.num_programs(0) - 1)
    def _():
        row_h = lax.broadcasted_iota(jnp.int32, (HALO, 1), 0)
        for src, taps, dest, edge, given, sums, count in (
            (dxp, cx_ref, dxh_ref, dxc_out, xh_ref, dcx_ref, n_x),
            (dbp, cbc_ref, dbch_ref, dbc_out, bh_ref, dcbc_ref, n_b),
        ):
            for j in range(count):
                cols = slice(j * 128, j * 128 + 128)
                head = src[j, 0:8, :]
                edge[:, cols] = head
                if not final:
                    continue
                acc = jnp.zeros((HALO, 128), F32)
                ahead = given[:, cols].astype(F32)
                for t in range(3):
                    for k in range(t + 1):
                        sums[8 * k : 8 * k + 1, cols] += (
                            ahead[HALO - 3 + t : HALO - 2 + t] * head[t - k : t - k + 1]
                        )
                    total = taps[0:1, cols] * head[t : t + 1]
                    for k in range(1, t + 1):
                        total = total + taps[k : k + 1, cols] * head[t - k : t - k + 1]
                    acc = acc + jnp.where(row_h == HALO - 3 + t, total, 0.0)
                dest[:, cols] = acc.astype(BF)
            if not final:
                dest[...] = jnp.zeros_like(dest)
        if final:
            hgrad_ref[...] = (
                dot_nt(dxh_ref[...], wx_ref[...]) + dot_nt(dbch_ref[...], wbc_ref[...])
            ).astype(BF)
        else:
            hgrad_ref[...] = jnp.zeros_like(hgrad_ref)


def scan_backward(
    top, count, xc, bcc, dt, a_cols, ahead, a_rows, dy, rowdot, saved, xin, bcin, slope_x, slope_bc,
    xh, bh, start, conv_x, conv_bc, skip_row, rate_row, spread, sum_mat, wx, wbc, dend, carried=(),
    in_place=(),
):
    toks, chans = xc.shape
    bcw = bcc.shape[1]
    n_state = bcw // 2
    heads = chans // HP

    def back(width):
        return pl.BlockSpec((BLOCK, width), lambda i: (top - i, 0))

    fixed = (xh, bh, start, conv_x, conv_bc, skip_row, rate_row, spread, sum_mat, wx, wbc, dend)
    anywhere = pl.BlockSpec(memory_space=pl.ANY)
    runner = call(
        functools.partial(
            scan_back_kernel, top=top, final=top + 1 == count, n_carried=len(carried)
        ),
        (count,),
        [
            back(chans), back(bcw), back(HEADS_PAD), back(HEADS_PAD),
            pl.BlockSpec((8, HEADS_PAD), lambda i: (top - i, 0)),
            pl.BlockSpec((heads, BLOCK), lambda i: (0, top - i)),
            back(chans), back(HEADS_PAD),
            pl.BlockSpec((1, n_state, chans), lambda i: (top - i, 0, 0)),
            back(chans), back(bcw), back(chans), back(bcw),
        ]
        + [whole(v.shape) for v in fixed]
        + [whole(v.shape) for v in carried]
        + [anywhere] * len(in_place),
        [
            back(chans), back(bcw), back(HEADS_PAD), whole((HALO, chans)), whole((HALO, bcw)),
            whole((HALO, wx.shape[0])), whole((32, chans)), whole((32, bcw)), whole((16, HEADS_PAD)),
            whole((n_state, chans)), whole((8, chans)), whole((8, bcw)),
        ],
        [
            out((toks, chans), BF), out((toks, bcw), F32), out((toks, HEADS_PAD), BF),
            out((HALO, chans), BF), out((HALO, bcw), BF), out((HALO, wx.shape[0]), BF),
            out((32, chans), F32), out((32, bcw), F32), out((16, HEADS_PAD), F32),
            out((n_state, chans), F32),
            out((8, chans), F32), out((8, bcw), F32),
        ],
        [
            pltpu.VMEM((BLOCK, chans), BF), pltpu.VMEM((BLOCK, chans), F32),
            pltpu.VMEM((chans // 128, BLOCK + 8, 128), F32),
            pltpu.VMEM((bcw // 128, BLOCK + 8, 128), F32), pltpu.VMEM((BLOCK, bcw), F32),
        ],
        in_place=[(25 + len(carried) + k, k) for k in range(len(in_place))],
        far_off=(9, 10, 11, 12),
        flops=2 * count * BLOCK * BLOCK * chans * 12, nbytes=16 * count * BLOCK * chans,
        vmem=12 * 1024 * 1024,
    )
    return runner, (
        xc, bcc, dt, a_cols, ahead, a_rows, dy, rowdot, saved, xin, bcin, slope_x, slope_bc, *fixed,
        *carried, *in_place,
    )


def input_grad_kernel(
    where_ref, dz_ref, dx_ref, dbc_ref, ddt_ref, wz_ref, wx_ref, wbc_ref, wdt_ref, part_ref
):
    del where_ref
    part = dot_nt(dz_ref[...], wz_ref[...])
    part += dot_nt(dx_ref[...], wx_ref[...])
    part += dot_nt(dbc_ref[...].astype(BF), wbc_ref[...])
    part += dot_nn(ddt_ref[...], wdt_ref[...])
    part_ref[...] = part.astype(part_ref.dtype)


def input_grad(far, place, dz, dxin, dbc, ddt, wz, wx, wbc, wdt):
    toks, chans = dz.shape
    width = wz.shape[0]
    half = toks // 2 // BLOCK

    def moved(w):
        return pl.BlockSpec(
            (BLOCK, w),
            lambda i, where: ((1 - where[3] if far else where[3]) * half + i, 0),
        )

    runner = call(
        input_grad_kernel,
        (half,),
        [
            moved(chans), moved(chans), moved(dbc.shape[1]), moved(HEADS_PAD),
            whole(wz.shape), whole(wx.shape), whole(wbc.shape), whole(wdt.shape),
        ],
        [pl.BlockSpec((BLOCK, width), lambda i, where: (i, 0))],
        [out((toks // 2, width), BF if far else F32)],
        prefetch=1, flops=2 * toks * width * chans, nbytes=4 * toks * chans,
    )
    return runner, (place, dz, dxin, dbc, ddt, wz, wx, wbc, wdt)


def norm_back_kernel(
    where_ref, near_ref, got_ref, res_ref, gain_ref, edge_ref, gres_ref, grad_ref, total
):
    total[...] = near_ref[...] + got_ref[...].astype(F32)
    block, width = total.shape
    last = pl.program_id(0) == pl.num_programs(0) - 1

    @pl.when(jnp.logical_and(last, jnp.logical_and(where_ref[2] == 0, where_ref[3] == 1)))
    def _():
        half = width // 2
        for k in range(2):
            total[block - HALO :, k * half : (k + 1) * half] += edge_ref[
                k * HALO : (k + 1) * HALO, :
            ].astype(F32)

    upper = res_ref[...].astype(F32)
    factor = lax.rsqrt(jnp.mean(upper * upper, axis=-1, keepdims=True) + EPSILON)
    scaled = total[...] * gain_ref[...]
    hat = upper * factor
    inner = jnp.mean(scaled * hat, axis=-1, keepdims=True)
    grad_ref[...] = (gres_ref[...] + factor * (scaled - hat * inner)).astype(BF)


def norm_backward(place, near, got, residual, gain, edge, grad_result):
    toks, width = near.shape

    def plain(w):
        return pl.BlockSpec((BLOCK, w), lambda i, where: (i, 0))

    runner = call(
        norm_back_kernel,
        (toks // BLOCK,),
        [
            plain(width), plain(width), plain(width), whole(gain.shape), whole(edge.shape),
            plain(width),
        ],
        [plain(width)],
        [jax.ShapeDtypeStruct((toks, width), BF)],
        [pltpu.VMEM((BLOCK, width), F32)],
        prefetch=1, nbytes=12 * toks * width, far_off=(2, 5),
    )
    return runner, (place, near, got, residual, gain, edge, grad_result)


class Moves:
    def __init__(self, n_dp, n_tensor):
        self.n_dp = n_dp
        self.n_all = n_dp * n_tensor
        self.n_tensor = n_tensor
        dp = lax.axis_index("dp")
        tensor = lax.axis_index("tensor")
        self.dp = dp
        self.row = tensor // 2
        self.core = tensor % 2
        self.z = dp // 2
        self.x = dp % 2
        self.place = jnp.stack([self.z, self.x, self.row, self.core]).astype(jnp.int32)

    def swap(self, value, z=0, x=0, y=0, c=0):
        mask = (z * 2 + x) * self.n_tensor + y * 2 + c
        return lax.ppermute(value, AXES, [(i, i ^ mask) for i in range(self.n_all)])

    def up(self, value):
        pairs = [(i, i + 2) for i in range(self.n_all) if i % self.n_tensor < 2]
        return lax.ppermute(value, AXES, pairs)

    def down(self, value):
        pairs = [(i + 2, i) for i in range(self.n_all) if i % self.n_tensor < 2]
        return lax.ppermute(value, AXES, pairs)


def join_kernel(where_ref, mine_ref, theirs_ref, all_ref):
    half = mine_ref.shape[0]
    core = where_ref[3]
    all_ref[pl.ds(pl.multiple_of(core * half, half), half), :] = mine_ref[...]
    all_ref[pl.ds(pl.multiple_of((1 - core) * half, half), half), :] = theirs_ref[...]


def join_tokens(place, mine, theirs):
    shape = (2 * mine.shape[0], mine.shape[1])
    runner = call(
        join_kernel, (1,), [whole(mine.shape)] * 2, [whole(shape)], [out(shape, mine.dtype)],
        prefetch=1, nbytes=8 * mine.size,
    )
    return runner, (place, mine, theirs)


def stack_kernel(first_ref, second_ref, both_ref):
    both_ref[0] = first_ref[...]
    both_ref[1] = second_ref[...]


def stack(first, second):
    runner = call(
        stack_kernel, (1,), [whole(first.shape)] * 2, [whole((2, *first.shape))],
        [out((2, *first.shape), first.dtype)], nbytes=8 * first.size,
    )
    return runner, (first, second)


def spots(z, x):
    for kx in range(2):
        for kz in range(2):
            slab = (z ^ kz) * 2 + (x ^ kx)
            yield 0, kx, kz, slab, 0
            yield 1, kx, kz, slab, 1
    for ky in range(2):
        for kz in range(2):
            yield 2, ky, kz, (z ^ (2 + kz)) * 2 + x, ky
            yield 3, ky, kz, (z ^ (2 + kz)) * 2 + (x ^ 1), ky


def place_first_kernel(where_ref, p0, p1, p2, p3, wx_ref, wbc_ref, wdt_ref, count_ref, dts, *, slab):
    pieces = (p0, p1, p2, p3)
    cols = p0.shape[-1]
    z, x, y = where_ref[0], where_ref[1], where_ref[2]
    bc_rows = slab // 4
    total = jnp.zeros((8, 128), F32)
    for arr, i, j, dp, ky in spots(z, x):
        piece = pieces[arr]
        row0 = pl.multiple_of(dp * slab, slab)
        wx_ref[pl.ds(row0, slab), ky * cols : ky * cols + cols] = piece[i, j, 0:slab, :]
        bc0 = pl.multiple_of(dp * slab + (y ^ ky) * 2 * bc_rows, bc_rows)
        bc1 = pl.multiple_of(dp * slab + (y ^ ky) * 2 * bc_rows + bc_rows, bc_rows)
        wbc_ref[pl.ds(bc0, bc_rows), :] = piece[i, j, slab : slab + bc_rows, 0 : cols // 2]
        wbc_ref[pl.ds(bc1, bc_rows), :] = piece[i, j, slab : slab + bc_rows, cols // 2 : cols]
        extra = piece[i, j, slab + bc_rows : slab + bc_rows + 16, 0:slab].astype(F32)
        dts[ky * 8 : ky * 8 + 8, pl.ds(row0, slab)] = extra[0:8]
        total = total + extra[8:16]
    wdt_ref[...] = jnp.zeros_like(wdt_ref)
    wdt_ref[0:16, :] = dts[...].astype(BF)
    count_ref[...] = jnp.broadcast_to(jnp.sum(total[0:1], axis=1, keepdims=True), (8, 128))


def place_second_kernel(where_ref, p0, p1, p2, p3, wz_ref, wo_ref, *, slab):
    pieces = (p0, p1, p2, p3)
    cols = p0.shape[-1]
    for arr, i, j, dp, ky in spots(where_ref[0], where_ref[1]):
        row0 = pl.multiple_of(dp * slab, slab)
        piece = pieces[arr]
        wz_ref[pl.ds(row0, slab), ky * cols : ky * cols + cols] = piece[i, j, 0:slab, :]
        wo_ref[pl.ds(row0, slab), ky * cols : ky * cols + cols] = piece[i, j, slab : 2 * slab, :]


def first_block_kernel(where_ref, wx_ref, wbc_ref, wdt_ref, valid_ref, block_ref):
    slab, cols = wx_ref.shape
    bc_rows = slab // 4
    block_ref[0:slab, :] = wx_ref[...]
    start = pl.multiple_of(where_ref[2] * 2 * bc_rows, 2 * bc_rows)
    half = wbc_ref[pl.ds(start, 2 * bc_rows), :]
    block_ref[slab : slab + bc_rows, 0 : cols // 2] = half[0:bc_rows]
    block_ref[slab : slab + bc_rows, cols // 2 :] = half[bc_rows:]
    row_i = lax.broadcasted_iota(jnp.int32, (slab, slab), 0)
    col_i = lax.broadcasted_iota(jnp.int32, (slab, slab), 1)
    turn = jnp.where(row_i == col_i, 1.0, 0.0).astype(BF)
    ones = valid_ref[...].astype(F32)
    quarter = ones.shape[1] // 4
    lane = lax.broadcasted_iota(jnp.int32, (8, cols), 1)
    counts = jnp.zeros((8, cols), F32)
    for k in range(4):
        total = jnp.sum(ones[:, k * quarter : (k + 1) * quarter])
        counts = counts + jnp.where(lane == k, total, 0.0)
    row = lax.broadcasted_iota(jnp.int32, (8, cols), 0)
    steps = jnp.concatenate([dot_tn(wdt_ref[...], turn), jnp.zeros((8, cols - slab), F32)], axis=1)
    extra = jnp.concatenate([steps, jnp.where(row == 0, counts, 0.0)], axis=0)
    block_ref[slab + bc_rows :, :] = extra.astype(BF)


def first_block(moves, w_x, w_bc, w_dt, valid):
    slab, cols = w_x.shape
    operands = (w_x, w_bc, w_dt, valid)
    shape = (slab + slab // 4 + 16, cols)
    runner = call(
        first_block_kernel, (1,), [whole(v.shape) for v in operands], [whole(shape)],
        [out(shape, BF)], prefetch=1, nbytes=4 * slab * cols,
    )
    return runner(moves.place, *operands)[0][0]


def place_first(moves, pieces, slab, bcw):
    cols = pieces[0].shape[-1]
    width = slab * moves.n_dp
    runner = call(
        functools.partial(place_first_kernel, slab=slab),
        (1,),
        [whole(p.shape) for p in pieces],
        [
            whole((width, 2 * cols)), whole((width, bcw)), whole((HEADS_PAD, width)),
            whole((8, 128)),
        ],
        [
            out((width, 2 * cols), BF), out((width, bcw), BF), out((HEADS_PAD, width), BF),
            out((8, 128), F32),
        ],
        [pltpu.VMEM((16, width), F32)],
        prefetch=1, nbytes=8 * width * cols,
    )
    return runner, (moves.place, *pieces)


def place_second(moves, pieces, slab):
    cols = pieces[0].shape[-1]
    width = slab * moves.n_dp
    runner = call(
        functools.partial(place_second_kernel, slab=slab),
        (1,),
        [whole(p.shape) for p in pieces],
        [whole((width, 2 * cols)), whole((width, 2 * cols))],
        [out((width, 2 * cols), BF), out((width, 2 * cols), BF)],
        prefetch=1, nbytes=16 * width * cols,
    )
    return runner, (moves.place, *pieces)


def gather_any(moves, w_x, w_bc, w_dt, w_z, w_out, valid):
    wide = []
    for weight in (w_x, w_z, w_out):
        own = lax.all_gather(weight, "dp", axis=0, tiled=True)
        wide.append(jnp.concatenate([own, moves.swap(own, y=1)], axis=1))
    wbc = lax.all_gather(w_bc, "dp", axis=0, tiled=True)
    own = lax.all_gather(w_dt, "dp", axis=0, tiled=True).T
    both = jnp.concatenate([own, moves.swap(own, y=1)], axis=0)
    wdt = jnp.zeros((HEADS_PAD, both.shape[1]), BF).at[0 : both.shape[0]].set(both)
    count = lax.psum(jnp.sum(valid), AXES)
    return (*wide, wbc, wdt, jnp.full((8, 128), count, F32))


def split_rows(hold, z, x, cols, a_own, a_msg, b_own, b_msg, step, slab, at, stride):
    def slabs(k):
        base = (k ^ (z % 2)) * 2 * slab
        near = hold[pl.ds(pl.multiple_of(base + x * slab, slab), slab), :].astype(BF)
        far = hold[pl.ds(pl.multiple_of(base + (1 - x) * slab, slab), slab), :].astype(BF)
        first = slice(2 * k * stride + at, 2 * k * stride + at + slab)
        second = slice((2 * k + 1) * stride + at, (2 * k + 1) * stride + at + slab)
        return near, far, first, second

    @pl.when(step == 0)
    def _():
        for k in range(2):
            near, far, first, second = slabs(k)
            a_own[first, :] = near[:, 0:cols]
            a_own[second, :] = far[:, 0:cols]
            a_msg[first, :] = near[:, cols:]
            a_msg[second, :] = far[:, cols:]

    @pl.when(step == 1)
    def _():
        for k in range(2):
            near, far, first, second = slabs(k)
            b_own[first, :] = near[:, 0:cols]
            b_own[second, :] = near[:, cols:]
            b_msg[first, :] = far[:, 0:cols]
            b_msg[second, :] = far[:, cols:]


def row_sums(weight, grad):
    total = jnp.zeros((grad.shape[0], 128), F32)
    for col in range(0, grad.shape[1], 128):
        total += weight[:, col : col + 128].astype(F32) * grad[:, col : col + 128]
    ones = jnp.ones((8, 128), BF)
    high, rest = split_low(total)
    return (dot_nt(ones, high) + dot_nt(ones, rest))[0:1]


def two_grads_kernel(
    where_ref, n_ref, dz_ref, gs_ref, gsgot_ref, u_ref, wz_ref, a_own, a_msg, b_own, b_msg,
    gain_ref, hold, *, slab,
):
    step = pl.program_id(0)
    cols = a_own.shape[-1]
    x = where_ref[1]
    z = where_ref[0]
    pair = (z // 2) ^ step
    outs = (a_own, a_msg, b_own, b_msg)
    hold[...] = dot_tn(n_ref[...], dz_ref[...])
    gain_ref[pl.ds(pair, 1), :] = row_sums(wz_ref[...], hold)
    split_rows(hold, z, x, cols, *outs, step, slab, 0, 2 * slab)
    half = gs_ref.shape[0]
    core = where_ref[3]
    u_own = u_ref[pl.ds(pl.multiple_of(core * half, half), half), :]
    u_other = u_ref[pl.ds(pl.multiple_of((1 - core) * half, half), half), :]
    hold[...] = dot_tn(gs_ref[...], u_own) + dot_tn(gsgot_ref[...], u_other)
    split_rows(hold, z, x, cols, *outs, step, slab, slab, 2 * slab)


def two_grads(moves, n_full, dz, gs, gs_got, u, wz):
    toks, width = n_full.shape
    chans = dz.shape[1]
    cols = chans // 2
    slab = width // 8
    lane_block = pl.BlockSpec((toks, 4 * slab), lambda i, where: (0, (where[0] // 2) ^ i))
    half_block = pl.BlockSpec((toks // 2, 4 * slab), lambda i, where: (0, (where[0] // 2) ^ i))
    shapes = [out((8 * slab, cols), BF)] * 4 + [out((2, 4 * slab), F32)]
    runner = call(
        functools.partial(two_grads_kernel, slab=slab),
        (2,),
        [
            lane_block, whole(dz.shape), half_block, half_block, whole(u.shape),
            pl.BlockSpec((4 * slab, chans), lambda i, where: ((where[0] // 2) ^ i, 0)),
        ],
        [whole(v.shape) for v in shapes],
        shapes,
        [pltpu.VMEM((4 * slab, chans), F32)],
        prefetch=1, flops=4 * toks * width * chans, nbytes=16 * toks * chans,
    )
    return runner, (moves.place, n_full, dz, gs, gs_got, u, wz)


RIDE_VALUES = 16
RIDE_ROWS = 48


def last_grads_kernel(
    where_ref, n_ref, halo_ref, dx_ref, dxh_ref, dbc_ref, dbcgot_ref, dbch_ref, dbchgot_ref,
    hgrad_ref, hgradgot_ref, ddt_ref, wx_ref, wbc_ref, wdt_ref, gainz_ref, dcx_ref, dcbc_ref,
    dgate_ref, dskip_ref, dhead_ref, loss_ref, gain_ref, sum_ref,
    a_own, a_msg, b_own, b_msg, ride_ref, hold, hold_bc, dbc_high, dbc_rest, gains, dwdt, values,
    *, slab,
):
    step = pl.program_id(0)
    cols = a_own.shape[-1]
    z, x, y, core = where_ref[0], where_ref[1], where_ref[2], where_ref[3]
    pair = (z // 2) ^ step
    eighth = slab // 4
    stride = slab + eighth

    @pl.when(step == 0)
    def _():
        dbc_high[...], dbc_rest[...] = split_low(dbc_ref[...] + dbcgot_ref[...])

    n_now = n_ref[...]
    halo = halo_ref[...]
    hold[...] = dot_tn(n_now, dx_ref[...]) + dot_tn(halo, dxh_ref[...])
    dbch_sum = (dbch_ref[...].astype(F32) + dbchgot_ref[...].astype(F32)).astype(BF)
    grad_bc = dot_tn(n_now, dbc_high[...]) + dot_tn(n_now, dbc_rest[...]) + dot_tn(halo, dbch_sum)
    grad_dt = dot_tn(ddt_ref[...], n_now)
    slabs = pl.ds(pl.multiple_of(pair * 4 * slab, 4 * slab), 4 * slab)
    dwdt[:, slabs] = grad_dt[0:16]
    sums = row_sums(wx_ref[...], hold) + 0.5 * row_sums(wbc_ref[...], grad_bc)
    sums += jnp.sum(grad_dt * wdt_ref[...].astype(F32), axis=0, keepdims=True)
    gains[0:1, slabs] = sums + gainz_ref[pl.ds(pair, 1), :]
    split_rows(hold, z, x, cols, a_own, a_msg, b_own, b_msg, step, slab, 0, stride)
    hold_bc[...] = grad_bc

    def bc_block(k, kx):
        base = (k ^ (z % 2)) * 2 * slab
        start = pl.multiple_of(base + (x ^ kx) * slab + core * 2 * eighth, eighth)
        block = hold_bc[pl.ds(start, 2 * eighth), :].astype(BF)
        return jnp.concatenate([block[0:eighth], block[eighth:]], axis=1)

    def bc_rows(k, i):
        return slice((2 * k + i) * stride + slab, (2 * k + i) * stride + slab + eighth)

    @pl.when(step == 0)
    def _():
        for k in range(2):
            for i in range(2):
                a_own[bc_rows(k, i), :] = bc_block(k, i)
                a_msg[bc_rows(k, i), :] = bc_block(k, i)

    @pl.when(step == 1)
    def _():
        for k in range(2):
            for i in range(2):
                b_own[bc_rows(k, i), :] = bc_block(k, 0)
                b_msg[bc_rows(k, i), :] = bc_block(k, 1)

    @pl.when(step == pl.num_programs(0) - 1)
    def _():
        values[...] = jnp.zeros_like(values)

        def per_channel(row, step_rows, total):
            mine, others = total[:, 0:cols], total[:, cols:]
            first_chip = jnp.where(y == 0, mine, others)
            second_chip = jnp.where(y == 0, others, mine)
            values[row : row + 1, :] = first_chip
            values[row + step_rows : row + step_rows + 1, :] = second_chip

        for k in range(4):
            per_channel(k, 4, jnp.sum(dcx_ref[8 * k : 8 * k + 8, :], axis=0, keepdims=True))
            values[12 + k // 2 : 13 + k // 2, (k % 2) * 256 : (k % 2) * 256 + 256] = jnp.sum(
                dcbc_ref[8 * k : 8 * k + 8, :], axis=0, keepdims=True
            )
        per_channel(8, 1, jnp.sum(dgate_ref[...], axis=0, keepdims=True))
        gain_total = gains[0:1, :] / gain_ref[...]
        values[10:11, :] = gain_total[:, 0:cols]
        values[11:12, :] = gain_total[:, cols:]
        skips = per_head(dskip_ref[...], sum_ref[...])
        heads = [
            jnp.sum(v, axis=0, keepdims=True)
            for v in (dhead_ref[0:8, :], dhead_ref[8:16, :], skips)
        ]
        loss = jnp.sum(loss_ref[...]) * jnp.where(
            lax.broadcasted_iota(jnp.int32, (1, 128), 1) == 0, 1.0, 0.0
        )
        for k, value in enumerate(heads):
            at = slice(k * 128, k * 128 + 128)
            turned_value = pltpu.roll(jnp.broadcast_to(value, (8, 128)), 120, 1)[0:1]
            values[14:15, at] = jnp.where(y == 0, value, turned_value)
            values[15:16, at] = jnp.where(y == 0, turned_value, value)
        values[14:15, 384:512] = jnp.where(y == 0, loss, 0.0)
        values[15:16, 384:512] = jnp.where(y == 0, 0.0, loss)
        sums_now = values[...]
        row = lax.broadcasted_iota(jnp.int32, sums_now.shape, 0)
        ride_ref[0:16, :] = jnp.where(
            row >= RIDE_VALUES - 2, two_parts(sums_now).astype(F32), sums_now
        ).astype(BF)
        grads = dwdt[...]
        turned_grads = jnp.concatenate([grads[8:16], grads[0:8]], axis=0)
        grads = jnp.where(y == 0, grads, turned_grads).astype(BF)
        ride_ref[16:32, :] = grads[:, 0:cols]
        ride_ref[32:48, :] = grads[:, cols:]
        a_msg[4 * stride : 4 * stride + RIDE_ROWS, :] = ride_ref[...]
        edge = add_low(hgrad_ref[...], hgradgot_ref[...])
        for k in range(2):
            at = 4 * stride + RIDE_ROWS + k * HALO
            a_msg[at : at + HALO, :] = edge[:, k * cols : (k + 1) * cols]


def last_grads(moves, n_full, halo, dxin, dxh, dbcs, edges, ddt, wx, wbc, wdt, small):
    toks, width = n_full.shape
    chans = dxin.shape[1]
    bcw = dbcs[0].shape[1]
    cols = chans // 2
    slab = width // 8
    stride = slab + slab // 4
    lane_block = pl.BlockSpec((toks, 4 * slab), lambda i, where: (0, (where[0] // 2) ^ i))
    shapes = [
        out((4 * stride, cols), BF), out((4 * stride + RIDE_ROWS + 2 * HALO, cols), BF),
        out((4 * stride, cols), BF), out((4 * stride, cols), BF), out((RIDE_ROWS, cols), BF),
    ]
    runner = call(
        functools.partial(last_grads_kernel, slab=slab),
        (2,),
        [
            lane_block, pl.BlockSpec((HALO, 4 * slab), lambda i, where: (0, (where[0] // 2) ^ i)),
            whole(dxin.shape), whole(dxh.shape),
            *[whole(v.shape) for v in (*dbcs, *edges)], whole(ddt.shape),
            pl.BlockSpec((4 * slab, chans), lambda i, where: ((where[0] // 2) ^ i, 0)),
            pl.BlockSpec((4 * slab, bcw), lambda i, where: ((where[0] // 2) ^ i, 0)),
            pl.BlockSpec((HEADS_PAD, 4 * slab), lambda i, where: (0, (where[0] // 2) ^ i)),
            *[whole(v.shape) for v in small],
        ],
        [whole(v.shape) for v in shapes],
        shapes,
        [
            pltpu.VMEM((4 * slab, chans), F32), pltpu.VMEM((4 * slab, bcw), F32),
            pltpu.VMEM((toks, bcw), BF), pltpu.VMEM((toks, bcw), BF), pltpu.VMEM((8, width), F32), pltpu.VMEM((16, width), F32),
            pltpu.VMEM((RIDE_VALUES, cols), F32),
        ],
        prefetch=1, flops=2 * toks * width * chans, nbytes=16 * toks * chans,
    )
    return runner, (
        moves.place, n_full, halo, dxin, dxh, *dbcs, *edges, ddt, wx, wbc, wdt, *small
    )


def add_low(first, second):
    return (first.astype(F32) + second.astype(F32)).astype(BF)


LOSS_LANE = 384


def two_parts(values):
    lane = lax.broadcasted_iota(jnp.int32, values.shape, 1)
    rest = pltpu.roll(values - values.astype(BF).astype(F32), 1, 1)
    return jnp.where(lane == LOSS_LANE + 1, rest, values).astype(BF)


def join_parts(ride):
    values = ride.astype(F32)
    lane = lax.broadcasted_iota(jnp.int32, values.shape, 1)
    last = lane == LOSS_LANE + 1
    whole_loss = values + jnp.where(
        lane == LOSS_LANE, pltpu.roll(values, values.shape[1] - 1, 1), 0.0
    )
    row = lax.broadcasted_iota(jnp.int32, values.shape, 0)
    tail = row >= RIDE_VALUES - 2
    return jnp.where(tail, jnp.where(last, 0.0, whole_loss), values)


def add_ride(first, second):
    total = join_parts(first[0:16]) + join_parts(second[0:16])
    row = lax.broadcasted_iota(jnp.int32, total.shape, 0)
    sums = jnp.where(row >= RIDE_VALUES - 2, two_parts(total).astype(F32), total).astype(BF)
    return jnp.concatenate([sums, add_low(first[16:], second[16:])], axis=0)


def fold_first_kernel(*refs, stride, ride):
    if ride:
        a_own, a_got, b_own, b_got, ride_ref, a_keep, a_msg, b_keep, b_msg, ride_out, edge = refs
    else:
        a_own, a_got, b_own, b_got, a_keep, a_msg, b_keep, b_msg = refs
    for own, got, keep, msg in ((a_own, a_got, a_keep, a_msg), (b_own, b_got, b_keep, b_msg)):
        for z in range(2):
            to = slice(z * stride, (z + 1) * stride)
            for i, dest in enumerate((keep, msg)):
                at = slice((2 * z + i) * stride, (2 * z + i + 1) * stride)
                dest[to, :] = add_low(own[at, :], got[at, :])
    if ride:
        total = add_ride(ride_ref[...], a_got[4 * stride : 4 * stride + RIDE_ROWS, :])
        ride_out[...] = total
        a_msg[2 * stride : 2 * stride + RIDE_ROWS, :] = total
        edge[...] = a_got[4 * stride + RIDE_ROWS :, :]


def fold_first(stride, a_own, a_got, b_own, b_got, ride=None):
    cols = a_own.shape[-1]
    n_ride = 0 if ride is None else RIDE_ROWS
    operands = (a_own, a_got, b_own, b_got) + (() if ride is None else (ride,))
    shapes = [
        out((2 * stride, cols), BF), out((2 * stride + n_ride, cols), BF),
        out((2 * stride, cols), BF), out((2 * stride, cols), BF),
    ] + ([] if ride is None else [out((RIDE_ROWS, cols), BF), out((2 * HALO, cols), BF)])
    runner = call(
        functools.partial(fold_first_kernel, stride=stride, ride=n_ride > 0),
        (1,), [whole(v.shape) for v in operands], [whole(v.shape) for v in shapes], shapes,
        nbytes=24 * stride * cols,
    )
    return runner, operands


def fold_second_kernel(*refs, stride, ride):
    if ride:
        a_own, a_got, b_own, b_got, ride_ref, own, far, msg, ride_out = refs
    else:
        a_own, a_got, b_own, b_got, own, far, msg = refs
    low, high = slice(0, stride), slice(stride, 2 * stride)
    own[...] = add_low(a_own[low, :], a_got[low, :])
    far[...] = add_low(b_own[low, :], b_got[low, :])
    msg[low, :] = add_low(a_own[high, :], a_got[high, :])
    msg[high, :] = add_low(b_own[high, :], b_got[high, :])
    if ride:
        total = add_ride(ride_ref[...], a_got[2 * stride : 2 * stride + RIDE_ROWS, :])
        ride_out[...] = total
        msg[2 * stride : 2 * stride + RIDE_ROWS, :] = total


def fold_second(stride, a_own, a_got, b_own, b_got, ride=None):
    cols = a_own.shape[-1]
    n_ride = 0 if ride is None else RIDE_ROWS
    operands = (a_own, a_got, b_own, b_got) + (() if ride is None else (ride,))
    shapes = [out((stride, cols), BF)] * 2 + [out((2 * stride + n_ride, cols), BF)]
    if ride is not None:
        shapes = shapes + [out((RIDE_ROWS, cols), BF)]
    runner = call(
        functools.partial(fold_second_kernel, stride=stride, ride=n_ride > 0),
        (1,), [whole(v.shape) for v in operands], [whole(v.shape) for v in shapes], shapes,
        nbytes=16 * stride * cols,
    )
    return runner, operands


def fold_third_kernel(*refs, stride, ride):
    if ride:
        own, far, got, ride_ref, keep, msg, ride_out = refs
    else:
        own, far, got, keep, msg = refs
    keep[...] = add_low(own[...], got[0:stride, :])
    msg[0:stride, :] = add_low(far[...], got[stride : 2 * stride, :])
    if ride:
        total = add_ride(ride_ref[...], got[2 * stride : 2 * stride + RIDE_ROWS, :])
        ride_out[...] = total
        msg[stride : stride + RIDE_ROWS, :] = total


def fold_third(stride, own, far, got, ride=None):
    cols = own.shape[-1]
    n_ride = 0 if ride is None else RIDE_ROWS
    operands = (own, far, got) + (() if ride is None else (ride,))
    shapes = [out((stride, cols), BF), out((stride + n_ride, cols), BF)]
    if ride is not None:
        shapes = shapes + [out((RIDE_ROWS, cols), BF)]
    runner = call(
        functools.partial(fold_third_kernel, stride=stride, ride=n_ride > 0),
        (1,), [whole(v.shape) for v in operands], [whole(v.shape) for v in shapes], shapes,
        nbytes=8 * stride * cols,
    )
    return runner, operands


def fold_two_kernel(own, got, first, second):
    slab = first.shape[0]
    for at, dest in ((0, first), (slab, second)):
        dest[...] = own[at : at + slab, :].astype(F32) + got[at : at + slab, :].astype(F32)


def fold_two(own, got):
    rows_all, cols = own.shape
    shapes = [jax.ShapeDtypeStruct((rows_all // 2, cols), F32)] * 2
    runner = call(
        fold_two_kernel, (1,), [whole(own.shape)] * 2, [whole(v.shape) for v in shapes], shapes,
        nbytes=12 * rows_all * cols,
    )
    return runner, (own, got)


def fold_last_kernel(
    where_ref, own, got, ride, wx_ref, cx_ref, gate_ref, heads_ref, dt_ref, swap_ref,
    values, dts, *, slab,
):
    stride = own.shape[0]
    total = own[...].astype(F32) + got[0:stride, :].astype(F32)
    wx_ref[...] = total[0:slab]
    values[...] = join_parts(ride[0:16, :]) + join_parts(got[stride : stride + 16, :])
    dts[...] = ride[16:48, :].astype(F32) + got[stride + 16 : stride + 48, :].astype(F32)
    y, z, x = where_ref[2], where_ref[0], where_ref[1]
    sums = values[...]
    cx_ref[...] = jnp.where(y == 0, sums[0:4], sums[4:8])
    gate_ref[...] = jnp.where(y == 0, sums[8:9], sums[9:10])
    heads_ref[...] = jnp.where(y == 0, sums[14:15], sums[15:16])
    slabs = dts.shape[1] // slab
    picked = jnp.zeros((8, slab), F32)
    for dp in range(2 * slabs):
        at = (dp % slabs) * slab
        block = dts[(dp // slabs) * 16 : (dp // slabs) * 16 + 16, at : at + slab]
        block = jnp.where(y == 0, block[0:8], block[8:16])
        picked = picked + jnp.where(z * 2 + x == dp, block, 0.0)
    dt_ref[...] = picked
    swap_ref[0 : stride - slab, :] = total[slab:stride]
    swap_ref[stride - slab : stride - slab + 8, :] = jnp.concatenate(
        [sums[10:14], sums[14:16], jnp.zeros_like(sums[0:2])], axis=0
    )


def fold_last(place, slab, own, got, ride):
    stride, cols = own.shape
    shapes = [
        jax.ShapeDtypeStruct((slab, cols), F32), out((4, cols), F32), out((1, cols), F32),
        out((1, cols), F32), out((8, slab), F32), out((stride - slab + 8, cols), F32),
    ]
    operands = (own, got, ride)
    runner = call(
        functools.partial(fold_last_kernel, slab=slab), (1,),
        [whole(v.shape) for v in operands], [whole(v.shape) for v in shapes], shapes,
        [pltpu.VMEM((RIDE_VALUES, cols), F32), pltpu.VMEM((32, cols), F32)],
        prefetch=1, nbytes=20 * stride * cols,
    )
    return runner, (place, *operands)


def body(
    residual, teacher, valid_mask, gain_in, w_z, w_x, w_bc, w_dt, conv_x, conv_bc, dt_bias, a_log,
    d_skip, gain_gate, w_out,
):
    _, pos_dev, width = residual.shape
    n_tensor = lax.axis_size("tensor")
    n_dp = lax.axis_size("dp")
    moves = Moves(n_dp, n_tensor)
    tokens_all = pos_dev * n_tensor * n_dp
    cols = w_z.shape[1]
    chans = 2 * cols
    own_heads = w_dt.shape[1]
    heads = 2 * own_heads
    inner = cols * n_tensor
    bcw = w_bc.shape[1]
    slab = w_z.shape[0]
    toks = 2 * pos_dev
    core = moves.core
    nb = toks // BLOCK
    by_permutes = n_dp == 8
    res_rows = residual.reshape(pos_dev, width)

    valid = valid_mask.reshape(pos_dev).astype(F32)
    if by_permutes:
        block1 = first_block(moves, w_x, w_bc, w_dt, valid_mask)
        others1 = [moves.swap(block1, z=k) for k in (1, 2, 3)]
        block2 = jnp.concatenate([w_z, w_out], axis=0)

    pack = jnp.concatenate(
        [
            conv_x, gain_gate[None],
            jnp.concatenate(
                [dt_bias, a_log, d_skip, jnp.zeros((cols - 3 * own_heads,), F32)]
            )[None],
            jnp.zeros((2, cols), F32),
            res_rows[pos_dev - HALO // 2 :].astype(F32).reshape(-1, cols),
        ],
        axis=0,
    )
    pack_other = moves.swap(pack, y=1)
    rows_ahead = pack_other[8:].reshape(HALO // 2, width)
    rows_ahead = jnp.where(core == 1, rows_ahead, moves.swap(rows_ahead, c=1))
    conv_x_core = jnp.concatenate([pack[0:4], pack_other[0:4]], axis=1)
    gain_row = jnp.concatenate([pack[4:5], pack_other[4:5]], axis=1)

    def head_param(k):
        at = slice(k * own_heads, (k + 1) * own_heads)
        return jnp.concatenate([pack[5, at], pack_other[5, at]])

    def pad_heads(values):
        return jnp.concatenate([values, jnp.zeros((HEADS_PAD - heads,), F32)])

    bias_col = pad_heads(head_param(0))[:, None]
    rates = pad_heads(-jnp.exp(head_param(1)))
    skip_row = jnp.repeat(head_param(2), HP)[None]
    head_of = (jnp.arange(chans) // HP)[None, :]
    lanes = jnp.arange(HEADS_PAD)[:, None]

    def norm(values):
        factor = lax.rsqrt(jnp.mean(values * values, axis=-1, keepdims=True) + EPSILON)
        return (values * factor * gain_in).astype(BF)

    normed = norm(res_rows.astype(F32))
    normed_other = moves.swap(normed, c=1)
    halo_rows = jnp.where(moves.row == 1, norm(rows_ahead), jnp.zeros((), BF))
    halo_rows = jnp.concatenate([jnp.zeros_like(halo_rows), halo_rows], axis=0)

    ch = Chain()
    halo = ch.hold(halo_rows)
    spread = ch.hold((lanes % (HEADS_PAD // 2) == head_of).astype(BF))
    sum_mat = ch.hold((lanes == head_of).astype(BF).T)
    conv_xs, conv_bcs, bias, rate_col, rate_row, skip, gain, gain_ins, valid_col = ch.hold(
        conv_x_core, conv_bc, bias_col, rates[:, None], rates[None, :], skip_row, gain_row,
        gain_in[None], valid[:, None],
    )
    n = ch.run(join_tokens(moves.place, normed, normed_other))

    def stacked(first, second):
        return ch.drop(ch.run(stack(first, second)))

    if by_permutes:
        a1 = stacked(block1, others1[0])
        a1x = moves.swap(a1, x=1)
        block2_held = ch.hold(block2)
        b1 = stacked(others1[1], others1[2])
        b1y = moves.swap(b1, y=1)
        block2 = ch.drop(block2_held)
        others2 = [moves.swap(block2, z=k) for k in (1, 2, 3)]
        a1, a1x, b1y, others2[0] = lax.optimization_barrier((a1, a1x, b1y, others2[0]))
        a1 = stacked(a1, a1x)
        a1y = moves.swap(a1, y=1)
        b1 = stacked(b1, b1y)
        b1x = moves.swap(b1, x=1)
        wx, wbc, wdt, count = ch.run(place_first(moves, (a1, a1y, b1, b1x), slab, bcw))
        count_other = moves.swap(count.value, c=1)
        a2 = stacked(block2, others2[0])
        b2 = stacked(others2[1], others2[2])
        a2x = moves.swap(a2, x=1)
        b2y = moves.swap(b2, y=1)
    else:
        *weights, counted = gather_any(moves, w_x, w_bc, w_dt, w_z, w_out, valid)
        wx, wz, wo, wbc, wdt, count = ch.hold(*weights, counted)
        count_other = jnp.zeros_like(counted)

    def run_front(first, count_, wide, passed):
        carried = ch.drop(*passed, *wide) if first else ()
        results = ch.run(
            front(
                first, count_,
                *now(n, halo, wx, wbc, wdt, conv_xs, conv_bcs, bias, rate_col, spread), carried,
            )
        )
        return results[:12], results[12:16], results[16], results[17:]

    front_split = FRONT_SPLIT if by_permutes else nb
    wide, passed, end, (x_halo, bc_halo) = run_front(0, front_split, (), ())
    if by_permutes:
        a2 = stacked(a2, a2x)
        a2y = moves.swap(a2, y=1)
        b2 = stacked(b2, b2y)
        b2x = moves.swap(b2, x=1)
    if front_split < nb:
        ch.drop(end)
        wide, passed, end, unused = run_front(front_split, nb - front_split, wide, passed)
        ch.drop(*unused)
    ch.drop(*passed)
    xin_held, xc, bcin_held, bcc, sx_held, sbc_held, dt, a_cols, ahead, a_rows, y, saved = wide
    from_front = ch.drop(xin_held, bcin_held, sx_held, sbc_held)
    start_got = moves.up(ch.drop(end))
    if by_permutes:
        wz, wo = ch.run(place_second(moves, (a2, a2y, b2, b2x), slab))
    start = ch.hold(start_got)

    given = (n, y, xc, bcc, a_cols, ahead, start, wz, wo, skip, gain, spread)
    gate, far, far_sq = ch.run(gate_out_proj(True, moves.place, *now(*given)))
    far_got = moves.swap(ch.drop(far), c=1)
    sq_got = moves.swap(ch.drop(far_sq), c=1)
    gate_value = ch.drop(gate)
    gate, near, near_sq = ch.run(
        gate_out_proj(False, moves.place, *now(*given), in_place=(gate_value,))
    )
    mixed, grad_result, gs, q, loss_part = ch.run(
        loss_step(
            ch.drop(near), far_got, ch.drop(near_sq), sq_got, res_rows,
            teacher.reshape(pos_dev, width), ch.drop(valid_col), count.value, count_other, inner,
            tokens_all,
        )
    )
    mixed, grad_result = ch.drop(mixed, grad_result)
    gs_got = moves.swap(gs.value, c=1)
    q_got = moves.swap(q.value, c=1)
    given = (wo, y, xc, gate, a_cols, ahead, bcc, start, skip, gain, spread, sum_mat)
    q_value = ch.drop(q)
    dz, dy, rowdot, u, dstart, dgate, dskip, dlow = ch.run(
        gate_backward(moves.place, gs.value, q_value, *now(*given))
    )
    ch.drop(dlow)
    in_place = ch.drop(dz, dy, rowdot, u)
    sums = ch.drop(dstart, dgate, dskip)
    operands = now(*given)
    ch.drop(gate, wo, y)
    gs_other = ch.hold(gs_got)
    dz, dy, rowdot, u, dstart, dgate, dskip, dlow = ch.run(
        gate_backward(moves.place, gs_got, q_got, *operands, sums=sums, in_place=in_place)
    )
    ch.drop(dstart)
    dend = moves.down(ch.drop(dlow))

    if by_permutes:
        prepared = two_grads(moves, *now(n, dz, gs, gs_other, u, wz))
        ch.drop(gs, gs_other, u)
        za, za_msg, zb, zb_msg, gain_z = ch.run(prepared)
        za_sent, zb_sent, dend = lax.optimization_barrier((*ch.drop(za_msg, zb_msg), dend))
        za_got = moves.swap(za_sent, y=1)
        zb_got = moves.swap(zb_sent, x=1)
    else:
        grad_z = dot_tn(n.value, dz.value)
        gs_all = jnp.where(
            core == 0,
            jnp.concatenate(now(gs, gs_other), axis=0),
            jnp.concatenate(now(gs_other, gs), axis=0),
        )
        grad_o = dot_tn(gs_all, u.value)
        ch.drop(gs, gs_other, u)

    first_given = (xc, bcc, dt, a_cols, ahead, a_rows, dy, rowdot, saved)
    last_given = (
        x_halo, bc_halo, start, conv_xs, conv_bcs, skip, rate_row, spread, sum_mat, wx, wbc,
    )

    def run_back(top, count_, whole_out, carried):
        whole_out = ch.drop(*whole_out) if whole_out else ()
        carried = ch.drop(*carried) if carried else ()
        prepared = scan_backward(
            top, count_, *now(*first_given), *from_front, *now(*last_given), dend, carried,
            whole_out,
        )
        if top + 1 == count_:
            ch.drop(*first_given, *last_given[:-4])
        results = ch.run(prepared)
        return results[:3], results[3:6], results[6:]

    back_split = BACK_SPLIT if by_permutes else nb
    whole_out, edges, carried = run_back(nb - 1, back_split, (), ())
    if by_permutes:
        za, za_msg, zb, zb_msg = ch.run(
            fold_first(2 * slab, ch.drop(za), za_got, ch.drop(zb), zb_got)
        )
        za_got = moves.swap(ch.drop(za_msg), x=1)
        zb_got = moves.swap(ch.drop(zb_msg), y=1)
    if back_split < nb:
        ch.drop(*edges)
        whole_out, edges, carried = run_back(
            nb - 1 - back_split, nb - back_split, whole_out, carried
        )
    dxin, dbc, ddt = whole_out
    dxh, dbch, halo_out = edges
    dcx, dcbc, dhead = carried[:3]
    ch.drop(*carried[3:])

    if by_permutes:
        dbc_got = moves.swap(dbc.value, c=1)
        dbch_got = moves.swap(dbch.value, c=1)
        halo_got = moves.swap(halo_out.value, c=1)
        small = ch.drop(gain_z, dcx, dcbc, dgate, dskip, dhead, loss_part)
        small += now(gain_ins, sum_mat)
        prepared = last_grads(
            moves, *now(n, halo, dxin, dxh), (dbc.value, dbc_got, dbch.value, dbch_got),
            (halo_out.value, halo_got), *now(ddt, wx, wbc, wdt), small,
        )
        ch.drop(n, halo, dxh, dbch, halo_out)
        xa, xa_msg, xb, xb_msg, ride = ch.run(prepared)
        xa_got = moves.swap(ch.drop(xa_msg), y=1)
        xb_got = moves.swap(ch.drop(xb_msg), x=1)
        z_own, z_far, z_msg = ch.run(
            fold_second(2 * slab, ch.drop(za), za_got, ch.drop(zb), zb_got)
        )
        z_got = moves.swap(ch.drop(z_msg), z=1)
    else:
        halo_sum = moves.down(add_low(halo_out.value, moves.swap(halo_out.value, c=1)))
        grad_x = dot_tn(n.value, dxin.value) + dot_tn(halo.value, dxh.value)
        grad_bc = dot_tn(n.value, dbc.value.astype(BF)) + dot_tn(halo.value, dbch.value)
        grad_dt = dot_tn(ddt.value, n.value)[0:heads]
        gain_sum = jnp.sum(wz.value.astype(F32) * grad_z, axis=1)
        gain_sum += jnp.sum(wx.value.astype(F32) * grad_x, axis=1)
        gain_sum += jnp.sum(wbc.value.astype(F32) * grad_bc, axis=1)
        gain_sum += jnp.sum(wdt.value[0:heads].astype(F32) * grad_dt, axis=0)

    given = (dz, dxin, dbc, ddt)
    weights = (wz, wx, wbc, wdt)
    far = ch.run(input_grad(True, moves.place, *now(*given), *now(*weights)))
    far_got = moves.swap(ch.drop(far), c=1)
    prepared = input_grad(False, moves.place, *now(*given), *now(*weights))
    ch.drop(*given, *weights)
    near = ch.run(prepared)
    stride = slab + slab // 4
    if by_permutes:
        z_own, z_msg = ch.run(fold_third(2 * slab, ch.drop(z_own), ch.drop(z_far), z_got))
        z_got = moves.swap(ch.drop(z_msg), z=2)
        xa, xa_msg, xb, xb_msg, ride, edge = ch.run(
            fold_first(stride, ch.drop(xa), xa_got, ch.drop(xb), xb_got, ch.drop(ride))
        )
        xa_got = moves.swap(ch.drop(xa_msg), x=1)
        xb_got = moves.swap(ch.drop(xb_msg), y=1)
    else:
        edge = ch.hold(jnp.concatenate([halo_sum[:, :cols], halo_sum[:, cols:]], axis=0))
    grad_residual = ch.drop(
        ch.run(
            norm_backward(
                moves.place, ch.drop(near), far_got, res_rows, gain_ins.value, ch.drop(edge),
                grad_result,
            )
        )
    )
    count_total = count.value[0, 0] + count_other[0, 0]

    if by_permutes:
        x_own, x_far, x_msg, ride = ch.run(
            fold_second(stride, ch.drop(xa), xa_got, ch.drop(xb), xb_got, ch.drop(ride))
        )
        x_got = moves.swap(ch.drop(x_msg), z=1)
        grad_w_z, grad_w_out = ch.drop(*ch.run(fold_two(ch.drop(z_own), z_got)))
        x_own, x_msg, ride = ch.run(
            fold_third(stride, ch.drop(x_own), ch.drop(x_far), x_got, ch.drop(ride))
        )
        x_got = moves.swap(ch.drop(x_msg), z=2)
        grad_w_x, g_conv_x, g_gate, g_heads, g_dt, mine = ch.drop(
            *ch.run(fold_last(moves.place, slab, ch.drop(x_own), x_got, ch.drop(ride)))
        )
        theirs = moves.swap(mine, c=1)
        n_bc = mine.shape[0] - 8
        shared = mine[n_bc:] + theirs[n_bc:]

        def bc_rows(part):
            return jnp.concatenate([part[:n_bc, :bcw], part[:n_bc, bcw:]], axis=0)

        grad_w_bc = jnp.where(
            core == 0,
            jnp.concatenate([bc_rows(mine), bc_rows(theirs)], axis=0),
            jnp.concatenate([bc_rows(theirs), bc_rows(mine)], axis=0),
        )
        grad_gain_in = shared[0:2].reshape(-1)
        grad_conv_bc = shared[2:4].reshape(4, bcw)
        loss = (shared[4, 384] + shared[5, 384]) / (count_total * width)
        g_bias, g_log, g_skip = [
            g_heads[0, at : at + own_heads] for at in (0, HEADS_PAD, 2 * HEADS_PAD)
        ]
        g_gain_gate = g_gate[0]
        g_dt = g_dt.T
    else:

        def in_order(values):
            half = values.shape[-1] // 2
            turn = jnp.concatenate([values[..., half:], values[..., :half]], axis=-1)
            return jnp.where(moves.row == 0, values, turn)

        small = [
            in_order(dcx.value.reshape(4, 8, chans).sum(axis=1)),
            in_order(dgate.value.sum(axis=0)),
            in_order(dhead.value[0:8, 0:heads].sum(axis=0)),
            in_order(dhead.value[8:16, 0:heads].sum(axis=0)),
            in_order(dskip.value.sum(axis=0).reshape(heads, HP).sum(axis=1)),
            in_order(grad_dt.T),
        ]
        shared = [
            dcbc.value.reshape(4, 8, bcw).sum(axis=1), loss_part.value.sum(), gain_sum / gain_in,
        ]
        big = jnp.stack([grad_z, grad_o, grad_x])
        big = big[:, :, :cols] + moves.swap(big[:, :, cols:], y=1)
        big = lax.psum_scatter(big, "dp", scatter_dimension=1, tiled=True)
        grad_w_z, grad_w_out, grad_w_x = big[0], big[1], big[2]
        grad_w_bc = lax.psum_scatter(
            lax.psum(grad_bc, "tensor"), "dp", scatter_dimension=0, tiled=True
        )
        sums = lax.psum(jnp.concatenate([v.reshape(-1) for v in small + shared]), "dp")
        sums = sums + moves.swap(sums, y=1)
        done = []
        at = 0
        for value in small:
            part = sums[at : at + value.size].reshape(value.shape)
            half = value.shape[-1] // 2
            done.append(
                lax.dynamic_slice_in_dim(part, moves.row * half, half, value.ndim - 1)
            )
            at += value.size
        g_conv_x, g_gain_gate, g_bias, g_log, g_skip, g_dt = done
        g_dt = lax.dynamic_slice_in_dim(g_dt, moves.dp * slab, slab, 0)
        tail = sums[at:]
        tail = tail + moves.swap(tail, c=1)
        n_conv = 4 * bcw
        grad_conv_bc = tail[:n_conv].reshape(4, bcw)
        loss = tail[n_conv] / (count_total * width)
        grad_gain_in = tail[n_conv + 1 :]
    return (
        mixed[None], loss, grad_residual[None], grad_gain_in, grad_w_z, grad_w_x, grad_w_bc, g_dt,
        g_conv_x, grad_conv_bc, g_bias, g_log, g_skip, g_gain_gate, grad_w_out,
    )


def solution(mesh):
    both = P("dp", "tensor")
    tokens = P("dp", "tensor", None)
    return jax.shard_map(
        body,
        mesh=mesh,
        in_specs=(
            tokens, tokens, both, P(), both, both, P("dp", None), both, P(None, "tensor"), P(),
            P("tensor"), P("tensor"), P("tensor"), P("tensor"), both,
        ),
        out_specs=(
            tokens, P(), tokens, P(), both, both, P("dp", None), both, P(None, "tensor"), P(),
            P("tensor"), P("tensor"), P("tensor"), P("tensor"), both,
        ),
        check_vma=False,
    )
```

```python
import functools

import jax
import jax.numpy as jnp
from jax import lax
from jax.experimental import pallas as pl
from jax.experimental.pallas import tpu as pltpu
from jax.sharding import PartitionSpec as P

HP = 64
BLOCK = 256
EPSILON = 1e-05
HEADS_PAD = 128
HALO = 16
BF = jnp.bfloat16
F32 = jnp.float32
HIGH = lax.Precision.HIGHEST
VMEM_LIMIT = 10 * 1024 * 1024
AXES = ("dp", "tensor")
FRONT_SPLIT = 1


def dot_nn(left, right):
    return lax.dot_general(left, right, (((1,), (0,)), ((), ())), preferred_element_type=F32)


def dot_nt(left, right):
    return lax.dot_general(left, right, (((1,), (1,)), ((), ())), preferred_element_type=F32)


def dot_tn(left, right):
    return lax.dot_general(left, right, (((0,), (0,)), ((), ())), preferred_element_type=F32)


def split_low(values):
    high = values.astype(BF)
    return high, (values - high.astype(F32)).astype(BF)


def dot_split(dot, left, right):
    high, rest = split_low(left)
    return dot(high, right) + dot(rest, right)


def by_expansion(values, spread_mat):
    rest = values - values.astype(BF).astype(F32)
    lane = lax.broadcasted_iota(jnp.int32, values.shape, 1)
    both = jnp.where(lane < HEADS_PAD // 2, values, pltpu.roll(rest, HEADS_PAD // 2, 1))
    return dot_nn(both.astype(BF), spread_mat)


def per_head(values, sum_mat):
    high, rest = split_low(values)
    return dot_nn(high, sum_mat) + dot_nn(rest, sum_mat)


def sigmoid(values):
    return jax.nn.sigmoid(values)


def call(
    kernel, grid, in_specs, out_specs, out_shape, scratch=(), prefetch=0, flops=0, nbytes=0,
    in_place=(), far_off=(), free=(), vmem=VMEM_LIMIT,
):
    n_in, n_out = len(in_specs), len(out_specs)

    def with_operands(*operands, keep=()):
        scalars, arrays = operands[:prefetch], list(operands[prefetch:])
        extra = [v for v in keep if not any(v is w for w in arrays)]
        n_extra, n_keep = len(extra), len(keep)
        every = arrays + extra
        aliases = {prefetch + i: o for i, o in in_place}
        for o, value in enumerate(keep):
            i = [k for k, w in enumerate(every) if w is value][0]
            aliases[prefetch + i] = n_out + o

        def wrapped(*refs):
            first = prefetch + n_in
            second = first + n_extra
            kernel(*refs[:first], *refs[second : second + n_out], *refs[second + n_out + n_keep :])

        anywhere = pl.BlockSpec(memory_space=pl.ANY)
        results = pl.pallas_call(
            wrapped,
            grid_spec=pltpu.PrefetchScalarGridSpec(
                num_scalar_prefetch=prefetch,
                grid=grid,
                in_specs=list(in_specs) + [anywhere] * n_extra,
                out_specs=list(out_specs) + [anywhere] * n_keep,
                scratch_shapes=list(scratch),
            ),
            out_shape=list(out_shape) + [out(v.shape, v.dtype) for v in keep],
            input_output_aliases=aliases,
            compiler_params=pltpu.CompilerParams(
                dimension_semantics=("arbitrary",) * len(grid), vmem_limit_bytes=vmem
            ),
            cost_estimate=pl.CostEstimate(flops=1, bytes_accessed=1, transcendentals=0),
        )(*scalars, *[
                v if i in free else in_hbm(v) if i in far_off else near_core(v)
                for i, v in enumerate(every)
            ])
        return results[:n_out], results[n_out:]

    return with_operands


class Held:
    def __init__(self, value):
        self.value = value


class Chain:
    def __init__(self):
        self.live = []

    def hold(self, *values):
        held = [Held(value) for value in values]
        self.live += held
        return held if len(held) > 1 else held[0]

    def drop(self, *held):
        self.live = [h for h in self.live if not any(h is d for d in held)]
        values = [h.value for h in held]
        return values if len(values) > 1 else values[0]

    def run(self, prepared):
        runner, operands = prepared
        results, kept = runner(*operands, keep=[h.value for h in self.live])
        for held, value in zip(self.live, kept):
            held.value = value
        return self.hold(*results)


def now(*held):
    return [h.value for h in held]


def whole(shape):
    del shape
    return pl.BlockSpec(memory_space=pltpu.VMEM)


def rows(block, width):
    return pl.BlockSpec((block, width), lambda i, *_: (i, 0))


def out(shape, dtype):
    return pltpu.VMEM(shape, dtype)


def in_hbm(values):
    return pltpu.with_memory_space_constraint(values, pltpu.HBM)


def near_core(values):
    return pltpu.with_memory_space_constraint(values, pltpu.VMEM)


def front_kernel(
    n_ref, halo_ref, wx_ref, wbc_ref, wdt_ref, cx_ref, cbc_ref, bias_ref, rate_ref, spread_ref,
    *refs, first,
):
    if first > 0:
        xtail_in, btail_in, before_in, state_in = refs[:4]
        refs = refs[4 + 8 :]
    (
        xc_ref, bcc_ref, dt_ref, a_ref, ahead_ref, at_ref, y_ref, saved_ref, xin_ref, bcin_ref,
        sx_ref, sbc_ref, xtail_ref, btail_ref, before, state, end_ref, xh_ref, bh_ref, xs, bs, xt,
    ) = refs
    step = pl.program_id(0)
    block = n_ref.shape[0]
    chans = wx_ref.shape[1]
    bcw = wbc_ref.shape[1]
    n_state = bcw // 2
    half = block // 2

    @pl.when(step == 0)
    def _():
        if first == 0:
            halo_x = dot_nn(halo_ref[...], wx_ref[...])
            halo_bc = dot_nn(halo_ref[...], wbc_ref[...])
            for j in range(chans // 128):
                xs[j, 0:8, :] = halo_x[8:16, j * 128 : j * 128 + 128]
            for j in range(bcw // 128):
                bs[j, 0:8, :] = halo_bc[8:16, j * 128 : j * 128 + 128]
            xh_ref[...] = halo_x.astype(BF)
            bh_ref[...] = halo_bc.astype(BF)
            before[...] = jnp.zeros_like(before)
            state[...] = jnp.zeros_like(state)
        else:
            xs[:, 0:8, :] = xtail_in[...]
            bs[:, 0:8, :] = btail_in[...]
            before[...] = before_in[...]
            state[...] = state_in[...]
            xh_ref[...] = jnp.zeros_like(xh_ref)
            bh_ref[...] = jnp.zeros_like(bh_ref)

    @pl.when(step > 0)
    def _():
        for j in range(chans // 128):
            xs[j, 0:8, :] = xs[j, block : block + 8, :]
        for j in range(bcw // 128):
            bs[j, 0:8, :] = bs[j, block : block + 8, :]

    n_now = n_ref[...]

    def convolve(held, j, taps):
        cols = slice(j * 128, j * 128 + 128)
        pre = held[j, 5 : block + 5, :] * taps[0:1, cols]
        for k in range(1, 4):
            pre += held[j, 5 + k : block + 5 + k, :] * taps[k : k + 1, cols]
        sig = sigmoid(pre)
        return (pre * sig).astype(BF), sig * (1.0 + pre * (1.0 - sig))

    bc_now = dot_nn(n_now, wbc_ref[...])
    bcin_ref[...] = bc_now
    for j in range(bcw // 128):
        bs[j, 8 : block + 8, :] = bc_now[:, j * 128 : j * 128 + 128]
        cols = slice(j * 128, j * 128 + 128)
        bcc_ref[:, cols], sbc_ref[:, cols] = convolve(bs, j, cbc_ref)
    dt_raw = dot_nt(wdt_ref[...], n_now) + bias_ref[...]
    tail = jnp.exp(-jnp.abs(dt_raw))
    log_part = jnp.where(
        tail < 0.01, tail * (1.0 - tail * (0.5 - tail * (1.0 / 3.0))), jnp.log(1.0 + tail)
    )
    dt_t = jnp.maximum(dt_raw, 0.0) + log_part
    row_i = lax.broadcasted_iota(jnp.int32, (block, block), 0)
    col_i = lax.broadcasted_iota(jnp.int32, (block, block), 1)
    upto = jnp.where(row_i <= col_i, 1.0, 0.0).astype(F32)
    a_t = jnp.dot(dt_t * rate_ref[...], upto, precision=HIGH, preferred_element_type=F32)
    at_ref[...] = a_t[0 : at_ref.shape[0]]
    a_now = a_t.T
    dt_now = dt_t.T
    a_ref[...] = a_now
    dt_ref[...] = dt_now
    ahead_ref[...] = before[...]
    a_last = a_now[block - 1 : block]
    before[...] = before[...] + a_last
    for part in range(0, chans, 256):
        x_now = dot_nn(n_now, wx_ref[:, part : part + 256])
        xin_ref[:, part : part + 256] = x_now.astype(BF)
        for j in (part // 128, part // 128 + 1):
            at = j * 128 - part
            xs[j, 8 : block + 8, :] = x_now[:, at : at + 128]
            cols = slice(j * 128, j * 128 + 128)
            xc_ref[:, cols], slope = convolve(xs, j, cx_ref)
            sx_ref[:, cols] = slope.astype(BF)

    spread = spread_ref[...]
    b_now = bcc_ref[:, 0:n_state]
    c_now = bcc_ref[:, n_state:]
    state_low = state[...].astype(BF)
    saved_ref[0] = state_low
    xt[...] = (xc_ref[...].astype(F32) * by_expansion(dt_now, spread)).astype(BF)
    y_ref[...] = dot_nn(c_now, state_low) * by_expansion(jnp.exp(a_now), spread)
    scores = dot_nt(c_now, b_now)
    row_i = lax.broadcasted_iota(jnp.int32, (half, half), 0)
    col_i = lax.broadcasted_iota(jnp.int32, (half, half), 1)
    shut = jnp.where(row_i >= col_i, 0.0, -1e30).astype(F32)
    lane = lax.broadcasted_iota(jnp.int32, (half, 128), 1)
    for pair in range(chans // 128):
        cols = slice(pair * 128, pair * 128 + 128)
        x_pair = xt[:, cols]
        tops, lows = [], []
        for sub in range(2):
            h = pair * 2 + sub
            a_row = a_t[h : h + 1, :]
            a_top = a_now[0:half, h : h + 1]
            a_low = a_now[half:block, h : h + 1]
            m_top = jnp.exp(a_top - a_row[:, 0:half] + shut) * scores[0:half, 0:half]
            m_left = jnp.exp(a_low - a_row[:, 0:half]) * scores[half:block, 0:half]
            m_low = jnp.exp(a_low - a_row[:, half:block] + shut) * scores[half:block, half:block]
            tops.append(dot_nn(m_top.astype(BF), x_pair[0:half]))
            lows.append(
                dot_nn(jnp.concatenate([m_left.astype(BF), m_low.astype(BF)], axis=1), x_pair)
            )
        y_ref[0:half, cols] += jnp.where(lane < HP, tops[0], tops[1])
        y_ref[half:block, cols] += jnp.where(lane < HP, lows[0], lows[1])
    tail_w = by_expansion(jnp.exp(a_last - a_now), spread)
    decay = by_expansion(jnp.broadcast_to(jnp.exp(a_last), (8, HEADS_PAD)), spread)
    state[...] = state[...] * decay[0:1] + dot_tn(
        b_now, (xt[...].astype(F32) * tail_w).astype(BF)
    )
    end_ref[...] = state[...].astype(BF)
    xtail_ref[...] = xs[:, block : block + 8, :]
    btail_ref[...] = bs[:, block : block + 8, :]


def front(first, count, n_full, halo, wx, wbc, wdt, conv_x, conv_bc, bias, rate, spread, carried):
    toks, width = n_full.shape
    chans = wx.shape[1]
    bcw = wbc.shape[1]
    n_state = bcw // 2
    heads = chans // HP
    nb = toks // BLOCK
    n_x, n_b = chans // 128, bcw // 128

    def at(w):
        return pl.BlockSpec((BLOCK, w), lambda i: (first + i, 0))

    def part(w, dtype):
        shape = pltpu.HBM((count * BLOCK, w), dtype)
        return pl.BlockSpec((BLOCK, w), lambda i: (i, 0)), shape

    parts = [part(chans, BF), part(bcw, F32), part(chans, BF), part(bcw, F32)]
    wide = [
        (at(chans), out((toks, chans), BF)), (at(bcw), out((toks, bcw), BF)),
        (at(HEADS_PAD), out((toks, HEADS_PAD), F32)), (at(HEADS_PAD), out((toks, HEADS_PAD), F32)),
        (pl.BlockSpec((8, HEADS_PAD), lambda i: (first + i, 0)), out((8 * nb, HEADS_PAD), F32)),
        (pl.BlockSpec((heads, BLOCK), lambda i: (0, first + i)), out((heads, toks), F32)),
        (at(chans), out((toks, chans), F32)),
        (
            pl.BlockSpec((1, n_state, chans), lambda i: (first + i, 0, 0)),
            out((nb, n_state, chans), BF),
        ),
    ]
    passed = [
        out((n_x, 8, 128), F32), out((n_b, 8, 128), F32), out((8, HEADS_PAD), F32),
        out((n_state, chans), F32),
    ]
    last = [out((n_state, chans), BF), out((HALO, chans), BF), out((HALO, bcw), BF)]
    fixed = (halo, wx, wbc, wdt, conv_x, conv_bc, bias, rate, spread)
    anywhere = pl.BlockSpec(memory_space=pl.ANY)
    runner = call(
        functools.partial(front_kernel, first=first),
        (count,),
        [at(width)]
        + [whole(v.shape) for v in fixed]
        + ([whole(v.shape) for v in passed] + [anywhere] * len(wide) if first else []),
        [spec for spec, _ in wide + parts] + [whole(v.shape) for v in passed + last],
        [shape for _, shape in wide + parts] + passed + last,
        [
            pltpu.VMEM((n_x, BLOCK + 8, 128), F32), pltpu.VMEM((n_b, BLOCK + 8, 128), F32),
            pltpu.VMEM((BLOCK, chans), BF),
        ],
        in_place=[(10 + 4 + k, k) for k in range(len(wide))] if first else [],
        flops=2 * count * BLOCK * (width * (chans + bcw) + 2 * BLOCK * chans),
        nbytes=20 * count * BLOCK * chans,
    )
    return runner, (n_full, *fixed, *carried)


def gate_kernel(
    where_ref, n_ref, y_ref, xc_ref, c_ref, a_ref, ahead_ref, start_ref, wz_ref, wo_ref, skip_ref,
    gain_ref, spread_ref, *refs,
):
    gate_out, part_ref, sq_ref, u_ref = refs[-4:]
    chans = y_ref.shape[1]
    n_now = n_ref[...]
    squares = jnp.zeros((n_now.shape[0], 128), F32)
    passed = jnp.exp(a_ref[...] + ahead_ref[0:1])
    c_now = c_ref[...]
    for col in range(0, chans, 256):
        cols = slice(col, col + 256)
        gate = dot_nn(n_now, wz_ref[:, cols])
        y_now = y_ref[:, cols] + dot_nn(c_now, start_ref[:, turned(cols, chans)]) * by_expansion(
            passed, spread_ref[:, cols]
        )
        gated = (y_now + skip_ref[:, cols] * xc_ref[:, cols].astype(F32)) * (
            gate * sigmoid(gate)
        )
        gate_out[:, cols] = gate
        u_ref[:, cols] = (gated * gain_ref[:, cols]).astype(BF)
        sq = gated * gated
        squares += sq[:, 0:128] + sq[:, 128:256]
    sq_ref[...] = jnp.broadcast_to(jnp.sum(squares, axis=1, keepdims=True), squares.shape)
    part_ref[...] = dot_nt(u_ref[...], wo_ref[...]).astype(part_ref.dtype)


def turned(cols, chans):
    start = (cols.start + chans // 2) % chans
    return slice(start, start + cols.stop - cols.start)


def gate_out_proj(
    far, place, n_full, y, xc, bcc, a_cols, ahead, start, wz, wo, skip_row, gain_row, spread,
    in_place=(),
):
    toks, width = n_full.shape
    chans = wz.shape[1]
    half = toks // 2 // BLOCK

    def spot(i, where):
        core = 1 - where[3] if far else where[3]
        return core * half + i

    def moved(w):
        return pl.BlockSpec((BLOCK, w), lambda i, where: (spot(i, where), 0))

    plain = pl.BlockSpec((BLOCK, width), lambda i, where: (i, 0))
    anywhere = pl.BlockSpec(memory_space=pl.ANY)
    runner = call(
        gate_kernel,
        (half,),
        [
            moved(width), moved(chans), moved(chans),
            pl.BlockSpec((BLOCK, start.shape[0]), lambda i, where: (spot(i, where), 1)),
            moved(HEADS_PAD),
            pl.BlockSpec((8, HEADS_PAD), lambda i, where: (spot(i, where), 0)),
            whole(start.shape), whole(wz.shape), whole(wo.shape),
            whole(skip_row.shape), whole(gain_row.shape), whole(spread.shape),
        ] + [anywhere] * len(in_place),
        [
            moved(chans), plain,
            pl.BlockSpec((BLOCK, 128), lambda i, where: (i, 0)),
        ],
        [
            out((toks, chans), F32), out((toks // 2, width), BF if far else F32),
            out((toks // 2, 128), F32),
        ],
        [pltpu.VMEM((BLOCK, chans), BF)],
        in_place=[(12 + k, k) for k in range(len(in_place))],
        prefetch=1, flops=2 * toks * width * chans, nbytes=7 * toks * chans,
    )
    return runner, (
        place, n_full, y, xc, bcc, a_cols, ahead, start, wz, wo, skip_row, gain_row, spread,
        *in_place,
    )


def loss_kernel(
    near_ref, got_ref, sq_ref, sqgot_ref, res_ref, teach_ref, valid_ref, count_ref, countgot_ref,
    mixed_ref, gres_ref, gs_ref, gsmsg_ref, q_ref, loss_ref, *, inner, tokens,
):
    @pl.when(pl.program_id(0) == 0)
    def _():
        loss_ref[...] = jnp.zeros_like(loss_ref)

    total = sq_ref[:, 0:1] + sqgot_ref[:, 0:1]
    factor = lax.rsqrt(total / inner + EPSILON)
    branch = near_ref[...] + got_ref[...].astype(F32)
    result = res_ref[...].astype(F32) + factor * branch
    mixed_ref[...] = result.astype(BF)
    error = result - teach_ref[...].astype(F32)
    valid = valid_ref[...]
    terms = jnp.sum((valid * error * error).reshape(-1, 8, error.shape[1]), axis=0)
    for col in range(0, error.shape[1], 128):
        loss_ref[...] += terms[:, col : col + 128]
    count = count_ref[0:1, 0:1] + countgot_ref[0:1, 0:1]
    grad = (valid * (tokens / count)) * error
    gres_ref[...] = grad
    gs = (grad * factor).astype(BF)
    gs_ref[...] = gs
    gsmsg_ref[...] = gs
    prods = jnp.sum(gs.astype(F32) * branch, axis=1, keepdims=True)
    q_ref[...] = jnp.broadcast_to(prods * factor * factor / inner, q_ref.shape)


def loss_step(
    near, got, sq, sqgot, residual, teacher, valid_col, count, count_got, inner, tokens
):
    toks, width = near.shape
    nb = toks // BLOCK
    runner = call(
        functools.partial(loss_kernel, inner=inner, tokens=tokens),
        (nb,),
        [
            rows(BLOCK, width), rows(BLOCK, width), rows(BLOCK, 128), rows(BLOCK, 128),
            rows(BLOCK, width), rows(BLOCK, width), rows(BLOCK, 1), whole(count.shape),
            whole(count_got.shape),
        ],
        [
            rows(BLOCK, width), rows(BLOCK, width), rows(BLOCK, width), rows(BLOCK, width),
            rows(BLOCK, 128), whole((8, 128)),
        ],
        [
            jax.ShapeDtypeStruct((toks, width), BF), pltpu.HBM((toks, width), F32),
            out((toks, width), BF), out((toks, width), BF), out((toks, 128), F32),
            out((8, 128), F32),
        ],
        nbytes=20 * toks * width, free=(4, 5),
    )
    return runner, (near, got, sq, sqgot, residual, teacher, valid_col, count, count_got)


def gate_back_kernel(
    where_ref, gs_ref, q_ref, wo_ref, y_ref, xc_ref, gate_ref, a_ref, ahead_ref, c_ref, start_ref,
    skip_ref, gain_ref, spread_ref, sum_ref, *refs, second,
):
    (
        dz_ref, dy_ref, rowdot_ref, u_ref, dstart_ref, dgain_ref, dskip_ref, dlow_ref, dyf,
    ) = refs[-9:]

    @pl.when(pl.program_id(0) == 0)
    def _():
        for place, ref in enumerate((dstart_ref, dgain_ref, dskip_ref)):
            ref[...] = refs[place][...] if second else jnp.zeros_like(ref)

    chans = y_ref.shape[1]
    q_now = q_ref[:, 0:1]
    gs = gs_ref[...]
    passed = jnp.exp(a_ref[...] + ahead_ref[0:1])
    c_now = c_ref[...]
    for col in range(0, chans, 256):
        cols = slice(col, col + 256)
        grad = dot_nn(gs, wo_ref[:, cols])
        gate = gate_ref[:, cols].astype(F32)
        sig = sigmoid(gate)
        silu = gate * sig
        x_now = xc_ref[:, cols].astype(F32)
        wide = by_expansion(passed, spread_ref[:, cols])
        y_now = y_ref[:, cols] + dot_nn(c_now, start_ref[:, turned(cols, chans)]) * wide
        mixed = y_now + skip_ref[:, cols] * x_now
        gated = mixed * silu
        dgain_ref[:, cols] += jnp.sum((grad * gated).reshape(-1, 8, 256), axis=0)
        u_ref[:, cols] = (gated * gain_ref[:, cols]).astype(BF)
        dgated = grad * gain_ref[:, cols] - gated * q_now
        dz_ref[:, cols] = (dgated * mixed * (sig * (1.0 + gate * (1.0 - sig)))).astype(BF)
        dy = (dgated * silu).astype(BF)
        dy_ref[:, cols] = dy
        dy32 = dy.astype(F32)
        dskip_ref[:, cols] += jnp.sum((dy32 * x_now).reshape(-1, 8, 256), axis=0)
        dyf[:, cols] = dy32 * y_now
        dstart_ref[:, cols] += dot_tn(c_now, (dy32 * wide).astype(BF))
    rowdot_ref[...] = per_head(dyf[...], sum_ref[...])
    dlow_ref[...] = dstart_ref[...].astype(BF)


def gate_backward(
    place, gs, q, wo, y, xc, gate, a_cols, ahead, bcc, start, skip_row, gain_row, spread, sum_mat,
    sums=(), in_place=(),
):
    toks, width = y.shape[0], gs.shape[1]
    chans = wo.shape[1]
    n_state = bcc.shape[1] // 2
    half = toks // 2 // BLOCK
    second = len(sums) > 0

    def spot(i, where):
        return (1 - where[3] if second else where[3]) * half + i

    def moved(w):
        return pl.BlockSpec((BLOCK, w), lambda i, where: (spot(i, where), 0))

    def plain(w):
        return pl.BlockSpec((BLOCK, w), lambda i, where: (i, 0))

    anywhere = pl.BlockSpec(memory_space=pl.ANY)
    runner = call(
        functools.partial(gate_back_kernel, second=second),
        (half,),
        [
            plain(width), plain(128), whole(wo.shape), moved(chans), moved(chans), moved(chans),
            moved(HEADS_PAD), pl.BlockSpec((8, HEADS_PAD), lambda i, where: (spot(i, where), 0)),
            pl.BlockSpec((BLOCK, n_state), lambda i, where: (spot(i, where), 1)),
            whole(start.shape), whole(skip_row.shape), whole(gain_row.shape),
            whole(spread.shape), whole(sum_mat.shape),
        ]
        + [whole(v.shape) for v in sums]
        + [anywhere] * len(in_place),
        [
            moved(chans), moved(chans), moved(HEADS_PAD), moved(chans), whole((n_state, chans)),
            whole((8, chans)), whole((8, chans)), whole((n_state, chans)),
        ],
        [
            out((toks, chans), BF), out((toks, chans), BF), out((toks, HEADS_PAD), F32),
            out((toks, chans), BF), out((n_state, chans), F32), out((8, chans), F32),
            out((8, chans), F32), out((n_state, chans), BF),
        ],
        [pltpu.VMEM((BLOCK, chans), F32)],
        in_place=[(14 + len(sums) + k, k) for k in range(len(in_place))],
        prefetch=1, flops=toks * width * chans, nbytes=7 * toks * chans,
    )
    return runner, (
        place, gs, q, wo, y, xc, gate, a_cols, ahead, bcc, start, skip_row, gain_row, spread,
        sum_mat, *sums, *in_place,
    )


def scan_back_kernel(
    xc_ref, bcc_ref, dt_ref, a_ref, ahead_ref, at_ref, dy_ref, rowdot_ref, saved_ref, xin_ref,
    bcin_ref, sx_ref, sbc_ref, xh_ref, bh_ref, start_ref, cx_ref, cbc_ref, skip_ref,
    rate_ref, spread_ref, sum_ref, wx_ref, wbc_ref, dend_ref, *refs, top, final, n_carried,
):
    carried = refs[:n_carried]
    (
        dxin_ref, dbc_ref, ddt_ref, dxh_ref, dbch_ref, hgrad_ref, dcx_ref, dcbc_ref, dhead_ref, dstate,
        dxc_out, dbc_out, xt, dxt, dxp, dbp, dbco,
    ) = refs[-17:]
    step = pl.program_id(0)
    block, chans = xc_ref.shape
    bcw = bcc_ref.shape[1]
    n_state = bcw // 2
    half = block // 2
    n_x = chans // 128
    n_b = bcw // 128

    @pl.when(step == 0)
    def _():
        if n_carried == 0:
            dstate[:, 0 : chans // 2] = dend_ref[:, chans // 2 :].astype(F32)
            dstate[:, chans // 2 :] = dend_ref[:, 0 : chans // 2].astype(F32)
            for ref in (dcx_ref, dcbc_ref, dhead_ref):
                ref[...] = jnp.zeros_like(ref)
            dxp[:, block : block + 8, :] = jnp.zeros((n_x, 8, 128), F32)
            dbp[:, block : block + 8, :] = jnp.zeros((n_b, 8, 128), F32)
        else:
            for ref, given in zip((dcx_ref, dcbc_ref, dhead_ref, dstate), carried):
                ref[...] = given[...]
            for j in range(n_x):
                dxp[j, block : block + 8, :] = carried[4][:, j * 128 : j * 128 + 128]
            for j in range(n_b):
                dbp[j, block : block + 8, :] = carried[5][:, j * 128 : j * 128 + 128]

    @pl.when(step > 0)
    def _():
        for j in range(n_x):
            dxp[j, block : block + 8, :] = dxp[j, 0:8, :]
        for j in range(n_b):
            dbp[j, block : block + 8, :] = dbp[j, 0:8, :]

    spread = spread_ref[...]
    sum_mat = sum_ref[...]
    b_now = bcc_ref[:, 0:n_state]
    c_now = bcc_ref[:, n_state:]
    a_now = a_ref[...]
    dt_now = dt_ref[...]
    a_last = a_now[block - 1 : block]
    dt_wide = by_expansion(dt_now, spread)
    xt[...] = (xc_ref[...].astype(F32) * dt_wide).astype(BF)
    tail = by_expansion(jnp.exp(a_last - a_now), spread)
    dstate_low = dstate[...].astype(BF)
    dxt[...] = dot_nn(b_now, dstate_low) * tail
    scores = dot_nt(b_now, c_now)
    row_i = lax.broadcasted_iota(jnp.int32, (half, half), 0)
    col_i = lax.broadcasted_iota(jnp.int32, (half, half), 1)
    shut = jnp.where(row_i <= col_i, 0.0, -1e30).astype(F32)
    lane = lax.broadcasted_iota(jnp.int32, (half, 128), 1)
    lane_full = lax.broadcasted_iota(jnp.int32, (block, 128), 1)
    g_top = jnp.zeros((half, block), F32)
    g_low = jnp.zeros((half, half), F32)
    for pair in range(n_x):
        cols = slice(pair * 128, pair * 128 + 128)
        x_pair = xt[:, cols]
        dy_pair = dy_ref[:, cols]
        none = jnp.zeros_like(x_pair)
        x_mine = [jnp.where(lane_full < HP, x_pair, none), jnp.where(lane_full < HP, none, x_pair)]
        w_uppers, w_lows, m_uppers, m_lows = [], [], [], []
        for sub in range(2):
            h = pair * 2 + sub
            a_row = at_ref[h : h + 1, :]
            a_top = a_now[0:half, h : h + 1]
            a_low = a_now[half:block, h : h + 1]
            w_top = jnp.exp(a_row[:, 0:half] - a_top + shut)
            w_right = jnp.exp(a_row[:, half:block] - a_top)
            w_low = jnp.exp(a_row[:, half:block] - a_low + shut)
            w_upper = jnp.concatenate([w_top, w_right], axis=1)
            w_uppers.append(w_upper)
            w_lows.append(w_low)
            m_uppers.append((w_upper * scores[0:half]).astype(BF))
            m_lows.append((w_low * scores[half:block, half:block]).astype(BF))
        tops = dot_nn(jnp.concatenate(m_uppers, axis=0), dy_pair)
        lows = dot_nn(jnp.concatenate(m_lows, axis=0), dy_pair[half:block])
        x_tops = jnp.concatenate([x_mine[0][0:half], x_mine[1][0:half]], axis=0)
        x_lows = jnp.concatenate([x_mine[0][half:block], x_mine[1][half:block]], axis=0)
        d_uppers = dot_nt(x_tops, dy_pair)
        d_lows = dot_nt(x_lows, dy_pair[half:block])
        g_top += w_uppers[0] * d_uppers[0:half] + w_uppers[1] * d_uppers[half:block]
        g_low += w_lows[0] * d_lows[0:half] + w_lows[1] * d_lows[half:block]
        dxt[0:half, cols] += jnp.where(lane < HP, tops[0:half], tops[half:block])
        dxt[half:block, cols] += jnp.where(lane < HP, lows[0:half], lows[half:block])
    came = by_expansion(jnp.exp(ahead_ref[...]), spread)
    start = jnp.concatenate(
        [start_ref[:, chans // 2 :], start_ref[:, 0 : chans // 2]], axis=1
    ).astype(F32)
    first_state = saved_ref[0].astype(F32) + start * came[0:1]
    dy_wide = (dy_ref[...].astype(F32) * by_expansion(jnp.exp(a_now), spread)).astype(BF)
    x_tail = (xt[...].astype(F32) * tail).astype(BF)
    d_b = dot_nt(x_tail, dstate_low)
    d_c = dot_nt(dy_wide, first_state.astype(BF))
    decay = by_expansion(jnp.broadcast_to(jnp.exp(a_last), (8, HEADS_PAD)), spread)
    last_state = first_state * decay[0:1] + dot_tn(b_now, x_tail)
    dbco[0:half, 0:n_state] = d_b[0:half] + dot_split(dot_nn, g_top, c_now)
    dbco[half:block, 0:n_state] = d_b[half:block] + dot_split(dot_nn, g_low, c_now[half:block])
    d_c_top = dot_split(dot_tn, g_top, b_now[0:half])
    dbco[0:half, n_state:] = d_c[0:half] + d_c_top[0:half]
    dbco[half:block, n_state:] = (
        d_c[half:block] + d_c_top[half:block] + dot_split(dot_tn, g_low, b_now[half:block])
    )
    coldot = per_head(dxt[...] * xt[...].astype(F32), sum_mat)
    direct = dot_nn((dxt[...] * xc_ref[...].astype(F32)).astype(BF), sum_mat)
    ends = jnp.sum(dstate[...] * last_state, axis=0, keepdims=True)
    ends = per_head(jnp.broadcast_to(ends, (8, chans)), sum_mat)
    row_k = lax.broadcasted_iota(jnp.int32, (block, HEADS_PAD), 0)
    d_a = rowdot_ref[...] - coldot + jnp.where(row_k == block - 1, ends[0:1], 0.0)
    row_b = lax.broadcasted_iota(jnp.int32, (block, block), 0)
    col_b = lax.broadcasted_iota(jnp.int32, (block, block), 1)
    onward = jnp.where(row_b <= col_b, 1.0, 0.0).astype(F32)
    d_step = jnp.dot(onward, d_a, precision=HIGH, preferred_element_type=F32)
    rate = rate_ref[0:1, :]
    slope = jnp.where(
        dt_now < 0.01, dt_now * (1.0 - dt_now * (0.5 - dt_now * (1.0 / 6.0))), 1.0 - jnp.exp(-dt_now)
    )
    d_raw = (direct + rate * d_step) * slope
    ddt_ref[...] = d_raw.astype(BF)
    dhead_ref[0:8, :] += jnp.sum(d_raw.reshape(-1, 8, HEADS_PAD), axis=0)
    dhead_ref[8:16, :] += jnp.sum((dt_now * d_step * rate).reshape(-1, 8, HEADS_PAD), axis=0)
    dstate[...] = dstate[...] * decay[0:1] + dot_tn(c_now, dy_wide)
    def conv_back(here, slope, grad_of, passed_on, taps, sums, dest, j):
        cols = slice(j * 128, j * 128 + 128)
        dpre = grad_of(cols) * slope[:, cols].astype(F32)
        passed_on[j, 0:block, :] = dpre
        x_now = here[:, cols].astype(F32)
        back = jnp.zeros_like(dpre)
        for k in range(4):
            later = dpre if k == 3 else passed_on[j, 3 - k : 3 - k + block, :]
            sums[8 * k : 8 * k + 8, cols] += jnp.sum((later * x_now).reshape(-1, 8, 128), axis=0)
            back += later * taps[k : k + 1, cols]
        dest[:, cols] = back.astype(dest.dtype)

    for j in range(n_b):
        conv_back(
            bcin_ref, sbc_ref, lambda cols: dbco[:, cols], dbp, cbc_ref, dcbc_ref, dbc_ref, j
        )
    for j in range(n_x):
        conv_back(
            xin_ref, sx_ref,
            lambda cols: dxt[:, cols] * dt_wide[:, cols]
            + skip_ref[:, cols] * dy_ref[:, cols].astype(F32),
            dxp, cx_ref, dcx_ref, dxin_ref, j,
        )

    @pl.when(step == pl.num_programs(0) - 1)
    def _():
        row_h = lax.broadcasted_iota(jnp.int32, (HALO, 1), 0)
        for src, taps, dest, edge, given, sums, count in (
            (dxp, cx_ref, dxh_ref, dxc_out, xh_ref, dcx_ref, n_x),
            (dbp, cbc_ref, dbch_ref, dbc_out, bh_ref, dcbc_ref, n_b),
        ):
            for j in range(count):
                cols = slice(j * 128, j * 128 + 128)
                head = src[j, 0:8, :]
                edge[:, cols] = head
                if not final:
                    continue
                acc = jnp.zeros((HALO, 128), F32)
                ahead = given[:, cols].astype(F32)
                for t in range(3):
                    for k in range(t + 1):
                        sums[8 * k : 8 * k + 1, cols] += (
                            ahead[HALO - 3 + t : HALO - 2 + t] * head[t - k : t - k + 1]
                        )
                    total = taps[0:1, cols] * head[t : t + 1]
                    for k in range(1, t + 1):
                        total = total + taps[k : k + 1, cols] * head[t - k : t - k + 1]
                    acc = acc + jnp.where(row_h == HALO - 3 + t, total, 0.0)
                dest[:, cols] = acc.astype(BF)
            if not final:
                dest[...] = jnp.zeros_like(dest)
        if final:
            hgrad_ref[...] = (
                dot_nt(dxh_ref[...], wx_ref[...]) + dot_nt(dbch_ref[...], wbc_ref[...])
            ).astype(BF)
        else:
            hgrad_ref[...] = jnp.zeros_like(hgrad_ref)


def scan_backward(
    top, count, base, xc, bcc, dt, a_cols, ahead, a_rows, dy, rowdot, saved, xin, bcin, slope_x,
    slope_bc,    xh, bh, start, conv_x, conv_bc, skip_row, rate_row, spread, sum_mat, wx, wbc, dend, carried=(),
    in_place=(),
):
    toks, chans = xc.shape
    bcw = bcc.shape[1]
    n_state = bcw // 2
    heads = chans // HP

    def back(width):
        return pl.BlockSpec((BLOCK, width), lambda i: (top - i, 0))

    def part(width):
        return pl.BlockSpec((BLOCK, width), lambda i: (top - i - base, 0))

    fixed = (xh, bh, start, conv_x, conv_bc, skip_row, rate_row, spread, sum_mat, wx, wbc, dend)
    anywhere = pl.BlockSpec(memory_space=pl.ANY)
    runner = call(
        functools.partial(
            scan_back_kernel, top=top, final=top + 1 == count, n_carried=len(carried)
        ),
        (count,),
        [
            back(chans), back(bcw), back(HEADS_PAD), back(HEADS_PAD),
            pl.BlockSpec((8, HEADS_PAD), lambda i: (top - i, 0)),
            pl.BlockSpec((heads, BLOCK), lambda i: (0, top - i)),
            back(chans), back(HEADS_PAD),
            pl.BlockSpec((1, n_state, chans), lambda i: (top - i, 0, 0)),
            part(chans), part(bcw), part(chans), part(bcw),
        ]
        + [whole(v.shape) for v in fixed]
        + [whole(v.shape) for v in carried]
        + [anywhere] * len(in_place),
        [
            back(chans), back(bcw), back(HEADS_PAD), whole((HALO, chans)), whole((HALO, bcw)),
            whole((HALO, wx.shape[0])), whole((32, chans)), whole((32, bcw)), whole((16, HEADS_PAD)),
            whole((n_state, chans)), whole((8, chans)), whole((8, bcw)),
        ],
        [
            out((toks, chans), BF), out((toks, bcw), F32), out((toks, HEADS_PAD), BF),
            out((HALO, chans), BF), out((HALO, bcw), BF), out((HALO, wx.shape[0]), BF),
            out((32, chans), F32), out((32, bcw), F32), out((16, HEADS_PAD), F32),
            out((n_state, chans), F32),
            out((8, chans), F32), out((8, bcw), F32),
        ],
        [
            pltpu.VMEM((BLOCK, chans), BF), pltpu.VMEM((BLOCK, chans), F32),
            pltpu.VMEM((chans // 128, BLOCK + 8, 128), F32),
            pltpu.VMEM((bcw // 128, BLOCK + 8, 128), F32), pltpu.VMEM((BLOCK, bcw), F32),
        ],
        in_place=[(25 + len(carried) + k, k) for k in range(len(in_place))],
        far_off=(9, 10, 11, 12),
        flops=2 * count * BLOCK * BLOCK * chans * 12, nbytes=16 * count * BLOCK * chans,
        vmem=15 * 1024 * 1024,
    )
    return runner, (
        xc, bcc, dt, a_cols, ahead, a_rows, dy, rowdot, saved, xin, bcin, slope_x, slope_bc, *fixed,
        *carried, *in_place,
    )


def input_grad_kernel(
    where_ref, dz_ref, dx_ref, dbc_ref, ddt_ref, wz_ref, wx_ref, wbc_ref, wdt_ref, part_ref
):
    del where_ref
    part = dot_nt(dz_ref[...], wz_ref[...])
    part += dot_nt(dx_ref[...], wx_ref[...])
    part += dot_nt(dbc_ref[...].astype(BF), wbc_ref[...])
    part += dot_nn(ddt_ref[...], wdt_ref[...])
    part_ref[...] = part.astype(part_ref.dtype)


def input_grad(far, place, dz, dxin, dbc, ddt, wz, wx, wbc, wdt):
    toks, chans = dz.shape
    width = wz.shape[0]
    half = toks // 2 // BLOCK

    def moved(w):
        return pl.BlockSpec(
            (BLOCK, w),
            lambda i, where: ((1 - where[3] if far else where[3]) * half + i, 0),
        )

    runner = call(
        input_grad_kernel,
        (half,),
        [
            moved(chans), moved(chans), moved(dbc.shape[1]), moved(HEADS_PAD),
            whole(wz.shape), whole(wx.shape), whole(wbc.shape), whole(wdt.shape),
        ],
        [pl.BlockSpec((BLOCK, width), lambda i, where: (i, 0))],
        [out((toks // 2, width), BF if far else F32)],
        prefetch=1, flops=2 * toks * width * chans, nbytes=4 * toks * chans,
    )
    return runner, (place, dz, dxin, dbc, ddt, wz, wx, wbc, wdt)


def norm_back_kernel(
    where_ref, near_ref, got_ref, res_ref, gain_ref, edge_ref, gres_ref, grad_ref, total
):
    total[...] = near_ref[...] + got_ref[...].astype(F32)
    block, width = total.shape
    last = pl.program_id(0) == pl.num_programs(0) - 1

    @pl.when(jnp.logical_and(last, jnp.logical_and(where_ref[2] == 0, where_ref[3] == 1)))
    def _():
        half = width // 2
        for k in range(2):
            total[block - HALO :, k * half : (k + 1) * half] += edge_ref[
                k * HALO : (k + 1) * HALO, :
            ].astype(F32)

    upper = res_ref[...].astype(F32)
    factor = lax.rsqrt(jnp.mean(upper * upper, axis=-1, keepdims=True) + EPSILON)
    scaled = total[...] * gain_ref[...]
    hat = upper * factor
    inner = jnp.mean(scaled * hat, axis=-1, keepdims=True)
    grad_ref[...] = (gres_ref[...] + factor * (scaled - hat * inner)).astype(BF)


def norm_backward(place, near, got, residual, gain, edge, grad_result):
    toks, width = near.shape

    def plain(w):
        return pl.BlockSpec((BLOCK, w), lambda i, where: (i, 0))

    runner = call(
        norm_back_kernel,
        (toks // BLOCK,),
        [
            plain(width), plain(width), plain(width), whole(gain.shape), whole(edge.shape),
            plain(width),
        ],
        [plain(width)],
        [jax.ShapeDtypeStruct((toks, width), BF)],
        [pltpu.VMEM((BLOCK, width), F32)],
        prefetch=1, nbytes=12 * toks * width, free=(2, 5),
    )
    return runner, (place, near, got, residual, gain, edge, grad_result)


class Moves:
    def __init__(self, n_dp, n_tensor):
        self.n_dp = n_dp
        self.n_all = n_dp * n_tensor
        self.n_tensor = n_tensor
        dp = lax.axis_index("dp")
        tensor = lax.axis_index("tensor")
        self.dp = dp
        self.row = tensor // 2
        self.core = tensor % 2
        self.z = dp // 2
        self.x = dp % 2
        self.place = jnp.stack([self.z, self.x, self.row, self.core]).astype(jnp.int32)

    def swap(self, value, z=0, x=0, y=0, c=0):
        mask = (z * 2 + x) * self.n_tensor + y * 2 + c
        return lax.ppermute(value, AXES, [(i, i ^ mask) for i in range(self.n_all)])

    def up(self, value):
        pairs = [(i, i + 2) for i in range(self.n_all) if i % self.n_tensor < 2]
        return lax.ppermute(value, AXES, pairs)

    def down(self, value):
        pairs = [(i + 2, i) for i in range(self.n_all) if i % self.n_tensor < 2]
        return lax.ppermute(value, AXES, pairs)


def join_kernel(where_ref, mine_ref, theirs_ref, all_ref):
    half = mine_ref.shape[0]
    core = where_ref[3]
    all_ref[pl.ds(pl.multiple_of(core * half, half), half), :] = mine_ref[...]
    all_ref[pl.ds(pl.multiple_of((1 - core) * half, half), half), :] = theirs_ref[...]


def join_tokens(place, mine, theirs):
    shape = (2 * mine.shape[0], mine.shape[1])
    runner = call(
        join_kernel, (1,), [whole(mine.shape)] * 2, [whole(shape)], [out(shape, mine.dtype)],
        prefetch=1, nbytes=8 * mine.size,
    )
    return runner, (place, mine, theirs)


def stack_kernel(first_ref, second_ref, both_ref):
    both_ref[0] = first_ref[...]
    both_ref[1] = second_ref[...]


def stack(first, second):
    runner = call(
        stack_kernel, (1,), [whole(first.shape)] * 2, [whole((2, *first.shape))],
        [out((2, *first.shape), first.dtype)], nbytes=8 * first.size,
    )
    return runner, (first, second)


def spots(z, x):
    for kx in range(2):
        for kz in range(2):
            slab = (z ^ kz) * 2 + (x ^ kx)
            yield 0, kx, kz, slab, 0
            yield 1, kx, kz, slab, 1
    for ky in range(2):
        for kz in range(2):
            yield 2, ky, kz, (z ^ (2 + kz)) * 2 + x, ky
            yield 3, ky, kz, (z ^ (2 + kz)) * 2 + (x ^ 1), ky


def place_first_kernel(where_ref, p0, p1, p2, p3, wx_ref, wbc_ref, wdt_ref, count_ref, msg_ref, dts, *, slab):
    pieces = (p0, p1, p2, p3)
    cols = p0.shape[-1]
    z, x, y = where_ref[0], where_ref[1], where_ref[2]
    bc_rows = slab // 4
    total = jnp.zeros((8, 128), F32)
    for arr, i, j, dp, ky in spots(z, x):
        piece = pieces[arr]
        row0 = pl.multiple_of(dp * slab, slab)
        wx_ref[pl.ds(row0, slab), ky * cols : ky * cols + cols] = piece[i, j, 0:slab, :]
        bc0 = pl.multiple_of(dp * slab + (y ^ ky) * 2 * bc_rows, bc_rows)
        bc1 = pl.multiple_of(dp * slab + (y ^ ky) * 2 * bc_rows + bc_rows, bc_rows)
        wbc_ref[pl.ds(bc0, bc_rows), :] = piece[i, j, slab : slab + bc_rows, 0 : cols // 2]
        wbc_ref[pl.ds(bc1, bc_rows), :] = piece[i, j, slab : slab + bc_rows, cols // 2 : cols]
        extra = piece[i, j, slab + bc_rows : slab + bc_rows + 16, 0:slab].astype(F32)
        dts[ky * 8 : ky * 8 + 8, pl.ds(row0, slab)] = extra[0:8]
        total = total + extra[8:16]
    wdt_ref[...] = jnp.zeros_like(wdt_ref)
    wdt_ref[0:16, :] = dts[...].astype(BF)
    count_ref[...] = jnp.broadcast_to(jnp.sum(total[0:1], axis=1, keepdims=True), (8, 128))
    msg_ref[...] = count_ref[...]


def place_second_kernel(where_ref, p0, p1, p2, p3, wz_ref, wo_ref, *, slab):
    pieces = (p0, p1, p2, p3)
    cols = p0.shape[-1]
    for arr, i, j, dp, ky in spots(where_ref[0], where_ref[1]):
        row0 = pl.multiple_of(dp * slab, slab)
        piece = pieces[arr]
        wz_ref[pl.ds(row0, slab), ky * cols : ky * cols + cols] = piece[i, j, 0:slab, :]
        wo_ref[pl.ds(row0, slab), ky * cols : ky * cols + cols] = piece[i, j, slab : 2 * slab, :]


def first_block_kernel(where_ref, wx_ref, wbc_ref, wdt_ref, valid_ref, block_ref):
    slab, cols = wx_ref.shape
    bc_rows = slab // 4
    block_ref[0:slab, :] = wx_ref[...]
    start = pl.multiple_of(where_ref[2] * 2 * bc_rows, 2 * bc_rows)
    half = wbc_ref[pl.ds(start, 2 * bc_rows), :]
    block_ref[slab : slab + bc_rows, 0 : cols // 2] = half[0:bc_rows]
    block_ref[slab : slab + bc_rows, cols // 2 :] = half[bc_rows:]
    row_i = lax.broadcasted_iota(jnp.int32, (slab, slab), 0)
    col_i = lax.broadcasted_iota(jnp.int32, (slab, slab), 1)
    turn = jnp.where(row_i == col_i, 1.0, 0.0).astype(BF)
    ones = valid_ref[...].astype(F32)
    quarter = ones.shape[1] // 4
    lane = lax.broadcasted_iota(jnp.int32, (8, cols), 1)
    counts = jnp.zeros((8, cols), F32)
    for k in range(4):
        total = jnp.sum(ones[:, k * quarter : (k + 1) * quarter])
        counts = counts + jnp.where(lane == k, total, 0.0)
    row = lax.broadcasted_iota(jnp.int32, (8, cols), 0)
    steps = jnp.concatenate([dot_tn(wdt_ref[...], turn), jnp.zeros((8, cols - slab), F32)], axis=1)
    extra = jnp.concatenate([steps, jnp.where(row == 0, counts, 0.0)], axis=0)
    block_ref[slab + bc_rows :, :] = extra.astype(BF)


def first_block(moves, w_x, w_bc, w_dt, valid):
    slab, cols = w_x.shape
    operands = (w_x, w_bc, w_dt, valid)
    shape = (slab + slab // 4 + 16, cols)
    runner = call(
        first_block_kernel, (1,),
        [pl.BlockSpec(v.shape, lambda i, where: (0, 0)) for v in operands], [whole(shape)],
        [out(shape, BF)], prefetch=1, nbytes=4 * slab * cols, free=(0, 1, 2, 3),
    )
    return runner(moves.place, *operands)[0][0]


def place_first(moves, pieces, slab, bcw):
    cols = pieces[0].shape[-1]
    width = slab * moves.n_dp
    runner = call(
        functools.partial(place_first_kernel, slab=slab),
        (1,),
        [whole(p.shape) for p in pieces],
        [
            whole((width, 2 * cols)), whole((width, bcw)), whole((HEADS_PAD, width)),
            whole((8, 128)), whole((8, 128)),
        ],
        [
            out((width, 2 * cols), BF), out((width, bcw), BF), out((HEADS_PAD, width), BF),
            out((8, 128), F32), out((8, 128), F32),
        ],
        [pltpu.VMEM((16, width), F32)],
        prefetch=1, nbytes=8 * width * cols,
    )
    return runner, (moves.place, *pieces)


def place_second(moves, pieces, slab):
    cols = pieces[0].shape[-1]
    width = slab * moves.n_dp
    runner = call(
        functools.partial(place_second_kernel, slab=slab),
        (1,),
        [whole(p.shape) for p in pieces],
        [whole((width, 2 * cols)), whole((width, 2 * cols))],
        [out((width, 2 * cols), BF), out((width, 2 * cols), BF)],
        prefetch=1, nbytes=16 * width * cols,
    )
    return runner, (moves.place, *pieces)


def gather_any(moves, w_x, w_bc, w_dt, w_z, w_out, valid):
    wide = []
    for weight in (w_x, w_z, w_out):
        own = lax.all_gather(weight, "dp", axis=0, tiled=True)
        wide.append(jnp.concatenate([own, moves.swap(own, y=1)], axis=1))
    wbc = lax.all_gather(w_bc, "dp", axis=0, tiled=True)
    own = lax.all_gather(w_dt, "dp", axis=0, tiled=True).T
    both = jnp.concatenate([own, moves.swap(own, y=1)], axis=0)
    wdt = jnp.zeros((HEADS_PAD, both.shape[1]), BF).at[0 : both.shape[0]].set(both)
    count = lax.psum(jnp.sum(valid), AXES)
    return (*wide, wbc, wdt, jnp.full((8, 128), count, F32))


def split_rows(hold, z, x, cols, a_own, a_msg, b_own, b_msg, step, slab, at, stride):
    def slabs(k):
        base = (k ^ (z % 2)) * 2 * slab
        near = hold[pl.ds(pl.multiple_of(base + x * slab, slab), slab), :].astype(BF)
        far = hold[pl.ds(pl.multiple_of(base + (1 - x) * slab, slab), slab), :].astype(BF)
        first = slice(2 * k * stride + at, 2 * k * stride + at + slab)
        second = slice((2 * k + 1) * stride + at, (2 * k + 1) * stride + at + slab)
        return near, far, first, second

    @pl.when(step == 0)
    def _():
        for k in range(2):
            near, far, first, second = slabs(k)
            a_own[first, :] = near[:, 0:cols]
            a_own[second, :] = far[:, 0:cols]
            a_msg[first, :] = near[:, cols:]
            a_msg[second, :] = far[:, cols:]

    @pl.when(step == 1)
    def _():
        for k in range(2):
            near, far, first, second = slabs(k)
            b_own[first, :] = near[:, 0:cols]
            b_own[second, :] = near[:, cols:]
            b_msg[first, :] = far[:, 0:cols]
            b_msg[second, :] = far[:, cols:]


def row_sums(weight, grad):
    total = jnp.zeros((grad.shape[0], 128), F32)
    for col in range(0, grad.shape[1], 128):
        total += weight[:, col : col + 128].astype(F32) * grad[:, col : col + 128]
    ones = jnp.ones((8, 128), BF)
    high, rest = split_low(total)
    return (dot_nt(ones, high) + dot_nt(ones, rest))[0:1]


def two_grads_kernel(
    where_ref, n_ref, dz_ref, gs_ref, gsgot_ref, u_ref, wz_ref, a_own, a_msg, b_own, b_msg,
    gain_ref, hold, *, slab,
):
    step = pl.program_id(0)
    cols = a_own.shape[-1]
    x = where_ref[1]
    z = where_ref[0]
    pair = (z // 2) ^ step
    outs = (a_own, a_msg, b_own, b_msg)
    hold[...] = dot_tn(n_ref[...], dz_ref[...])
    gain_ref[pl.ds(pair, 1), :] = row_sums(wz_ref[...], hold)
    split_rows(hold, z, x, cols, *outs, step, slab, 0, 2 * slab)
    half = gs_ref.shape[0]
    core = where_ref[3]
    u_own = u_ref[pl.ds(pl.multiple_of(core * half, half), half), :]
    u_other = u_ref[pl.ds(pl.multiple_of((1 - core) * half, half), half), :]
    hold[...] = dot_tn(gs_ref[...], u_own) + dot_tn(gsgot_ref[...], u_other)
    split_rows(hold, z, x, cols, *outs, step, slab, slab, 2 * slab)


def two_grads(moves, n_full, dz, gs, gs_got, u, wz):
    toks, width = n_full.shape
    chans = dz.shape[1]
    cols = chans // 2
    slab = width // 8
    lane_block = pl.BlockSpec((toks, 4 * slab), lambda i, where: (0, (where[0] // 2) ^ i))
    half_block = pl.BlockSpec((toks // 2, 4 * slab), lambda i, where: (0, (where[0] // 2) ^ i))
    shapes = [out((8 * slab, cols), BF)] * 4 + [out((2, 4 * slab), F32)]
    runner = call(
        functools.partial(two_grads_kernel, slab=slab),
        (2,),
        [
            lane_block, whole(dz.shape), half_block, half_block, whole(u.shape),
            pl.BlockSpec((4 * slab, chans), lambda i, where: ((where[0] // 2) ^ i, 0)),
        ],
        [whole(v.shape) for v in shapes],
        shapes,
        [pltpu.VMEM((4 * slab, chans), F32)],
        prefetch=1, flops=4 * toks * width * chans, nbytes=16 * toks * chans,
    )
    return runner, (moves.place, n_full, dz, gs, gs_got, u, wz)


RIDE_VALUES = 16
RIDE_ROWS = 48


def last_grads_kernel(
    where_ref, n_ref, halo_ref, dx_ref, dxh_ref, dbc_ref, dbcgot_ref, dbch_ref, dbchgot_ref,
    hgrad_ref, hgradgot_ref, ddt_ref, wx_ref, wbc_ref, wdt_ref, gainz_ref, dcx_ref, dcbc_ref,
    dgate_ref, dskip_ref, dhead_ref, loss_ref, gain_ref, sum_ref,
    a_own, a_msg, b_own, b_msg, ride_ref, hold, hold_bc, dbc_high, dbc_rest, gains, dwdt, values,
    *, slab,
):
    step = pl.program_id(0)
    cols = a_own.shape[-1]
    z, x, y, core = where_ref[0], where_ref[1], where_ref[2], where_ref[3]
    pair = (z // 2) ^ step
    eighth = slab // 4
    stride = slab + eighth

    @pl.when(step == 0)
    def _():
        dbc_high[...], dbc_rest[...] = split_low(dbc_ref[...] + dbcgot_ref[...])

    n_now = n_ref[...]
    halo = halo_ref[...]
    hold[...] = dot_tn(n_now, dx_ref[...]) + dot_tn(halo, dxh_ref[...])
    dbch_sum = (dbch_ref[...].astype(F32) + dbchgot_ref[...].astype(F32)).astype(BF)
    grad_bc = dot_tn(n_now, dbc_high[...]) + dot_tn(n_now, dbc_rest[...]) + dot_tn(halo, dbch_sum)
    grad_dt = dot_tn(ddt_ref[...], n_now)
    slabs = pl.ds(pl.multiple_of(pair * 4 * slab, 4 * slab), 4 * slab)
    dwdt[:, slabs] = grad_dt[0:16]
    sums = row_sums(wx_ref[...], hold) + 0.5 * row_sums(wbc_ref[...], grad_bc)
    sums += jnp.sum(grad_dt * wdt_ref[...].astype(F32), axis=0, keepdims=True)
    gains[0:1, slabs] = sums + gainz_ref[pl.ds(pair, 1), :]
    split_rows(hold, z, x, cols, a_own, a_msg, b_own, b_msg, step, slab, 0, stride)
    hold_bc[...] = grad_bc

    def bc_block(k, kx):
        base = (k ^ (z % 2)) * 2 * slab
        start = pl.multiple_of(base + (x ^ kx) * slab + core * 2 * eighth, eighth)
        block = hold_bc[pl.ds(start, 2 * eighth), :].astype(BF)
        return jnp.concatenate([block[0:eighth], block[eighth:]], axis=1)

    def bc_rows(k, i):
        return slice((2 * k + i) * stride + slab, (2 * k + i) * stride + slab + eighth)

    @pl.when(step == 0)
    def _():
        for k in range(2):
            for i in range(2):
                a_own[bc_rows(k, i), :] = bc_block(k, i)
                a_msg[bc_rows(k, i), :] = bc_block(k, i)

    @pl.when(step == 1)
    def _():
        for k in range(2):
            for i in range(2):
                b_own[bc_rows(k, i), :] = bc_block(k, 0)
                b_msg[bc_rows(k, i), :] = bc_block(k, 1)

    @pl.when(step == pl.num_programs(0) - 1)
    def _():
        values[...] = jnp.zeros_like(values)

        def per_channel(row, step_rows, total):
            mine, others = total[:, 0:cols], total[:, cols:]
            first_chip = jnp.where(y == 0, mine, others)
            second_chip = jnp.where(y == 0, others, mine)
            values[row : row + 1, :] = first_chip
            values[row + step_rows : row + step_rows + 1, :] = second_chip

        for k in range(4):
            per_channel(k, 4, jnp.sum(dcx_ref[8 * k : 8 * k + 8, :], axis=0, keepdims=True))
            values[12 + k // 2 : 13 + k // 2, (k % 2) * 256 : (k % 2) * 256 + 256] = jnp.sum(
                dcbc_ref[8 * k : 8 * k + 8, :], axis=0, keepdims=True
            )
        per_channel(8, 1, jnp.sum(dgate_ref[...], axis=0, keepdims=True))
        gain_total = gains[0:1, :] / gain_ref[...]
        values[10:11, :] = gain_total[:, 0:cols]
        values[11:12, :] = gain_total[:, cols:]
        skips = per_head(dskip_ref[...], sum_ref[...])
        heads = [
            jnp.sum(v, axis=0, keepdims=True)
            for v in (dhead_ref[0:8, :], dhead_ref[8:16, :], skips)
        ]
        loss = jnp.sum(loss_ref[...]) * jnp.where(
            lax.broadcasted_iota(jnp.int32, (1, 128), 1) == 0, 1.0, 0.0
        )
        for k, value in enumerate(heads):
            at = slice(k * 128, k * 128 + 128)
            turned_value = pltpu.roll(jnp.broadcast_to(value, (8, 128)), 120, 1)[0:1]
            values[14:15, at] = jnp.where(y == 0, value, turned_value)
            values[15:16, at] = jnp.where(y == 0, turned_value, value)
        values[14:15, 384:512] = jnp.where(y == 0, loss, 0.0)
        values[15:16, 384:512] = jnp.where(y == 0, 0.0, loss)
        sums_now = values[...]
        row = lax.broadcasted_iota(jnp.int32, sums_now.shape, 0)
        ride_ref[0:16, :] = jnp.where(
            row >= RIDE_VALUES - 2, two_parts(sums_now).astype(F32), sums_now
        ).astype(BF)
        grads = dwdt[...]
        turned_grads = jnp.concatenate([grads[8:16], grads[0:8]], axis=0)
        grads = jnp.where(y == 0, grads, turned_grads).astype(BF)
        ride_ref[16:32, :] = grads[:, 0:cols]
        ride_ref[32:48, :] = grads[:, cols:]
        a_msg[4 * stride : 4 * stride + RIDE_ROWS, :] = ride_ref[...]
        edge = add_low(hgrad_ref[...], hgradgot_ref[...])
        for k in range(2):
            at = 4 * stride + RIDE_ROWS + k * HALO
            a_msg[at : at + HALO, :] = edge[:, k * cols : (k + 1) * cols]


def last_grads(moves, n_full, halo, dxin, dxh, dbcs, edges, ddt, wx, wbc, wdt, small):
    toks, width = n_full.shape
    chans = dxin.shape[1]
    bcw = dbcs[0].shape[1]
    cols = chans // 2
    slab = width // 8
    stride = slab + slab // 4
    lane_block = pl.BlockSpec((toks, 4 * slab), lambda i, where: (0, (where[0] // 2) ^ i))
    shapes = [
        out((4 * stride, cols), BF), out((4 * stride + RIDE_ROWS + 2 * HALO, cols), BF),
        out((4 * stride, cols), BF), out((4 * stride, cols), BF), out((RIDE_ROWS, cols), BF),
    ]
    runner = call(
        functools.partial(last_grads_kernel, slab=slab),
        (2,),
        [
            lane_block, pl.BlockSpec((HALO, 4 * slab), lambda i, where: (0, (where[0] // 2) ^ i)),
            whole(dxin.shape), whole(dxh.shape),
            *[whole(v.shape) for v in (*dbcs, *edges)], whole(ddt.shape),
            pl.BlockSpec((4 * slab, chans), lambda i, where: ((where[0] // 2) ^ i, 0)),
            pl.BlockSpec((4 * slab, bcw), lambda i, where: ((where[0] // 2) ^ i, 0)),
            pl.BlockSpec((HEADS_PAD, 4 * slab), lambda i, where: (0, (where[0] // 2) ^ i)),
            *[whole(v.shape) for v in small],
        ],
        [whole(v.shape) for v in shapes],
        shapes,
        [
            pltpu.VMEM((4 * slab, chans), F32), pltpu.VMEM((4 * slab, bcw), F32),
            pltpu.VMEM((toks, bcw), BF), pltpu.VMEM((toks, bcw), BF), pltpu.VMEM((8, width), F32), pltpu.VMEM((16, width), F32),
            pltpu.VMEM((RIDE_VALUES, cols), F32),
        ],
        prefetch=1, flops=2 * toks * width * chans, nbytes=16 * toks * chans,
    )
    return runner, (
        moves.place, n_full, halo, dxin, dxh, *dbcs, *edges, ddt, wx, wbc, wdt, *small
    )


def add_low(first, second):
    return (first.astype(F32) + second.astype(F32)).astype(BF)


LOSS_LANE = 384


def two_parts(values):
    lane = lax.broadcasted_iota(jnp.int32, values.shape, 1)
    rest = pltpu.roll(values - values.astype(BF).astype(F32), 1, 1)
    return jnp.where(lane == LOSS_LANE + 1, rest, values).astype(BF)


def join_parts(ride):
    values = ride.astype(F32)
    lane = lax.broadcasted_iota(jnp.int32, values.shape, 1)
    last = lane == LOSS_LANE + 1
    whole_loss = values + jnp.where(
        lane == LOSS_LANE, pltpu.roll(values, values.shape[1] - 1, 1), 0.0
    )
    row = lax.broadcasted_iota(jnp.int32, values.shape, 0)
    tail = row >= RIDE_VALUES - 2
    return jnp.where(tail, jnp.where(last, 0.0, whole_loss), values)


def add_ride(first, second):
    total = join_parts(first[0:16]) + join_parts(second[0:16])
    row = lax.broadcasted_iota(jnp.int32, total.shape, 0)
    sums = jnp.where(row >= RIDE_VALUES - 2, two_parts(total).astype(F32), total).astype(BF)
    return jnp.concatenate([sums, add_low(first[16:], second[16:])], axis=0)


def fold_first_kernel(*refs, stride, ride):
    if ride:
        a_own, a_got, b_own, b_got, ride_ref, a_keep, a_msg, b_keep, b_msg, ride_out, edge = refs
    else:
        a_own, a_got, b_own, b_got, a_keep, a_msg, b_keep, b_msg = refs
    for own, got, keep, msg in ((a_own, a_got, a_keep, a_msg), (b_own, b_got, b_keep, b_msg)):
        for z in range(2):
            to = slice(z * stride, (z + 1) * stride)
            for i, dest in enumerate((keep, msg)):
                at = slice((2 * z + i) * stride, (2 * z + i + 1) * stride)
                dest[to, :] = add_low(own[at, :], got[at, :])
    if ride:
        total = add_ride(ride_ref[...], a_got[4 * stride : 4 * stride + RIDE_ROWS, :])
        ride_out[...] = total
        a_msg[2 * stride : 2 * stride + RIDE_ROWS, :] = total
        edge[...] = a_got[4 * stride + RIDE_ROWS :, :]


def fold_first(stride, a_own, a_got, b_own, b_got, ride=None):
    cols = a_own.shape[-1]
    n_ride = 0 if ride is None else RIDE_ROWS
    operands = (a_own, a_got, b_own, b_got) + (() if ride is None else (ride,))
    shapes = [
        out((2 * stride, cols), BF), out((2 * stride + n_ride, cols), BF),
        out((2 * stride, cols), BF), out((2 * stride, cols), BF),
    ] + ([] if ride is None else [out((RIDE_ROWS, cols), BF), out((2 * HALO, cols), BF)])
    runner = call(
        functools.partial(fold_first_kernel, stride=stride, ride=n_ride > 0),
        (1,), [whole(v.shape) for v in operands], [whole(v.shape) for v in shapes], shapes,
        nbytes=24 * stride * cols,
    )
    return runner, operands


def fold_second_kernel(*refs, stride, ride):
    if ride:
        a_own, a_got, b_own, b_got, ride_ref, own, far, msg, ride_out = refs
    else:
        a_own, a_got, b_own, b_got, own, far, msg = refs
    low, high = slice(0, stride), slice(stride, 2 * stride)
    own[...] = add_low(a_own[low, :], a_got[low, :])
    far[...] = add_low(b_own[low, :], b_got[low, :])
    msg[low, :] = add_low(a_own[high, :], a_got[high, :])
    msg[high, :] = add_low(b_own[high, :], b_got[high, :])
    if ride:
        total = add_ride(ride_ref[...], a_got[2 * stride : 2 * stride + RIDE_ROWS, :])
        ride_out[...] = total
        msg[2 * stride : 2 * stride + RIDE_ROWS, :] = total


def fold_second(stride, a_own, a_got, b_own, b_got, ride=None):
    cols = a_own.shape[-1]
    n_ride = 0 if ride is None else RIDE_ROWS
    operands = (a_own, a_got, b_own, b_got) + (() if ride is None else (ride,))
    shapes = [out((stride, cols), BF)] * 2 + [out((2 * stride + n_ride, cols), BF)]
    if ride is not None:
        shapes = shapes + [out((RIDE_ROWS, cols), BF)]
    runner = call(
        functools.partial(fold_second_kernel, stride=stride, ride=n_ride > 0),
        (1,), [whole(v.shape) for v in operands], [whole(v.shape) for v in shapes], shapes,
        nbytes=16 * stride * cols,
    )
    return runner, operands


def fold_third_kernel(*refs, stride, ride):
    if ride:
        own, far, got, ride_ref, keep, msg, ride_out = refs
    else:
        own, far, got, keep, msg = refs
    keep[...] = add_low(own[...], got[0:stride, :])
    msg[0:stride, :] = add_low(far[...], got[stride : 2 * stride, :])
    if ride:
        total = add_ride(ride_ref[...], got[2 * stride : 2 * stride + RIDE_ROWS, :])
        ride_out[...] = total
        msg[stride : stride + RIDE_ROWS, :] = total


def fold_third(stride, own, far, got, ride=None):
    cols = own.shape[-1]
    n_ride = 0 if ride is None else RIDE_ROWS
    operands = (own, far, got) + (() if ride is None else (ride,))
    shapes = [out((stride, cols), BF), out((stride + n_ride, cols), BF)]
    if ride is not None:
        shapes = shapes + [out((RIDE_ROWS, cols), BF)]
    runner = call(
        functools.partial(fold_third_kernel, stride=stride, ride=n_ride > 0),
        (1,), [whole(v.shape) for v in operands], [whole(v.shape) for v in shapes], shapes,
        nbytes=8 * stride * cols,
    )
    return runner, operands


def fold_two_kernel(own, got, first, second):
    slab = first.shape[0]
    for at, dest in ((0, first), (slab, second)):
        dest[...] = own[at : at + slab, :].astype(F32) + got[at : at + slab, :].astype(F32)


def fold_two(own, got):
    rows_all, cols = own.shape
    shapes = [jax.ShapeDtypeStruct((rows_all // 2, cols), F32)] * 2
    runner = call(
        fold_two_kernel, (1,), [whole(own.shape)] * 2, [whole(v.shape) for v in shapes], shapes,
        nbytes=12 * rows_all * cols,
    )
    return runner, (own, got)


def fold_last_kernel(
    where_ref, own, got, ride, wx_ref, cx_ref, gate_ref, heads_ref, dt_ref, swap_ref,
    values, dts, *, slab,
):
    stride = own.shape[0]
    total = own[...].astype(F32) + got[0:stride, :].astype(F32)
    wx_ref[...] = total[0:slab]
    values[...] = join_parts(ride[0:16, :]) + join_parts(got[stride : stride + 16, :])
    dts[...] = ride[16:48, :].astype(F32) + got[stride + 16 : stride + 48, :].astype(F32)
    y, z, x = where_ref[2], where_ref[0], where_ref[1]
    sums = values[...]
    cx_ref[...] = jnp.where(y == 0, sums[0:4], sums[4:8])
    gate_ref[...] = jnp.where(y == 0, sums[8:9], sums[9:10])
    heads_ref[...] = jnp.where(y == 0, sums[14:15], sums[15:16])
    slabs = dts.shape[1] // slab
    picked = jnp.zeros((8, slab), F32)
    for dp in range(2 * slabs):
        at = (dp % slabs) * slab
        block = dts[(dp // slabs) * 16 : (dp // slabs) * 16 + 16, at : at + slab]
        block = jnp.where(y == 0, block[0:8], block[8:16])
        picked = picked + jnp.where(z * 2 + x == dp, block, 0.0)
    dt_ref[...] = jnp.concatenate([picked, jnp.zeros((slab - 8, slab), F32)], axis=0).T[:, 0:8]
    swap_ref[0 : stride - slab, :] = total[slab:stride]
    swap_ref[stride - slab : stride - slab + 8, :] = jnp.concatenate(
        [sums[10:14], sums[14:16], jnp.zeros_like(sums[0:2])], axis=0
    )


def end_kernel(where_ref, mine, theirs, bc_ref, conv_ref, gain_ref, loss_ref):
    n_bc = mine.shape[0] - 8
    bcw = bc_ref.shape[1]
    core = where_ref[3]
    for part, at in ((mine, core), (theirs, 1 - core)):
        for k in range(2):
            row0 = pl.multiple_of((at * 2 + k) * n_bc, n_bc)
            bc_ref[pl.ds(row0, n_bc), :] = part[0:n_bc, k * bcw : (k + 1) * bcw]
    shared = mine[n_bc:, :] + theirs[n_bc:, :]
    for k in range(2):
        gain_ref[:, k * 2 * bcw : (k + 1) * 2 * bcw] = shared[k : k + 1]
    for k in range(4):
        conv_ref[k : k + 1, :] = shared[2 + k // 2 : 3 + k // 2, (k % 2) * bcw : (k % 2 + 1) * bcw]
    loss_ref[...] = shared[4:5, LOSS_LANE : LOSS_LANE + 1] + shared[5:6, LOSS_LANE : LOSS_LANE + 1]


def finish(place, mine, theirs, slab, bcw):
    shapes = [
        jax.ShapeDtypeStruct((slab, bcw), F32), jax.ShapeDtypeStruct((4, bcw), F32),
        jax.ShapeDtypeStruct((1, 4 * bcw), F32), jax.ShapeDtypeStruct((1, 1), F32),
    ]
    runner = call(
        end_kernel, (1,), [whole(mine.shape)] * 2, [whole(v.shape) for v in shapes], shapes,
        prefetch=1, nbytes=4 * slab * bcw,
    )
    return runner, (place, mine, theirs)


def fold_last(place, slab, own, got, ride):
    stride, cols = own.shape
    shapes = [
        jax.ShapeDtypeStruct((slab, cols), F32), jax.ShapeDtypeStruct((4, cols), F32),
        out((1, cols), F32), out((1, cols), F32), jax.ShapeDtypeStruct((slab, 8), F32),
        out((stride - slab + 8, cols), F32),
    ]
    operands = (own, got, ride)
    runner = call(
        functools.partial(fold_last_kernel, slab=slab), (1,),
        [whole(v.shape) for v in operands], [whole(v.shape) for v in shapes], shapes,
        [pltpu.VMEM((RIDE_VALUES, cols), F32), pltpu.VMEM((32, cols), F32)],
        prefetch=1, nbytes=20 * stride * cols,
    )
    return runner, (place, *operands)


def body(
    residual, teacher, valid_mask, gain_in, w_z, w_x, w_bc, w_dt, conv_x, conv_bc, dt_bias, a_log,
    d_skip, gain_gate, w_out,
):
    _, pos_dev, width = residual.shape
    n_tensor = lax.axis_size("tensor")
    n_dp = lax.axis_size("dp")
    moves = Moves(n_dp, n_tensor)
    tokens_all = pos_dev * n_tensor * n_dp
    cols = w_z.shape[1]
    chans = 2 * cols
    own_heads = w_dt.shape[1]
    heads = 2 * own_heads
    inner = cols * n_tensor
    bcw = w_bc.shape[1]
    slab = w_z.shape[0]
    toks = 2 * pos_dev
    core = moves.core
    nb = toks // BLOCK
    by_permutes = n_dp == 8
    res_rows = residual.reshape(pos_dev, width)

    valid = valid_mask.reshape(pos_dev).astype(F32)
    if by_permutes:
        block1 = first_block(moves, w_x, w_bc, w_dt, valid_mask)
        others1 = [moves.swap(block1, z=k) for k in (1, 2, 3)]
        block2 = jnp.concatenate([w_z, w_out], axis=0)

    pack = jnp.concatenate(
        [
            conv_x, gain_gate[None],
            jnp.concatenate(
                [dt_bias, a_log, d_skip, jnp.zeros((cols - 3 * own_heads,), F32)]
            )[None],
            jnp.zeros((2, cols), F32),
            res_rows[pos_dev - HALO // 2 :].astype(F32).reshape(-1, cols),
        ],
        axis=0,
    )
    pack_other = moves.swap(pack, y=1)
    rows_ahead = pack_other[8:].reshape(HALO // 2, width)
    rows_ahead = jnp.where(core == 1, rows_ahead, moves.swap(rows_ahead, c=1))
    conv_x_core = jnp.concatenate([pack[0:4], pack_other[0:4]], axis=1)
    gain_row = jnp.concatenate([pack[4:5], pack_other[4:5]], axis=1)

    def head_param(k):
        at = slice(k * own_heads, (k + 1) * own_heads)
        return jnp.concatenate([pack[5, at], pack_other[5, at]])

    def pad_heads(values):
        return jnp.concatenate([values, jnp.zeros((HEADS_PAD - heads,), F32)])

    bias_col = pad_heads(head_param(0))[:, None]
    rates = pad_heads(-jnp.exp(head_param(1)))
    skip_row = jnp.repeat(head_param(2), HP)[None]
    head_of = (jnp.arange(chans) // HP)[None, :]
    lanes = jnp.arange(HEADS_PAD)[:, None]

    def norm(values):
        factor = lax.rsqrt(jnp.mean(values * values, axis=-1, keepdims=True) + EPSILON)
        return (values * factor * gain_in).astype(BF)

    normed = norm(res_rows.astype(F32))
    normed_other = moves.swap(normed, c=1)
    halo_rows = jnp.where(moves.row == 1, norm(rows_ahead), jnp.zeros((), BF))
    halo_rows = jnp.concatenate([jnp.zeros_like(halo_rows), halo_rows], axis=0)

    ch = Chain()
    halo = ch.hold(halo_rows)
    spread = ch.hold((lanes % (HEADS_PAD // 2) == head_of).astype(BF))
    sum_mat = ch.hold((lanes == head_of).astype(BF).T)
    conv_xs, conv_bcs, bias, rate_col, rate_row, skip, gain, gain_ins, valid_col = ch.hold(
        conv_x_core, conv_bc, bias_col, rates[:, None], rates[None, :], skip_row, gain_row,
        gain_in[None], valid[:, None],
    )
    n = ch.run(join_tokens(moves.place, normed, normed_other))

    def stacked(first, second):
        return ch.drop(ch.run(stack(first, second)))

    if by_permutes:
        a1 = stacked(block1, others1[0])
        a1x = moves.swap(a1, x=1)
        block2_held = ch.hold(block2)
        b1 = stacked(others1[1], others1[2])
        b1y = moves.swap(b1, y=1)
        block2 = ch.drop(block2_held)
        others2 = [moves.swap(block2, z=k) for k in (1, 2, 3)]
        a1, a1x, b1y, others2[0] = lax.optimization_barrier((a1, a1x, b1y, others2[0]))
        a1 = stacked(a1, a1x)
        a1y = moves.swap(a1, y=1)
        b1 = stacked(b1, b1y)
        b1x = moves.swap(b1, x=1)
        wx, wbc, wdt, count, count_msg = ch.run(
            place_first(moves, (a1, a1y, b1, b1x), slab, bcw)
        )
        count_other = moves.swap(ch.drop(count_msg), c=1)
        a2 = stacked(block2, others2[0])
        b2 = stacked(others2[1], others2[2])
        a2x = moves.swap(a2, x=1)
        b2y = moves.swap(b2, y=1)
    else:
        *weights, counted = gather_any(moves, w_x, w_bc, w_dt, w_z, w_out, valid)
        wx, wz, wo, wbc, wdt, count = ch.hold(*weights, counted)
        count_other = jnp.zeros_like(counted)

    def run_front(first, count_, wide, passed):
        carried = ch.drop(*passed, *wide) if first else ()
        results = ch.run(
            front(
                first, count_,
                *now(n, halo, wx, wbc, wdt, conv_xs, conv_bcs, bias, rate_col, spread), carried,
            )
        )
        return results[:8], ch.drop(*results[8:12]), results[12:16], results[16], results[17:]

    front_split = FRONT_SPLIT if by_permutes else nb
    wide, first_part, passed, end, (x_halo, bc_halo) = run_front(0, front_split, (), ())
    last_part = first_part
    if by_permutes:
        a2 = stacked(a2, a2x)
        a2y = moves.swap(a2, y=1)
        b2 = stacked(b2, b2y)
        b2x = moves.swap(b2, x=1)
    if front_split < nb:
        ch.drop(end)
        wide, last_part, passed, end, unused = run_front(
            front_split, nb - front_split, wide, passed
        )
        ch.drop(*unused)
    ch.drop(*passed)
    xc, bcc, dt, a_cols, ahead, a_rows, y, saved = wide
    start_got = moves.up(ch.drop(end))
    if by_permutes:
        wz, wo = ch.run(place_second(moves, (a2, a2y, b2, b2x), slab))
    start = ch.hold(start_got)

    given = (n, y, xc, bcc, a_cols, ahead, start, wz, wo, skip, gain, spread)
    gate, far, far_sq = ch.run(gate_out_proj(True, moves.place, *now(*given)))
    far_got = moves.swap(ch.drop(far), c=1)
    sq_got = moves.swap(ch.drop(far_sq), c=1)
    gate_value = ch.drop(gate)
    gate, near, near_sq = ch.run(
        gate_out_proj(False, moves.place, *now(*given), in_place=(gate_value,))
    )
    mixed, grad_result, gs, gs_msg, q, loss_part = ch.run(
        loss_step(
            ch.drop(near), far_got, ch.drop(near_sq), sq_got, res_rows,
            teacher.reshape(pos_dev, width), ch.drop(valid_col), count.value, count_other, inner,
            tokens_all,
        )
    )
    mixed, grad_result = ch.drop(mixed, grad_result)
    gs_got = moves.swap(ch.drop(gs_msg), c=1)
    q_got = moves.swap(q.value, c=1)
    given = (wo, y, xc, gate, a_cols, ahead, bcc, start, skip, gain, spread, sum_mat)
    q_value = ch.drop(q)
    dz, dy, rowdot, u, dstart, dgate, dskip, dlow = ch.run(
        gate_backward(moves.place, gs.value, q_value, *now(*given))
    )
    ch.drop(dlow)
    in_place = ch.drop(dz, dy, rowdot, u)
    sums = ch.drop(dstart, dgate, dskip)
    operands = now(*given)
    ch.drop(gate, wo, y)
    gs_other = ch.hold(gs_got)
    dz, dy, rowdot, u, dstart, dgate, dskip, dlow = ch.run(
        gate_backward(moves.place, gs_got, q_got, *operands, sums=sums, in_place=in_place)
    )
    ch.drop(dstart)
    dend = moves.down(ch.drop(dlow))

    if by_permutes:
        prepared = two_grads(moves, *now(n, dz, gs, gs_other, u, wz))
        ch.drop(gs, gs_other, u)
        za, za_msg, zb, zb_msg, gain_z = ch.run(prepared)
        za_sent, zb_sent, dend = lax.optimization_barrier((*ch.drop(za_msg, zb_msg), dend))
        za_got = moves.swap(za_sent, y=1)
        zb_got = moves.swap(zb_sent, x=1)
    else:
        grad_z = dot_tn(n.value, dz.value)
        gs_all = jnp.where(
            core == 0,
            jnp.concatenate(now(gs, gs_other), axis=0),
            jnp.concatenate(now(gs_other, gs), axis=0),
        )
        grad_o = dot_tn(gs_all, u.value)
        ch.drop(gs, gs_other, u)

    first_given = (xc, bcc, dt, a_cols, ahead, a_rows, dy, rowdot, saved)
    last_given = (
        x_halo, bc_halo, start, conv_xs, conv_bcs, skip, rate_row, spread, sum_mat, wx, wbc,
    )

    def run_back(top, count_, base, part, whole_out, carried):
        whole_out = ch.drop(*whole_out) if whole_out else ()
        carried = ch.drop(*carried) if carried else ()
        prepared = scan_backward(
            top, count_, base, *now(*first_given), *part, *now(*last_given), dend, carried,
            whole_out,
        )
        if top + 1 == count_:
            ch.drop(*first_given, *last_given[:-4])
        results = ch.run(prepared)
        return results[:3], results[3:6], results[6:]

    back_split = nb - front_split if by_permutes else nb
    whole_out, edges, carried = run_back(nb - 1, back_split, nb - back_split, last_part, (), ())
    if by_permutes:
        za, za_msg, zb, zb_msg = ch.run(
            fold_first(2 * slab, ch.drop(za), za_got, ch.drop(zb), zb_got)
        )
        za_got = moves.swap(ch.drop(za_msg), x=1)
        zb_got = moves.swap(ch.drop(zb_msg), y=1)
    if back_split < nb:
        ch.drop(*edges)
        whole_out, edges, carried = run_back(
            nb - 1 - back_split, nb - back_split, 0, first_part, whole_out, carried
        )
    dxin, dbc, ddt = whole_out
    dxh, dbch, halo_out = edges
    dcx, dcbc, dhead = carried[:3]
    ch.drop(*carried[3:])

    if by_permutes:
        dbc_got = moves.swap(dbc.value, c=1)
        dbch_got = moves.swap(dbch.value, c=1)
        halo_got = moves.swap(halo_out.value, c=1)
        small = ch.drop(gain_z, dcx, dcbc, dgate, dskip, dhead, loss_part)
        small += now(gain_ins, sum_mat)
        prepared = last_grads(
            moves, *now(n, halo, dxin, dxh), (dbc.value, dbc_got, dbch.value, dbch_got),
            (halo_out.value, halo_got), *now(ddt, wx, wbc, wdt), small,
        )
        ch.drop(n, halo, dxh, dbch, halo_out)
        xa, xa_msg, xb, xb_msg, ride = ch.run(prepared)
        xb_got = moves.swap(ch.drop(xb_msg), x=1)
        xa_got = moves.swap(ch.drop(xa_msg), y=1)
        z_own, z_far, z_msg = ch.run(
            fold_second(2 * slab, ch.drop(za), za_got, ch.drop(zb), zb_got)
        )
        z_got = moves.swap(ch.drop(z_msg), z=1)
    else:
        halo_sum = moves.down(add_low(halo_out.value, moves.swap(halo_out.value, c=1)))
        grad_x = dot_tn(n.value, dxin.value) + dot_tn(halo.value, dxh.value)
        grad_bc = dot_tn(n.value, dbc.value.astype(BF)) + dot_tn(halo.value, dbch.value)
        grad_dt = dot_tn(ddt.value, n.value)[0:heads]
        gain_sum = jnp.sum(wz.value.astype(F32) * grad_z, axis=1)
        gain_sum += jnp.sum(wx.value.astype(F32) * grad_x, axis=1)
        gain_sum += jnp.sum(wbc.value.astype(F32) * grad_bc, axis=1)
        gain_sum += jnp.sum(wdt.value[0:heads].astype(F32) * grad_dt, axis=0)

    given = (dz, dxin, dbc, ddt)
    weights = (wz, wx, wbc, wdt)
    far = ch.run(input_grad(True, moves.place, *now(*given), *now(*weights)))
    far_got = moves.swap(ch.drop(far), c=1)
    prepared = input_grad(False, moves.place, *now(*given), *now(*weights))
    ch.drop(*given, *weights)
    near = ch.run(prepared)
    stride = slab + slab // 4
    if by_permutes:
        xa, xa_msg, xb, xb_msg, ride, edge = ch.run(
            fold_first(stride, ch.drop(xa), xa_got, ch.drop(xb), xb_got, ch.drop(ride))
        )
        xa_got = moves.swap(ch.drop(xa_msg), x=1)
        xb_got = moves.swap(ch.drop(xb_msg), y=1)
    else:
        edge = ch.hold(jnp.concatenate([halo_sum[:, :cols], halo_sum[:, cols:]], axis=0))
    grad_residual = ch.drop(
        ch.run(
            norm_backward(
                moves.place, ch.drop(near), far_got, res_rows, gain_ins.value, ch.drop(edge),
                grad_result,
            )
        )
    )
    count_total = count.value[0, 0] + count_other[0, 0]

    if by_permutes:
        z_own, z_msg = ch.run(fold_third(2 * slab, ch.drop(z_own), ch.drop(z_far), z_got))
        z_got = moves.swap(ch.drop(z_msg), z=2)
        x_own, x_far, x_msg, ride = ch.run(
            fold_second(stride, ch.drop(xa), xa_got, ch.drop(xb), xb_got, ch.drop(ride))
        )
        x_got = moves.swap(ch.drop(x_msg), z=1)
        x_own, x_msg, ride = ch.run(
            fold_third(stride, ch.drop(x_own), ch.drop(x_far), x_got, ch.drop(ride))
        )
        grad_w_z, grad_w_out = ch.drop(*ch.run(fold_two(ch.drop(z_own), z_got)))
        x_got = moves.swap(ch.drop(x_msg), z=2)
        grad_w_x, g_conv_x, g_gate, g_heads, g_dt, mine = ch.drop(
            *ch.run(fold_last(moves.place, slab, ch.drop(x_own), x_got, ch.drop(ride)))
        )
        theirs = moves.swap(mine, c=1)
        grad_w_bc, grad_conv_bc, gain_sums, loss_sum = ch.drop(
            *ch.run(finish(moves.place, mine, theirs, slab, bcw))
        )
        grad_gain_in = gain_sums[0]
        loss = loss_sum[0, 0] / (count_total * width)
        g_bias, g_log, g_skip = [
            g_heads[0, at : at + own_heads] for at in (0, HEADS_PAD, 2 * HEADS_PAD)
        ]
        g_gain_gate = g_gate[0]
    else:

        def in_order(values):
            half = values.shape[-1] // 2
            turn = jnp.concatenate([values[..., half:], values[..., :half]], axis=-1)
            return jnp.where(moves.row == 0, values, turn)

        small = [
            in_order(dcx.value.reshape(4, 8, chans).sum(axis=1)),
            in_order(dgate.value.sum(axis=0)),
            in_order(dhead.value[0:8, 0:heads].sum(axis=0)),
            in_order(dhead.value[8:16, 0:heads].sum(axis=0)),
            in_order(dskip.value.sum(axis=0).reshape(heads, HP).sum(axis=1)),
            in_order(grad_dt.T),
        ]
        shared = [
            dcbc.value.reshape(4, 8, bcw).sum(axis=1), loss_part.value.sum(), gain_sum / gain_in,
        ]
        big = jnp.stack([grad_z, grad_o, grad_x])
        big = big[:, :, :cols] + moves.swap(big[:, :, cols:], y=1)
        big = lax.psum_scatter(big, "dp", scatter_dimension=1, tiled=True)
        grad_w_z, grad_w_out, grad_w_x = big[0], big[1], big[2]
        grad_w_bc = lax.psum_scatter(
            lax.psum(grad_bc, "tensor"), "dp", scatter_dimension=0, tiled=True
        )
        sums = lax.psum(jnp.concatenate([v.reshape(-1) for v in small + shared]), "dp")
        sums = sums + moves.swap(sums, y=1)
        done = []
        at = 0
        for value in small:
            part = sums[at : at + value.size].reshape(value.shape)
            half = value.shape[-1] // 2
            done.append(
                lax.dynamic_slice_in_dim(part, moves.row * half, half, value.ndim - 1)
            )
            at += value.size
        g_conv_x, g_gain_gate, g_bias, g_log, g_skip, g_dt = done
        g_dt = lax.dynamic_slice_in_dim(g_dt, moves.dp * slab, slab, 0)
        tail = sums[at:]
        tail = tail + moves.swap(tail, c=1)
        n_conv = 4 * bcw
        grad_conv_bc = tail[:n_conv].reshape(4, bcw)
        loss = tail[n_conv] / (count_total * width)
        grad_gain_in = tail[n_conv + 1 :]
    return (
        mixed[None], loss, grad_residual[None], grad_gain_in, grad_w_z, grad_w_x, grad_w_bc, g_dt,
        g_conv_x, grad_conv_bc, g_bias, g_log, g_skip, g_gain_gate, grad_w_out,
    )


def solution(mesh):
    both = P("dp", "tensor")
    tokens = P("dp", "tensor", None)
    return jax.shard_map(
        body,
        mesh=mesh,
        in_specs=(
            tokens, tokens, both, P(), both, both, P("dp", None), both, P(None, "tensor"), P(),
            P("tensor"), P("tensor"), P("tensor"), P("tensor"), both,
        ),
        out_specs=(
            tokens, P(), tokens, P(), both, both, P("dp", None), both, P(None, "tensor"), P(),
            P("tensor"), P("tensor"), P("tensor"), P("tensor"), both,
        ),
        check_vma=False,
    )
```

```python
import functools

import jax
import jax.numpy as jnp
from jax import lax
from jax.experimental import pallas as pl
from jax.experimental.pallas import tpu as pltpu
from jax.sharding import PartitionSpec as P

HP = 64
BLOCK = 256
EPSILON = 1e-05
HEADS_PAD = 128
HALO = 16
BF = jnp.bfloat16
F32 = jnp.float32
HIGH = lax.Precision.HIGHEST
VMEM_LIMIT = 10 * 1024 * 1024
AXES = ("dp", "tensor")
FRONT_SPLIT = 1


def dot_nn(left, right):
    return lax.dot_general(left, right, (((1,), (0,)), ((), ())), preferred_element_type=F32)


def dot_nt(left, right):
    return lax.dot_general(left, right, (((1,), (1,)), ((), ())), preferred_element_type=F32)


def dot_tn(left, right):
    return lax.dot_general(left, right, (((0,), (0,)), ((), ())), preferred_element_type=F32)


def split_low(values):
    high = values.astype(BF)
    return high, (values - high.astype(F32)).astype(BF)


def dot_split(dot, left, right):
    high, rest = split_low(left)
    return dot(high, right) + dot(rest, right)


def by_expansion(values, spread_mat):
    rest = values - values.astype(BF).astype(F32)
    lane = lax.broadcasted_iota(jnp.int32, values.shape, 1)
    both = jnp.where(lane < HEADS_PAD // 2, values, pltpu.roll(rest, HEADS_PAD // 2, 1))
    return dot_nn(both.astype(BF), spread_mat)


def per_head(values, sum_mat):
    high, rest = split_low(values)
    return dot_nn(high, sum_mat) + dot_nn(rest, sum_mat)


def sigmoid(values):
    return jax.nn.sigmoid(values)


def call(
    kernel, grid, in_specs, out_specs, out_shape, scratch=(), prefetch=0, flops=0, nbytes=0,
    in_place=(), far_off=(), free=(), vmem=VMEM_LIMIT,
):
    n_in, n_out = len(in_specs), len(out_specs)

    def with_operands(*operands, keep=()):
        scalars, arrays = operands[:prefetch], list(operands[prefetch:])
        extra = [v for v in keep if not any(v is w for w in arrays)]
        n_extra, n_keep = len(extra), len(keep)
        every = arrays + extra
        aliases = {prefetch + i: o for i, o in in_place}
        for o, value in enumerate(keep):
            i = [k for k, w in enumerate(every) if w is value][0]
            aliases[prefetch + i] = n_out + o

        def wrapped(*refs):
            first = prefetch + n_in
            second = first + n_extra
            kernel(*refs[:first], *refs[second : second + n_out], *refs[second + n_out + n_keep :])

        anywhere = pl.BlockSpec(memory_space=pl.ANY)
        results = pl.pallas_call(
            wrapped,
            grid_spec=pltpu.PrefetchScalarGridSpec(
                num_scalar_prefetch=prefetch,
                grid=grid,
                in_specs=list(in_specs) + [anywhere] * n_extra,
                out_specs=list(out_specs) + [anywhere] * n_keep,
                scratch_shapes=list(scratch),
            ),
            out_shape=list(out_shape) + [out(v.shape, v.dtype) for v in keep],
            input_output_aliases=aliases,
            compiler_params=pltpu.CompilerParams(
                dimension_semantics=("arbitrary",) * len(grid), vmem_limit_bytes=vmem
            ),
            cost_estimate=pl.CostEstimate(flops=1, bytes_accessed=1, transcendentals=0),
        )(*scalars, *[
                v if i in free else in_hbm(v) if i in far_off else near_core(v)
                for i, v in enumerate(every)
            ])
        return results[:n_out], results[n_out:]

    return with_operands


class Held:
    def __init__(self, value):
        self.value = value


class Chain:
    def __init__(self):
        self.live = []

    def hold(self, *values):
        held = [Held(value) for value in values]
        self.live += held
        return held if len(held) > 1 else held[0]

    def drop(self, *held):
        self.live = [h for h in self.live if not any(h is d for d in held)]
        values = [h.value for h in held]
        return values if len(values) > 1 else values[0]

    def run(self, prepared):
        runner, operands = prepared
        results, kept = runner(*operands, keep=[h.value for h in self.live])
        for held, value in zip(self.live, kept):
            held.value = value
        return self.hold(*results)


def now(*held):
    return [h.value for h in held]


def whole(shape):
    del shape
    return pl.BlockSpec(memory_space=pltpu.VMEM)


def rows(block, width):
    return pl.BlockSpec((block, width), lambda i, *_: (i, 0))


def out(shape, dtype):
    return pltpu.VMEM(shape, dtype)


def in_hbm(values):
    return pltpu.with_memory_space_constraint(values, pltpu.HBM)


def near_core(values):
    return pltpu.with_memory_space_constraint(values, pltpu.VMEM)


def front_kernel(
    n_ref, halo_ref, wx_ref, wbc_ref, wdt_ref, cx_ref, cbc_ref, bias_ref, rate_ref, spread_ref,
    *refs, first,
):
    if first > 0:
        xtail_in, btail_in, before_in, state_in = refs[:4]
        refs = refs[4 + 8 :]
    (
        xc_ref, bcc_ref, dt_ref, a_ref, ahead_ref, at_ref, y_ref, saved_ref, xin_ref, bcin_ref,
        sx_ref, sbc_ref, xtail_ref, btail_ref, before, state, end_ref, xh_ref, bh_ref, xs, bs, xt,
    ) = refs
    step = pl.program_id(0)
    block = n_ref.shape[0]
    chans = wx_ref.shape[1]
    bcw = wbc_ref.shape[1]
    n_state = bcw // 2
    half = block // 2

    @pl.when(step == 0)
    def _():
        if first == 0:
            halo_x = dot_nn(halo_ref[...], wx_ref[...])
            halo_bc = dot_nn(halo_ref[...], wbc_ref[...])
            for j in range(chans // 128):
                xs[j, 0:8, :] = halo_x[8:16, j * 128 : j * 128 + 128]
            for j in range(bcw // 128):
                bs[j, 0:8, :] = halo_bc[8:16, j * 128 : j * 128 + 128]
            xh_ref[...] = halo_x.astype(BF)
            bh_ref[...] = halo_bc.astype(BF)
            before[...] = jnp.zeros_like(before)
            state[...] = jnp.zeros_like(state)
        else:
            xs[:, 0:8, :] = xtail_in[...]
            bs[:, 0:8, :] = btail_in[...]
            before[...] = before_in[...]
            state[...] = state_in[...]
            xh_ref[...] = jnp.zeros_like(xh_ref)
            bh_ref[...] = jnp.zeros_like(bh_ref)

    @pl.when(step > 0)
    def _():
        for j in range(chans // 128):
            xs[j, 0:8, :] = xs[j, block : block + 8, :]
        for j in range(bcw // 128):
            bs[j, 0:8, :] = bs[j, block : block + 8, :]

    n_now = n_ref[...]

    def convolve(held, j, taps):
        cols = slice(j * 128, j * 128 + 128)
        pre = held[j, 5 : block + 5, :] * taps[0:1, cols]
        for k in range(1, 4):
            pre += held[j, 5 + k : block + 5 + k, :] * taps[k : k + 1, cols]
        sig = sigmoid(pre)
        return (pre * sig).astype(BF), sig * (1.0 + pre * (1.0 - sig))

    bc_now = dot_nn(n_now, wbc_ref[...])
    bcin_ref[...] = bc_now
    for j in range(bcw // 128):
        bs[j, 8 : block + 8, :] = bc_now[:, j * 128 : j * 128 + 128]
        cols = slice(j * 128, j * 128 + 128)
        bcc_ref[:, cols], sbc_ref[:, cols] = convolve(bs, j, cbc_ref)
    dt_raw = dot_nt(wdt_ref[...], n_now) + bias_ref[...]
    tail = jnp.exp(-jnp.abs(dt_raw))
    log_part = jnp.where(
        tail < 0.01, tail * (1.0 - tail * (0.5 - tail * (1.0 / 3.0))), jnp.log(1.0 + tail)
    )
    dt_t = jnp.maximum(dt_raw, 0.0) + log_part
    row_i = lax.broadcasted_iota(jnp.int32, (block, block), 0)
    col_i = lax.broadcasted_iota(jnp.int32, (block, block), 1)
    upto = jnp.where(row_i <= col_i, 1.0, 0.0).astype(F32)
    a_t = jnp.dot(dt_t * rate_ref[...], upto, precision=HIGH, preferred_element_type=F32)
    at_ref[...] = a_t[0 : at_ref.shape[0]]
    a_now = a_t.T
    dt_now = dt_t.T
    a_ref[...] = a_now
    dt_ref[...] = dt_now
    ahead_ref[...] = before[...]
    a_last = a_now[block - 1 : block]
    before[...] = before[...] + a_last
    for part in range(0, chans, 256):
        x_now = dot_nn(n_now, wx_ref[:, part : part + 256])
        xin_ref[:, part : part + 256] = x_now.astype(BF)
        for j in (part // 128, part // 128 + 1):
            at = j * 128 - part
            xs[j, 8 : block + 8, :] = x_now[:, at : at + 128]
            cols = slice(j * 128, j * 128 + 128)
            xc_ref[:, cols], slope = convolve(xs, j, cx_ref)
            sx_ref[:, cols] = slope.astype(BF)

    spread = spread_ref[...]
    b_now = bcc_ref[:, 0:n_state]
    c_now = bcc_ref[:, n_state:]
    state_low = state[...].astype(BF)
    saved_ref[0] = state_low
    xt[...] = (xc_ref[...].astype(F32) * by_expansion(dt_now, spread)).astype(BF)
    y_ref[...] = dot_nn(c_now, state_low) * by_expansion(jnp.exp(a_now), spread)
    scores = dot_nt(c_now, b_now)
    row_i = lax.broadcasted_iota(jnp.int32, (half, half), 0)
    col_i = lax.broadcasted_iota(jnp.int32, (half, half), 1)
    shut = jnp.where(row_i >= col_i, 0.0, -1e30).astype(F32)
    lane = lax.broadcasted_iota(jnp.int32, (half, 128), 1)
    for pair in range(chans // 128):
        cols = slice(pair * 128, pair * 128 + 128)
        x_pair = xt[:, cols]
        tops, lows = [], []
        for sub in range(2):
            h = pair * 2 + sub
            a_row = a_t[h : h + 1, :]
            a_top = a_now[0:half, h : h + 1]
            a_low = a_now[half:block, h : h + 1]
            m_top = jnp.exp(a_top - a_row[:, 0:half] + shut) * scores[0:half, 0:half]
            m_left = jnp.exp(a_low - a_row[:, 0:half]) * scores[half:block, 0:half]
            m_low = jnp.exp(a_low - a_row[:, half:block] + shut) * scores[half:block, half:block]
            tops.append(dot_nn(m_top.astype(BF), x_pair[0:half]))
            lows.append(
                dot_nn(jnp.concatenate([m_left.astype(BF), m_low.astype(BF)], axis=1), x_pair)
            )
        y_ref[0:half, cols] += jnp.where(lane < HP, tops[0], tops[1])
        y_ref[half:block, cols] += jnp.where(lane < HP, lows[0], lows[1])
    tail_w = by_expansion(jnp.exp(a_last - a_now), spread)
    decay = by_expansion(jnp.broadcast_to(jnp.exp(a_last), (8, HEADS_PAD)), spread)
    state[...] = state[...] * decay[0:1] + dot_tn(
        b_now, (xt[...].astype(F32) * tail_w).astype(BF)
    )
    end_ref[...] = state[...].astype(BF)
    xtail_ref[...] = xs[:, block : block + 8, :]
    btail_ref[...] = bs[:, block : block + 8, :]


def front(first, count, n_full, halo, wx, wbc, wdt, conv_x, conv_bc, bias, rate, spread, carried):
    toks, width = n_full.shape
    chans = wx.shape[1]
    bcw = wbc.shape[1]
    n_state = bcw // 2
    heads = chans // HP
    nb = toks // BLOCK
    n_x, n_b = chans // 128, bcw // 128

    def at(w):
        return pl.BlockSpec((BLOCK, w), lambda i: (first + i, 0))

    def part(w, dtype):
        shape = pltpu.HBM((count * BLOCK, w), dtype)
        return pl.BlockSpec((BLOCK, w), lambda i: (i, 0)), shape

    parts = [part(chans, BF), part(bcw, F32), part(chans, BF), part(bcw, F32)]
    wide = [
        (at(chans), out((toks, chans), BF)), (at(bcw), out((toks, bcw), BF)),
        (at(HEADS_PAD), out((toks, HEADS_PAD), F32)), (at(HEADS_PAD), out((toks, HEADS_PAD), F32)),
        (pl.BlockSpec((8, HEADS_PAD), lambda i: (first + i, 0)), out((8 * nb, HEADS_PAD), F32)),
        (pl.BlockSpec((heads, BLOCK), lambda i: (0, first + i)), out((heads, toks), F32)),
        (at(chans), out((toks, chans), F32)),
        (
            pl.BlockSpec((1, n_state, chans), lambda i: (first + i, 0, 0)),
            out((nb, n_state, chans), BF),
        ),
    ]
    passed = [
        out((n_x, 8, 128), F32), out((n_b, 8, 128), F32), out((8, HEADS_PAD), F32),
        out((n_state, chans), F32),
    ]
    last = [out((n_state, chans), BF), out((HALO, chans), BF), out((HALO, bcw), BF)]
    fixed = (halo, wx, wbc, wdt, conv_x, conv_bc, bias, rate, spread)
    anywhere = pl.BlockSpec(memory_space=pl.ANY)
    runner = call(
        functools.partial(front_kernel, first=first),
        (count,),
        [at(width)]
        + [whole(v.shape) for v in fixed]
        + ([whole(v.shape) for v in passed] + [anywhere] * len(wide) if first else []),
        [spec for spec, _ in wide + parts] + [whole(v.shape) for v in passed + last],
        [shape for _, shape in wide + parts] + passed + last,
        [
            pltpu.VMEM((n_x, BLOCK + 8, 128), F32), pltpu.VMEM((n_b, BLOCK + 8, 128), F32),
            pltpu.VMEM((BLOCK, chans), BF),
        ],
        in_place=[(10 + 4 + k, k) for k in range(len(wide))] if first else [],
        flops=2 * count * BLOCK * (width * (chans + bcw) + 2 * BLOCK * chans),
        nbytes=20 * count * BLOCK * chans,
    )
    return runner, (n_full, *fixed, *carried)


def gate_kernel(
    where_ref, n_ref, y_ref, xc_ref, c_ref, a_ref, ahead_ref, start_ref, wz_ref, wo_ref, skip_ref,
    gain_ref, spread_ref, *refs,
):
    gate_out, part_ref, sq_ref, u_ref = refs[-4:]
    chans = y_ref.shape[1]
    n_now = n_ref[...]
    squares = jnp.zeros((n_now.shape[0], 128), F32)
    passed = jnp.exp(a_ref[...] + ahead_ref[0:1])
    c_now = c_ref[...]
    for col in range(0, chans, 256):
        cols = slice(col, col + 256)
        gate = dot_nn(n_now, wz_ref[:, cols])
        y_now = y_ref[:, cols] + dot_nn(c_now, start_ref[:, turned(cols, chans)]) * by_expansion(
            passed, spread_ref[:, cols]
        )
        gated = (y_now + skip_ref[:, cols] * xc_ref[:, cols].astype(F32)) * (
            gate * sigmoid(gate)
        )
        gate_out[:, cols] = gate
        u_ref[:, cols] = (gated * gain_ref[:, cols]).astype(BF)
        sq = gated * gated
        squares += sq[:, 0:128] + sq[:, 128:256]
    sq_ref[...] = jnp.broadcast_to(jnp.sum(squares, axis=1, keepdims=True), squares.shape)
    part_ref[...] = dot_nt(u_ref[...], wo_ref[...]).astype(part_ref.dtype)


def turned(cols, chans):
    start = (cols.start + chans // 2) % chans
    return slice(start, start + cols.stop - cols.start)


def gate_out_proj(
    far, place, n_full, y, xc, bcc, a_cols, ahead, start, wz, wo, skip_row, gain_row, spread,
    in_place=(),
):
    toks, width = n_full.shape
    chans = wz.shape[1]
    half = toks // 2 // BLOCK

    def spot(i, where):
        core = 1 - where[3] if far else where[3]
        return core * half + i

    def moved(w):
        return pl.BlockSpec((BLOCK, w), lambda i, where: (spot(i, where), 0))

    plain = pl.BlockSpec((BLOCK, width), lambda i, where: (i, 0))
    anywhere = pl.BlockSpec(memory_space=pl.ANY)
    runner = call(
        gate_kernel,
        (half,),
        [
            moved(width), moved(chans), moved(chans),
            pl.BlockSpec((BLOCK, start.shape[0]), lambda i, where: (spot(i, where), 1)),
            moved(HEADS_PAD),
            pl.BlockSpec((8, HEADS_PAD), lambda i, where: (spot(i, where), 0)),
            whole(start.shape), whole(wz.shape), whole(wo.shape),
            whole(skip_row.shape), whole(gain_row.shape), whole(spread.shape),
        ] + [anywhere] * len(in_place),
        [
            moved(chans), plain,
            pl.BlockSpec((BLOCK, 128), lambda i, where: (i, 0)),
        ],
        [
            out((toks, chans), F32), out((toks // 2, width), BF if far else F32),
            out((toks // 2, 128), F32),
        ],
        [pltpu.VMEM((BLOCK, chans), BF)],
        in_place=[(12 + k, k) for k in range(len(in_place))],
        prefetch=1, flops=2 * toks * width * chans, nbytes=7 * toks * chans,
    )
    return runner, (
        place, n_full, y, xc, bcc, a_cols, ahead, start, wz, wo, skip_row, gain_row, spread,
        *in_place,
    )


def loss_kernel(
    near_ref, got_ref, sq_ref, sqgot_ref, res_ref, teach_ref, valid_ref, count_ref, countgot_ref,
    mixed_ref, gres_ref, gs_ref, gsmsg_ref, q_ref, loss_ref, *, inner, tokens,
):
    @pl.when(pl.program_id(0) == 0)
    def _():
        loss_ref[...] = jnp.zeros_like(loss_ref)

    total = sq_ref[:, 0:1] + sqgot_ref[:, 0:1]
    factor = lax.rsqrt(total / inner + EPSILON)
    branch = near_ref[...] + got_ref[...].astype(F32)
    result = res_ref[...].astype(F32) + factor * branch
    mixed_ref[...] = result.astype(BF)
    error = result - teach_ref[...].astype(F32)
    valid = valid_ref[...]
    terms = jnp.sum((valid * error * error).reshape(-1, 8, error.shape[1]), axis=0)
    for col in range(0, error.shape[1], 128):
        loss_ref[...] += terms[:, col : col + 128]
    count = count_ref[0:1, 0:1] + countgot_ref[0:1, 0:1]
    grad = (valid * (tokens / count)) * error
    gres_ref[...] = grad
    gs = (grad * factor).astype(BF)
    gs_ref[...] = gs
    gsmsg_ref[...] = gs
    prods = jnp.sum(gs.astype(F32) * branch, axis=1, keepdims=True)
    q_ref[...] = jnp.broadcast_to(prods * factor * factor / inner, q_ref.shape)


def loss_step(
    near, got, sq, sqgot, residual, teacher, valid_col, count, count_got, inner, tokens
):
    toks, width = near.shape
    nb = toks // BLOCK
    runner = call(
        functools.partial(loss_kernel, inner=inner, tokens=tokens),
        (nb,),
        [
            rows(BLOCK, width), rows(BLOCK, width), rows(BLOCK, 128), rows(BLOCK, 128),
            rows(BLOCK, width), rows(BLOCK, width), rows(BLOCK, 1), whole(count.shape),
            whole(count_got.shape),
        ],
        [
            rows(BLOCK, width), rows(BLOCK, width), rows(BLOCK, width), rows(BLOCK, width),
            rows(BLOCK, 128), whole((8, 128)),
        ],
        [
            jax.ShapeDtypeStruct((toks, width), BF), pltpu.HBM((toks, width), F32),
            out((toks, width), BF), out((toks, width), BF), out((toks, 128), F32),
            out((8, 128), F32),
        ],
        nbytes=20 * toks * width, free=(4, 5),
    )
    return runner, (near, got, sq, sqgot, residual, teacher, valid_col, count, count_got)


def gate_back_kernel(
    where_ref, gs_ref, q_ref, wo_ref, y_ref, xc_ref, gate_ref, a_ref, ahead_ref, c_ref, start_ref,
    skip_ref, gain_ref, spread_ref, sum_ref, *refs, second,
):
    (
        dz_ref, dy_ref, rowdot_ref, u_ref, dstart_ref, dgain_ref, dskip_ref, dlow_ref, dyf,
    ) = refs[-9:]

    @pl.when(pl.program_id(0) == 0)
    def _():
        for place, ref in enumerate((dstart_ref, dgain_ref, dskip_ref)):
            ref[...] = refs[place][...] if second else jnp.zeros_like(ref)

    chans = y_ref.shape[1]
    q_now = q_ref[:, 0:1]
    gs = gs_ref[...]
    passed = jnp.exp(a_ref[...] + ahead_ref[0:1])
    c_now = c_ref[...]
    for col in range(0, chans, 256):
        cols = slice(col, col + 256)
        grad = dot_nn(gs, wo_ref[:, cols])
        gate = gate_ref[:, cols].astype(F32)
        sig = sigmoid(gate)
        silu = gate * sig
        x_now = xc_ref[:, cols].astype(F32)
        wide = by_expansion(passed, spread_ref[:, cols])
        y_now = y_ref[:, cols] + dot_nn(c_now, start_ref[:, turned(cols, chans)]) * wide
        mixed = y_now + skip_ref[:, cols] * x_now
        gated = mixed * silu
        dgain_ref[:, cols] += jnp.sum((grad * gated).reshape(-1, 8, 256), axis=0)
        u_ref[:, cols] = (gated * gain_ref[:, cols]).astype(BF)
        dgated = grad * gain_ref[:, cols] - gated * q_now
        dz_ref[:, cols] = (dgated * mixed * (sig * (1.0 + gate * (1.0 - sig)))).astype(BF)
        dy = (dgated * silu).astype(BF)
        dy_ref[:, cols] = dy
        dy32 = dy.astype(F32)
        dskip_ref[:, cols] += jnp.sum((dy32 * x_now).reshape(-1, 8, 256), axis=0)
        dyf[:, cols] = dy32 * y_now
        dstart_ref[:, cols] += dot_tn(c_now, (dy32 * wide).astype(BF))
    rowdot_ref[...] = per_head(dyf[...], sum_ref[...])
    dlow_ref[...] = dstart_ref[...].astype(BF)


def gate_backward(
    place, gs, q, wo, y, xc, gate, a_cols, ahead, bcc, start, skip_row, gain_row, spread, sum_mat,
    sums=(), in_place=(),
):
    toks, width = y.shape[0], gs.shape[1]
    chans = wo.shape[1]
    n_state = bcc.shape[1] // 2
    half = toks // 2 // BLOCK
    second = len(sums) > 0

    def spot(i, where):
        return (1 - where[3] if second else where[3]) * half + i

    def moved(w):
        return pl.BlockSpec((BLOCK, w), lambda i, where: (spot(i, where), 0))

    def plain(w):
        return pl.BlockSpec((BLOCK, w), lambda i, where: (i, 0))

    anywhere = pl.BlockSpec(memory_space=pl.ANY)
    runner = call(
        functools.partial(gate_back_kernel, second=second),
        (half,),
        [
            plain(width), plain(128), whole(wo.shape), moved(chans), moved(chans), moved(chans),
            moved(HEADS_PAD), pl.BlockSpec((8, HEADS_PAD), lambda i, where: (spot(i, where), 0)),
            pl.BlockSpec((BLOCK, n_state), lambda i, where: (spot(i, where), 1)),
            whole(start.shape), whole(skip_row.shape), whole(gain_row.shape),
            whole(spread.shape), whole(sum_mat.shape),
        ]
        + [whole(v.shape) for v in sums]
        + [anywhere] * len(in_place),
        [
            moved(chans), moved(chans), moved(HEADS_PAD), moved(chans), whole((n_state, chans)),
            whole((8, chans)), whole((8, chans)), whole((n_state, chans)),
        ],
        [
            out((toks, chans), BF), out((toks, chans), BF), out((toks, HEADS_PAD), F32),
            out((toks, chans), BF), out((n_state, chans), F32), out((8, chans), F32),
            out((8, chans), F32), out((n_state, chans), BF),
        ],
        [pltpu.VMEM((BLOCK, chans), F32)],
        in_place=[(14 + len(sums) + k, k) for k in range(len(in_place))],
        prefetch=1, flops=toks * width * chans, nbytes=7 * toks * chans,
    )
    return runner, (
        place, gs, q, wo, y, xc, gate, a_cols, ahead, bcc, start, skip_row, gain_row, spread,
        sum_mat, *sums, *in_place,
    )


def scan_back_kernel(
    xc_ref, bcc_ref, dt_ref, a_ref, ahead_ref, at_ref, dy_ref, rowdot_ref, saved_ref, xin_ref,
    bcin_ref, sx_ref, sbc_ref, xh_ref, bh_ref, start_ref, cx_ref, cbc_ref, skip_ref,
    rate_ref, spread_ref, sum_ref, wx_ref, wbc_ref, dend_ref, *refs, top, final, n_carried,
):
    carried = refs[:n_carried]
    (
        dxin_ref, dbc_ref, ddt_ref, dxh_ref, dbch_ref, hgrad_ref, dcx_ref, dcbc_ref, dhead_ref, dstate,
        dxc_out, dbc_out, xt, dxt, dxp, dbp, dbco,
    ) = refs[-17:]
    step = pl.program_id(0)
    block, chans = xc_ref.shape
    bcw = bcc_ref.shape[1]
    n_state = bcw // 2
    half = block // 2
    n_x = chans // 128
    n_b = bcw // 128

    @pl.when(step == 0)
    def _():
        if n_carried == 0:
            dstate[:, 0 : chans // 2] = dend_ref[:, chans // 2 :].astype(F32)
            dstate[:, chans // 2 :] = dend_ref[:, 0 : chans // 2].astype(F32)
            for ref in (dcx_ref, dcbc_ref, dhead_ref):
                ref[...] = jnp.zeros_like(ref)
            dxp[:, block : block + 8, :] = jnp.zeros((n_x, 8, 128), F32)
            dbp[:, block : block + 8, :] = jnp.zeros((n_b, 8, 128), F32)
        else:
            for ref, given in zip((dcx_ref, dcbc_ref, dhead_ref, dstate), carried):
                ref[...] = given[...]
            for j in range(n_x):
                dxp[j, block : block + 8, :] = carried[4][:, j * 128 : j * 128 + 128]
            for j in range(n_b):
                dbp[j, block : block + 8, :] = carried[5][:, j * 128 : j * 128 + 128]

    @pl.when(step > 0)
    def _():
        for j in range(n_x):
            dxp[j, block : block + 8, :] = dxp[j, 0:8, :]
        for j in range(n_b):
            dbp[j, block : block + 8, :] = dbp[j, 0:8, :]

    spread = spread_ref[...]
    sum_mat = sum_ref[...]
    b_now = bcc_ref[:, 0:n_state]
    c_now = bcc_ref[:, n_state:]
    a_now = a_ref[...]
    dt_now = dt_ref[...]
    a_last = a_now[block - 1 : block]
    dt_wide = by_expansion(dt_now, spread)
    xt[...] = (xc_ref[...].astype(F32) * dt_wide).astype(BF)
    tail = by_expansion(jnp.exp(a_last - a_now), spread)
    dstate_low = dstate[...].astype(BF)
    dxt[...] = dot_nn(b_now, dstate_low) * tail
    scores = dot_nt(b_now, c_now)
    row_i = lax.broadcasted_iota(jnp.int32, (half, half), 0)
    col_i = lax.broadcasted_iota(jnp.int32, (half, half), 1)
    shut = jnp.where(row_i <= col_i, 0.0, -1e30).astype(F32)
    lane = lax.broadcasted_iota(jnp.int32, (half, 128), 1)
    lane_full = lax.broadcasted_iota(jnp.int32, (block, 128), 1)
    g_top = jnp.zeros((half, block), F32)
    g_low = jnp.zeros((half, half), F32)
    for pair in range(n_x):
        cols = slice(pair * 128, pair * 128 + 128)
        x_pair = xt[:, cols]
        dy_pair = dy_ref[:, cols]
        none = jnp.zeros_like(x_pair)
        x_mine = [jnp.where(lane_full < HP, x_pair, none), jnp.where(lane_full < HP, none, x_pair)]
        w_uppers, w_lows, m_uppers, m_lows = [], [], [], []
        for sub in range(2):
            h = pair * 2 + sub
            a_row = at_ref[h : h + 1, :]
            a_top = a_now[0:half, h : h + 1]
            a_low = a_now[half:block, h : h + 1]
            w_top = jnp.exp(a_row[:, 0:half] - a_top + shut)
            w_right = jnp.exp(a_row[:, half:block] - a_top)
            w_low = jnp.exp(a_row[:, half:block] - a_low + shut)
            w_upper = jnp.concatenate([w_top, w_right], axis=1)
            w_uppers.append(w_upper)
            w_lows.append(w_low)
            m_uppers.append((w_upper * scores[0:half]).astype(BF))
            m_lows.append((w_low * scores[half:block, half:block]).astype(BF))
        tops = dot_nn(jnp.concatenate(m_uppers, axis=0), dy_pair)
        lows = dot_nn(jnp.concatenate(m_lows, axis=0), dy_pair[half:block])
        x_tops = jnp.concatenate([x_mine[0][0:half], x_mine[1][0:half]], axis=0)
        x_lows = jnp.concatenate([x_mine[0][half:block], x_mine[1][half:block]], axis=0)
        d_uppers = dot_nt(x_tops, dy_pair)
        d_lows = dot_nt(x_lows, dy_pair[half:block])
        g_top += w_uppers[0] * d_uppers[0:half] + w_uppers[1] * d_uppers[half:block]
        g_low += w_lows[0] * d_lows[0:half] + w_lows[1] * d_lows[half:block]
        dxt[0:half, cols] += jnp.where(lane < HP, tops[0:half], tops[half:block])
        dxt[half:block, cols] += jnp.where(lane < HP, lows[0:half], lows[half:block])
    came = by_expansion(jnp.exp(ahead_ref[...]), spread)
    start = jnp.concatenate(
        [start_ref[:, chans // 2 :], start_ref[:, 0 : chans // 2]], axis=1
    ).astype(F32)
    first_state = saved_ref[0].astype(F32) + start * came[0:1]
    dy_wide = (dy_ref[...].astype(F32) * by_expansion(jnp.exp(a_now), spread)).astype(BF)
    x_tail = (xt[...].astype(F32) * tail).astype(BF)
    d_b = dot_nt(x_tail, dstate_low)
    d_c = dot_nt(dy_wide, first_state.astype(BF))
    decay = by_expansion(jnp.broadcast_to(jnp.exp(a_last), (8, HEADS_PAD)), spread)
    last_state = first_state * decay[0:1] + dot_tn(b_now, x_tail)
    dbco[0:half, 0:n_state] = d_b[0:half] + dot_split(dot_nn, g_top, c_now)
    dbco[half:block, 0:n_state] = d_b[half:block] + dot_split(dot_nn, g_low, c_now[half:block])
    d_c_top = dot_split(dot_tn, g_top, b_now[0:half])
    dbco[0:half, n_state:] = d_c[0:half] + d_c_top[0:half]
    dbco[half:block, n_state:] = (
        d_c[half:block] + d_c_top[half:block] + dot_split(dot_tn, g_low, b_now[half:block])
    )
    coldot = per_head(dxt[...] * xt[...].astype(F32), sum_mat)
    direct = dot_nn((dxt[...] * xc_ref[...].astype(F32)).astype(BF), sum_mat)
    ends = jnp.sum(dstate[...] * last_state, axis=0, keepdims=True)
    ends = per_head(jnp.broadcast_to(ends, (8, chans)), sum_mat)
    row_k = lax.broadcasted_iota(jnp.int32, (block, HEADS_PAD), 0)
    d_a = rowdot_ref[...] - coldot + jnp.where(row_k == block - 1, ends[0:1], 0.0)
    row_b = lax.broadcasted_iota(jnp.int32, (block, block), 0)
    col_b = lax.broadcasted_iota(jnp.int32, (block, block), 1)
    onward = jnp.where(row_b <= col_b, 1.0, 0.0).astype(F32)
    d_step = jnp.dot(onward, d_a, precision=HIGH, preferred_element_type=F32)
    rate = rate_ref[0:1, :]
    slope = jnp.where(
        dt_now < 0.01, dt_now * (1.0 - dt_now * (0.5 - dt_now * (1.0 / 6.0))), 1.0 - jnp.exp(-dt_now)
    )
    d_raw = (direct + rate * d_step) * slope
    ddt_ref[...] = d_raw.astype(BF)
    dhead_ref[0:8, :] += jnp.sum(d_raw.reshape(-1, 8, HEADS_PAD), axis=0)
    dhead_ref[8:16, :] += jnp.sum((dt_now * d_step * rate).reshape(-1, 8, HEADS_PAD), axis=0)
    dstate[...] = dstate[...] * decay[0:1] + dot_tn(c_now, dy_wide)
    def conv_back(here, slope, grad_of, passed_on, taps, sums, dest, j):
        cols = slice(j * 128, j * 128 + 128)
        dpre = grad_of(cols) * slope[:, cols].astype(F32)
        passed_on[j, 0:block, :] = dpre
        x_now = here[:, cols].astype(F32)
        back = jnp.zeros_like(dpre)
        for k in range(4):
            later = dpre if k == 3 else passed_on[j, 3 - k : 3 - k + block, :]
            sums[8 * k : 8 * k + 8, cols] += jnp.sum((later * x_now).reshape(-1, 8, 128), axis=0)
            back += later * taps[k : k + 1, cols]
        dest[:, cols] = back.astype(dest.dtype)

    for j in range(n_b):
        conv_back(
            bcin_ref, sbc_ref, lambda cols: dbco[:, cols], dbp, cbc_ref, dcbc_ref, dbc_ref, j
        )
    for j in range(n_x):
        conv_back(
            xin_ref, sx_ref,
            lambda cols: dxt[:, cols] * dt_wide[:, cols]
            + skip_ref[:, cols] * dy_ref[:, cols].astype(F32),
            dxp, cx_ref, dcx_ref, dxin_ref, j,
        )

    @pl.when(step == pl.num_programs(0) - 1)
    def _():
        row_h = lax.broadcasted_iota(jnp.int32, (HALO, 1), 0)
        for src, taps, dest, edge, given, sums, count in (
            (dxp, cx_ref, dxh_ref, dxc_out, xh_ref, dcx_ref, n_x),
            (dbp, cbc_ref, dbch_ref, dbc_out, bh_ref, dcbc_ref, n_b),
        ):
            for j in range(count):
                cols = slice(j * 128, j * 128 + 128)
                head = src[j, 0:8, :]
                edge[:, cols] = head
                if not final:
                    continue
                acc = jnp.zeros((HALO, 128), F32)
                ahead = given[:, cols].astype(F32)
                for t in range(3):
                    for k in range(t + 1):
                        sums[8 * k : 8 * k + 1, cols] += (
                            ahead[HALO - 3 + t : HALO - 2 + t] * head[t - k : t - k + 1]
                        )
                    total = taps[0:1, cols] * head[t : t + 1]
                    for k in range(1, t + 1):
                        total = total + taps[k : k + 1, cols] * head[t - k : t - k + 1]
                    acc = acc + jnp.where(row_h == HALO - 3 + t, total, 0.0)
                dest[:, cols] = acc.astype(BF)
            if not final:
                dest[...] = jnp.zeros_like(dest)
        if final:
            hgrad_ref[...] = (
                dot_nt(dxh_ref[...], wx_ref[...]) + dot_nt(dbch_ref[...], wbc_ref[...])
            ).astype(BF)
        else:
            hgrad_ref[...] = jnp.zeros_like(hgrad_ref)


def scan_backward(
    top, count, base, xc, bcc, dt, a_cols, ahead, a_rows, dy, rowdot, saved, xin, bcin, slope_x,
    slope_bc,    xh, bh, start, conv_x, conv_bc, skip_row, rate_row, spread, sum_mat, wx, wbc, dend, carried=(),
    in_place=(),
):
    toks, chans = xc.shape
    bcw = bcc.shape[1]
    n_state = bcw // 2
    heads = chans // HP

    def back(width):
        return pl.BlockSpec((BLOCK, width), lambda i: (top - i, 0))

    def part(width):
        return pl.BlockSpec((BLOCK, width), lambda i: (top - i - base, 0))

    fixed = (xh, bh, start, conv_x, conv_bc, skip_row, rate_row, spread, sum_mat, wx, wbc, dend)
    anywhere = pl.BlockSpec(memory_space=pl.ANY)
    runner = call(
        functools.partial(
            scan_back_kernel, top=top, final=top + 1 == count, n_carried=len(carried)
        ),
        (count,),
        [
            back(chans), back(bcw), back(HEADS_PAD), back(HEADS_PAD),
            pl.BlockSpec((8, HEADS_PAD), lambda i: (top - i, 0)),
            pl.BlockSpec((heads, BLOCK), lambda i: (0, top - i)),
            back(chans), back(HEADS_PAD),
            pl.BlockSpec((1, n_state, chans), lambda i: (top - i, 0, 0)),
            part(chans), part(bcw), part(chans), part(bcw),
        ]
        + [whole(v.shape) for v in fixed]
        + [whole(v.shape) for v in carried]
        + [anywhere] * len(in_place),
        [
            back(chans), back(bcw), back(HEADS_PAD), whole((HALO, chans)), whole((HALO, bcw)),
            whole((HALO, wx.shape[0])), whole((32, chans)), whole((32, bcw)), whole((16, HEADS_PAD)),
            whole((n_state, chans)), whole((8, chans)), whole((8, bcw)),
        ],
        [
            out((toks, chans), BF), out((toks, bcw), F32), out((toks, HEADS_PAD), BF),
            out((HALO, chans), BF), out((HALO, bcw), BF), out((HALO, wx.shape[0]), BF),
            out((32, chans), F32), out((32, bcw), F32), out((16, HEADS_PAD), F32),
            out((n_state, chans), F32),
            out((8, chans), F32), out((8, bcw), F32),
        ],
        [
            pltpu.VMEM((BLOCK, chans), BF), pltpu.VMEM((BLOCK, chans), F32),
            pltpu.VMEM((chans // 128, BLOCK + 8, 128), F32),
            pltpu.VMEM((bcw // 128, BLOCK + 8, 128), F32), pltpu.VMEM((BLOCK, bcw), F32),
        ],
        in_place=[(25 + len(carried) + k, k) for k in range(len(in_place))],
        far_off=(9, 10, 11, 12),
        flops=2 * count * BLOCK * BLOCK * chans * 12, nbytes=16 * count * BLOCK * chans,
        vmem=15 * 1024 * 1024,
    )
    return runner, (
        xc, bcc, dt, a_cols, ahead, a_rows, dy, rowdot, saved, xin, bcin, slope_x, slope_bc, *fixed,
        *carried, *in_place,
    )


def input_grad_kernel(
    where_ref, dz_ref, dx_ref, dbc_ref, ddt_ref, wz_ref, wx_ref, wbc_ref, wdt_ref, part_ref
):
    del where_ref
    part = dot_nt(dz_ref[...], wz_ref[...])
    part += dot_nt(dx_ref[...], wx_ref[...])
    part += dot_nt(dbc_ref[...].astype(BF), wbc_ref[...])
    part += dot_nn(ddt_ref[...], wdt_ref[...])
    part_ref[...] = part.astype(part_ref.dtype)


def input_grad(far, place, dz, dxin, dbc, ddt, wz, wx, wbc, wdt):
    toks, chans = dz.shape
    width = wz.shape[0]
    half = toks // 2 // BLOCK

    def moved(w):
        return pl.BlockSpec(
            (BLOCK, w),
            lambda i, where: ((1 - where[3] if far else where[3]) * half + i, 0),
        )

    runner = call(
        input_grad_kernel,
        (half,),
        [
            moved(chans), moved(chans), moved(dbc.shape[1]), moved(HEADS_PAD),
            whole(wz.shape), whole(wx.shape), whole(wbc.shape), whole(wdt.shape),
        ],
        [pl.BlockSpec((BLOCK, width), lambda i, where: (i, 0))],
        [out((toks // 2, width), BF if far else F32)],
        prefetch=1, flops=2 * toks * width * chans, nbytes=4 * toks * chans,
    )
    return runner, (place, dz, dxin, dbc, ddt, wz, wx, wbc, wdt)


def norm_back_kernel(
    where_ref, near_ref, got_ref, res_ref, gain_ref, edge_ref, gres_ref, grad_ref, total
):
    total[...] = near_ref[...] + got_ref[...].astype(F32)
    block, width = total.shape
    last = pl.program_id(0) == pl.num_programs(0) - 1

    @pl.when(jnp.logical_and(last, jnp.logical_and(where_ref[2] == 0, where_ref[3] == 1)))
    def _():
        half = width // 2
        for k in range(2):
            total[block - HALO :, k * half : (k + 1) * half] += edge_ref[
                k * HALO : (k + 1) * HALO, :
            ].astype(F32)

    upper = res_ref[...].astype(F32)
    factor = lax.rsqrt(jnp.mean(upper * upper, axis=-1, keepdims=True) + EPSILON)
    scaled = total[...] * gain_ref[...]
    hat = upper * factor
    inner = jnp.mean(scaled * hat, axis=-1, keepdims=True)
    grad_ref[...] = (gres_ref[...] + factor * (scaled - hat * inner)).astype(BF)


def norm_backward(place, near, got, residual, gain, edge, grad_result):
    toks, width = near.shape

    def plain(w):
        return pl.BlockSpec((BLOCK, w), lambda i, where: (i, 0))

    runner = call(
        norm_back_kernel,
        (toks // BLOCK,),
        [
            plain(width), plain(width), plain(width), whole(gain.shape), whole(edge.shape),
            plain(width),
        ],
        [plain(width)],
        [jax.ShapeDtypeStruct((toks, width), BF)],
        [pltpu.VMEM((BLOCK, width), F32)],
        prefetch=1, nbytes=12 * toks * width, free=(2, 5),
    )
    return runner, (place, near, got, residual, gain, edge, grad_result)


class Moves:
    def __init__(self, n_dp, n_tensor):
        self.n_dp = n_dp
        self.n_all = n_dp * n_tensor
        self.n_tensor = n_tensor
        dp = lax.axis_index("dp")
        tensor = lax.axis_index("tensor")
        self.dp = dp
        self.row = tensor // 2
        self.core = tensor % 2
        self.z = dp // 2
        self.x = dp % 2
        self.place = jnp.stack([self.z, self.x, self.row, self.core]).astype(jnp.int32)

    def swap(self, value, z=0, x=0, y=0, c=0):
        mask = (z * 2 + x) * self.n_tensor + y * 2 + c
        return lax.ppermute(value, AXES, [(i, i ^ mask) for i in range(self.n_all)])

    def up(self, value):
        pairs = [(i, i + 2) for i in range(self.n_all) if i % self.n_tensor < 2]
        return lax.ppermute(value, AXES, pairs)

    def down(self, value):
        pairs = [(i + 2, i) for i in range(self.n_all) if i % self.n_tensor < 2]
        return lax.ppermute(value, AXES, pairs)


def join_kernel(where_ref, mine_ref, theirs_ref, all_ref):
    half = mine_ref.shape[0]
    core = where_ref[3]
    all_ref[pl.ds(pl.multiple_of(core * half, half), half), :] = mine_ref[...]
    all_ref[pl.ds(pl.multiple_of((1 - core) * half, half), half), :] = theirs_ref[...]


def join_tokens(place, mine, theirs):
    shape = (2 * mine.shape[0], mine.shape[1])
    runner = call(
        join_kernel, (1,), [whole(mine.shape)] * 2, [whole(shape)], [out(shape, mine.dtype)],
        prefetch=1, nbytes=8 * mine.size,
    )
    return runner, (place, mine, theirs)


def stack_kernel(first_ref, second_ref, both_ref):
    both_ref[0] = first_ref[...]
    both_ref[1] = second_ref[...]


def stack(first, second):
    runner = call(
        stack_kernel, (1,), [whole(first.shape)] * 2, [whole((2, *first.shape))],
        [out((2, *first.shape), first.dtype)], nbytes=8 * first.size,
    )
    return runner, (first, second)


def spots(z, x):
    for kx in range(2):
        for kz in range(2):
            slab = (z ^ kz) * 2 + (x ^ kx)
            yield 0, kx, kz, slab, 0
            yield 1, kx, kz, slab, 1
    for ky in range(2):
        for kz in range(2):
            yield 2, ky, kz, (z ^ (2 + kz)) * 2 + x, ky
            yield 3, ky, kz, (z ^ (2 + kz)) * 2 + (x ^ 1), ky


def place_first_kernel(where_ref, p0, p1, p2, p3, wx_ref, wbc_ref, wdt_ref, count_ref, msg_ref, dts, *, slab):
    pieces = (p0, p1, p2, p3)
    cols = p0.shape[-1]
    z, x, y = where_ref[0], where_ref[1], where_ref[2]
    bc_rows = slab // 4
    total = jnp.zeros((8, 128), F32)
    for arr, i, j, dp, ky in spots(z, x):
        piece = pieces[arr]
        row0 = pl.multiple_of(dp * slab, slab)
        wx_ref[pl.ds(row0, slab), ky * cols : ky * cols + cols] = piece[i, j, 0:slab, :]
        bc0 = pl.multiple_of(dp * slab + (y ^ ky) * 2 * bc_rows, bc_rows)
        bc1 = pl.multiple_of(dp * slab + (y ^ ky) * 2 * bc_rows + bc_rows, bc_rows)
        wbc_ref[pl.ds(bc0, bc_rows), :] = piece[i, j, slab : slab + bc_rows, 0 : cols // 2]
        wbc_ref[pl.ds(bc1, bc_rows), :] = piece[i, j, slab : slab + bc_rows, cols // 2 : cols]
        extra = piece[i, j, slab + bc_rows : slab + bc_rows + 16, 0:slab].astype(F32)
        dts[ky * 8 : ky * 8 + 8, pl.ds(row0, slab)] = extra[0:8]
        total = total + extra[8:16]
    wdt_ref[...] = jnp.zeros_like(wdt_ref)
    wdt_ref[0:16, :] = dts[...].astype(BF)
    count_ref[...] = jnp.broadcast_to(jnp.sum(total[0:1], axis=1, keepdims=True), (8, 128))
    msg_ref[...] = count_ref[...]


def place_second_kernel(where_ref, p0, p1, p2, p3, wz_ref, wo_ref, *, slab):
    pieces = (p0, p1, p2, p3)
    cols = p0.shape[-1]
    for arr, i, j, dp, ky in spots(where_ref[0], where_ref[1]):
        row0 = pl.multiple_of(dp * slab, slab)
        piece = pieces[arr]
        wz_ref[pl.ds(row0, slab), ky * cols : ky * cols + cols] = piece[i, j, 0:slab, :]
        wo_ref[pl.ds(row0, slab), ky * cols : ky * cols + cols] = piece[i, j, slab : 2 * slab, :]


def first_block_kernel(where_ref, wx_ref, wbc_ref, wdt_ref, valid_ref, block_ref):
    slab, cols = wx_ref.shape
    bc_rows = slab // 4
    block_ref[0:slab, :] = wx_ref[...]
    start = pl.multiple_of(where_ref[2] * 2 * bc_rows, 2 * bc_rows)
    half = wbc_ref[pl.ds(start, 2 * bc_rows), :]
    block_ref[slab : slab + bc_rows, 0 : cols // 2] = half[0:bc_rows]
    block_ref[slab : slab + bc_rows, cols // 2 :] = half[bc_rows:]
    row_i = lax.broadcasted_iota(jnp.int32, (slab, slab), 0)
    col_i = lax.broadcasted_iota(jnp.int32, (slab, slab), 1)
    turn = jnp.where(row_i == col_i, 1.0, 0.0).astype(BF)
    ones = valid_ref[...].astype(F32)
    quarter = ones.shape[1] // 4
    lane = lax.broadcasted_iota(jnp.int32, (8, cols), 1)
    counts = jnp.zeros((8, cols), F32)
    for k in range(4):
        total = jnp.sum(ones[:, k * quarter : (k + 1) * quarter])
        counts = counts + jnp.where(lane == k, total, 0.0)
    row = lax.broadcasted_iota(jnp.int32, (8, cols), 0)
    steps = jnp.concatenate([dot_tn(wdt_ref[...], turn), jnp.zeros((8, cols - slab), F32)], axis=1)
    extra = jnp.concatenate([steps, jnp.where(row == 0, counts, 0.0)], axis=0)
    block_ref[slab + bc_rows :, :] = extra.astype(BF)


def first_block(moves, w_x, w_bc, w_dt, valid):
    slab, cols = w_x.shape
    operands = (w_x, w_bc, w_dt, valid)
    shape = (slab + slab // 4 + 16, cols)
    runner = call(
        first_block_kernel, (1,),
        [pl.BlockSpec(v.shape, lambda i, where: (0, 0)) for v in operands], [whole(shape)],
        [out(shape, BF)], prefetch=1, nbytes=4 * slab * cols, far_off=(0, 1, 2, 3),
    )
    return runner(moves.place, *operands)[0][0]


def place_first(moves, pieces, slab, bcw):
    cols = pieces[0].shape[-1]
    width = slab * moves.n_dp
    runner = call(
        functools.partial(place_first_kernel, slab=slab),
        (1,),
        [whole(p.shape) for p in pieces],
        [
            whole((width, 2 * cols)), whole((width, bcw)), whole((HEADS_PAD, width)),
            whole((8, 128)), whole((8, 128)),
        ],
        [
            out((width, 2 * cols), BF), out((width, bcw), BF), out((HEADS_PAD, width), BF),
            out((8, 128), F32), out((8, 128), F32),
        ],
        [pltpu.VMEM((16, width), F32)],
        prefetch=1, nbytes=8 * width * cols,
    )
    return runner, (moves.place, *pieces)


def place_second(moves, pieces, slab):
    cols = pieces[0].shape[-1]
    width = slab * moves.n_dp
    runner = call(
        functools.partial(place_second_kernel, slab=slab),
        (1,),
        [whole(p.shape) for p in pieces],
        [whole((width, 2 * cols)), whole((width, 2 * cols))],
        [out((width, 2 * cols), BF), out((width, 2 * cols), BF)],
        prefetch=1, nbytes=16 * width * cols,
    )
    return runner, (moves.place, *pieces)


def gather_any(moves, w_x, w_bc, w_dt, w_z, w_out, valid):
    wide = []
    for weight in (w_x, w_z, w_out):
        own = lax.all_gather(weight, "dp", axis=0, tiled=True)
        wide.append(jnp.concatenate([own, moves.swap(own, y=1)], axis=1))
    wbc = lax.all_gather(w_bc, "dp", axis=0, tiled=True)
    own = lax.all_gather(w_dt, "dp", axis=0, tiled=True).T
    both = jnp.concatenate([own, moves.swap(own, y=1)], axis=0)
    wdt = jnp.zeros((HEADS_PAD, both.shape[1]), BF).at[0 : both.shape[0]].set(both)
    count = lax.psum(jnp.sum(valid), AXES)
    return (*wide, wbc, wdt, jnp.full((8, 128), count, F32))


def split_rows(hold, z, x, cols, a_own, a_msg, b_own, b_msg, step, slab, at, stride):
    def slabs(k):
        base = (k ^ (z % 2)) * 2 * slab
        near = hold[pl.ds(pl.multiple_of(base + x * slab, slab), slab), :].astype(BF)
        far = hold[pl.ds(pl.multiple_of(base + (1 - x) * slab, slab), slab), :].astype(BF)
        first = slice(2 * k * stride + at, 2 * k * stride + at + slab)
        second = slice((2 * k + 1) * stride + at, (2 * k + 1) * stride + at + slab)
        return near, far, first, second

    @pl.when(step == 0)
    def _():
        for k in range(2):
            near, far, first, second = slabs(k)
            a_own[first, :] = near[:, 0:cols]
            a_own[second, :] = far[:, 0:cols]
            a_msg[first, :] = near[:, cols:]
            a_msg[second, :] = far[:, cols:]

    @pl.when(step == 1)
    def _():
        for k in range(2):
            near, far, first, second = slabs(k)
            b_own[first, :] = near[:, 0:cols]
            b_own[second, :] = near[:, cols:]
            b_msg[first, :] = far[:, 0:cols]
            b_msg[second, :] = far[:, cols:]


def row_sums(weight, grad):
    total = jnp.zeros((grad.shape[0], 128), F32)
    for col in range(0, grad.shape[1], 128):
        total += weight[:, col : col + 128].astype(F32) * grad[:, col : col + 128]
    ones = jnp.ones((8, 128), BF)
    high, rest = split_low(total)
    return (dot_nt(ones, high) + dot_nt(ones, rest))[0:1]


def two_grads_kernel(
    where_ref, n_ref, dz_ref, gs_ref, gsgot_ref, u_ref, wz_ref, a_own, a_msg, b_own, b_msg,
    gain_ref, hold, *, slab,
):
    step = pl.program_id(0)
    cols = a_own.shape[-1]
    x = where_ref[1]
    z = where_ref[0]
    pair = (z // 2) ^ step
    outs = (a_own, a_msg, b_own, b_msg)
    hold[...] = dot_tn(n_ref[...], dz_ref[...])
    gain_ref[pl.ds(pair, 1), :] = row_sums(wz_ref[...], hold)
    split_rows(hold, z, x, cols, *outs, step, slab, 0, 2 * slab)
    half = gs_ref.shape[0]
    core = where_ref[3]
    u_own = u_ref[pl.ds(pl.multiple_of(core * half, half), half), :]
    u_other = u_ref[pl.ds(pl.multiple_of((1 - core) * half, half), half), :]
    hold[...] = dot_tn(gs_ref[...], u_own) + dot_tn(gsgot_ref[...], u_other)
    split_rows(hold, z, x, cols, *outs, step, slab, slab, 2 * slab)


def two_grads(moves, n_full, dz, gs, gs_got, u, wz):
    toks, width = n_full.shape
    chans = dz.shape[1]
    cols = chans // 2
    slab = width // 8
    lane_block = pl.BlockSpec((toks, 4 * slab), lambda i, where: (0, (where[0] // 2) ^ i))
    half_block = pl.BlockSpec((toks // 2, 4 * slab), lambda i, where: (0, (where[0] // 2) ^ i))
    shapes = [out((8 * slab, cols), BF)] * 4 + [out((2, 4 * slab), F32)]
    runner = call(
        functools.partial(two_grads_kernel, slab=slab),
        (2,),
        [
            lane_block, whole(dz.shape), half_block, half_block, whole(u.shape),
            pl.BlockSpec((4 * slab, chans), lambda i, where: ((where[0] // 2) ^ i, 0)),
        ],
        [whole(v.shape) for v in shapes],
        shapes,
        [pltpu.VMEM((4 * slab, chans), F32)],
        prefetch=1, flops=4 * toks * width * chans, nbytes=16 * toks * chans,
    )
    return runner, (moves.place, n_full, dz, gs, gs_got, u, wz)


RIDE_VALUES = 16
RIDE_ROWS = 48


def last_grads_kernel(
    where_ref, n_ref, halo_ref, dx_ref, dxh_ref, dbc_ref, dbcgot_ref, dbch_ref, dbchgot_ref,
    hgrad_ref, hgradgot_ref, ddt_ref, wx_ref, wbc_ref, wdt_ref, gainz_ref, dcx_ref, dcbc_ref,
    dgate_ref, dskip_ref, dhead_ref, loss_ref, gain_ref, sum_ref,
    a_own, a_msg, b_own, b_msg, ride_ref, hold, hold_bc, dbc_high, dbc_rest, gains, dwdt, values,
    *, slab,
):
    step = pl.program_id(0)
    cols = a_own.shape[-1]
    z, x, y, core = where_ref[0], where_ref[1], where_ref[2], where_ref[3]
    pair = (z // 2) ^ step
    eighth = slab // 4
    stride = slab + eighth

    @pl.when(step == 0)
    def _():
        dbc_high[...], dbc_rest[...] = split_low(dbc_ref[...] + dbcgot_ref[...])

    n_now = n_ref[...]
    halo = halo_ref[...]
    hold[...] = dot_tn(n_now, dx_ref[...]) + dot_tn(halo, dxh_ref[...])
    dbch_sum = (dbch_ref[...].astype(F32) + dbchgot_ref[...].astype(F32)).astype(BF)
    grad_bc = dot_tn(n_now, dbc_high[...]) + dot_tn(n_now, dbc_rest[...]) + dot_tn(halo, dbch_sum)
    grad_dt = dot_tn(ddt_ref[...], n_now)
    slabs = pl.ds(pl.multiple_of(pair * 4 * slab, 4 * slab), 4 * slab)
    dwdt[:, slabs] = grad_dt[0:16]
    sums = row_sums(wx_ref[...], hold) + 0.5 * row_sums(wbc_ref[...], grad_bc)
    sums += jnp.sum(grad_dt * wdt_ref[...].astype(F32), axis=0, keepdims=True)
    gains[0:1, slabs] = sums + gainz_ref[pl.ds(pair, 1), :]
    split_rows(hold, z, x, cols, a_own, a_msg, b_own, b_msg, step, slab, 0, stride)
    hold_bc[...] = grad_bc

    def bc_block(k, kx):
        base = (k ^ (z % 2)) * 2 * slab
        start = pl.multiple_of(base + (x ^ kx) * slab + core * 2 * eighth, eighth)
        block = hold_bc[pl.ds(start, 2 * eighth), :].astype(BF)
        return jnp.concatenate([block[0:eighth], block[eighth:]], axis=1)

    def bc_rows(k, i):
        return slice((2 * k + i) * stride + slab, (2 * k + i) * stride + slab + eighth)

    @pl.when(step == 0)
    def _():
        for k in range(2):
            for i in range(2):
                a_own[bc_rows(k, i), :] = bc_block(k, i)
                a_msg[bc_rows(k, i), :] = bc_block(k, i)

    @pl.when(step == 1)
    def _():
        for k in range(2):
            for i in range(2):
                b_own[bc_rows(k, i), :] = bc_block(k, 0)
                b_msg[bc_rows(k, i), :] = bc_block(k, 1)

    @pl.when(step == pl.num_programs(0) - 1)
    def _():
        values[...] = jnp.zeros_like(values)

        def per_channel(row, step_rows, total):
            mine, others = total[:, 0:cols], total[:, cols:]
            first_chip = jnp.where(y == 0, mine, others)
            second_chip = jnp.where(y == 0, others, mine)
            values[row : row + 1, :] = first_chip
            values[row + step_rows : row + step_rows + 1, :] = second_chip

        for k in range(4):
            per_channel(k, 4, jnp.sum(dcx_ref[8 * k : 8 * k + 8, :], axis=0, keepdims=True))
            values[12 + k // 2 : 13 + k // 2, (k % 2) * 256 : (k % 2) * 256 + 256] = jnp.sum(
                dcbc_ref[8 * k : 8 * k + 8, :], axis=0, keepdims=True
            )
        per_channel(8, 1, jnp.sum(dgate_ref[...], axis=0, keepdims=True))
        gain_total = gains[0:1, :] / gain_ref[...]
        values[10:11, :] = gain_total[:, 0:cols]
        values[11:12, :] = gain_total[:, cols:]
        skips = per_head(dskip_ref[...], sum_ref[...])
        heads = [
            jnp.sum(v, axis=0, keepdims=True)
            for v in (dhead_ref[0:8, :], dhead_ref[8:16, :], skips)
        ]
        loss = jnp.sum(loss_ref[...]) * jnp.where(
            lax.broadcasted_iota(jnp.int32, (1, 128), 1) == 0, 1.0, 0.0
        )
        for k, value in enumerate(heads):
            at = slice(k * 128, k * 128 + 128)
            turned_value = pltpu.roll(jnp.broadcast_to(value, (8, 128)), 120, 1)[0:1]
            values[14:15, at] = jnp.where(y == 0, value, turned_value)
            values[15:16, at] = jnp.where(y == 0, turned_value, value)
        values[14:15, 384:512] = jnp.where(y == 0, loss, 0.0)
        values[15:16, 384:512] = jnp.where(y == 0, 0.0, loss)
        sums_now = values[...]
        row = lax.broadcasted_iota(jnp.int32, sums_now.shape, 0)
        ride_ref[0:16, :] = jnp.where(
            row >= RIDE_VALUES - 2, two_parts(sums_now).astype(F32), sums_now
        ).astype(BF)
        grads = dwdt[...]
        turned_grads = jnp.concatenate([grads[8:16], grads[0:8]], axis=0)
        grads = jnp.where(y == 0, grads, turned_grads).astype(BF)
        ride_ref[16:32, :] = grads[:, 0:cols]
        ride_ref[32:48, :] = grads[:, cols:]
        a_msg[4 * stride : 4 * stride + RIDE_ROWS, :] = ride_ref[...]
        edge = add_low(hgrad_ref[...], hgradgot_ref[...])
        for k in range(2):
            at = 4 * stride + RIDE_ROWS + k * HALO
            a_msg[at : at + HALO, :] = edge[:, k * cols : (k + 1) * cols]


def last_grads(moves, n_full, halo, dxin, dxh, dbcs, edges, ddt, wx, wbc, wdt, small):
    toks, width = n_full.shape
    chans = dxin.shape[1]
    bcw = dbcs[0].shape[1]
    cols = chans // 2
    slab = width // 8
    stride = slab + slab // 4
    lane_block = pl.BlockSpec((toks, 4 * slab), lambda i, where: (0, (where[0] // 2) ^ i))
    shapes = [
        out((4 * stride, cols), BF), out((4 * stride + RIDE_ROWS + 2 * HALO, cols), BF),
        out((4 * stride, cols), BF), out((4 * stride, cols), BF), out((RIDE_ROWS, cols), BF),
    ]
    runner = call(
        functools.partial(last_grads_kernel, slab=slab),
        (2,),
        [
            lane_block, pl.BlockSpec((HALO, 4 * slab), lambda i, where: (0, (where[0] // 2) ^ i)),
            whole(dxin.shape), whole(dxh.shape),
            *[whole(v.shape) for v in (*dbcs, *edges)], whole(ddt.shape),
            pl.BlockSpec((4 * slab, chans), lambda i, where: ((where[0] // 2) ^ i, 0)),
            pl.BlockSpec((4 * slab, bcw), lambda i, where: ((where[0] // 2) ^ i, 0)),
            pl.BlockSpec((HEADS_PAD, 4 * slab), lambda i, where: (0, (where[0] // 2) ^ i)),
            *[whole(v.shape) for v in small],
        ],
        [whole(v.shape) for v in shapes],
        shapes,
        [
            pltpu.VMEM((4 * slab, chans), F32), pltpu.VMEM((4 * slab, bcw), F32),
            pltpu.VMEM((toks, bcw), BF), pltpu.VMEM((toks, bcw), BF), pltpu.VMEM((8, width), F32), pltpu.VMEM((16, width), F32),
            pltpu.VMEM((RIDE_VALUES, cols), F32),
        ],
        prefetch=1, flops=2 * toks * width * chans, nbytes=16 * toks * chans,
    )
    return runner, (
        moves.place, n_full, halo, dxin, dxh, *dbcs, *edges, ddt, wx, wbc, wdt, *small
    )


def add_low(first, second):
    return (first.astype(F32) + second.astype(F32)).astype(BF)


LOSS_LANE = 384


def two_parts(values):
    lane = lax.broadcasted_iota(jnp.int32, values.shape, 1)
    rest = pltpu.roll(values - values.astype(BF).astype(F32), 1, 1)
    return jnp.where(lane == LOSS_LANE + 1, rest, values).astype(BF)


def join_parts(ride):
    values = ride.astype(F32)
    lane = lax.broadcasted_iota(jnp.int32, values.shape, 1)
    last = lane == LOSS_LANE + 1
    whole_loss = values + jnp.where(
        lane == LOSS_LANE, pltpu.roll(values, values.shape[1] - 1, 1), 0.0
    )
    row = lax.broadcasted_iota(jnp.int32, values.shape, 0)
    tail = row >= RIDE_VALUES - 2
    return jnp.where(tail, jnp.where(last, 0.0, whole_loss), values)


def add_ride(first, second):
    total = join_parts(first[0:16]) + join_parts(second[0:16])
    row = lax.broadcasted_iota(jnp.int32, total.shape, 0)
    sums = jnp.where(row >= RIDE_VALUES - 2, two_parts(total).astype(F32), total).astype(BF)
    return jnp.concatenate([sums, add_low(first[16:], second[16:])], axis=0)


def fold_first_kernel(*refs, stride, ride):
    if ride:
        a_own, a_got, b_own, b_got, ride_ref, a_keep, a_msg, b_keep, b_msg, ride_out, edge = refs
    else:
        a_own, a_got, b_own, b_got, a_keep, a_msg, b_keep, b_msg = refs
    for own, got, keep, msg in ((a_own, a_got, a_keep, a_msg), (b_own, b_got, b_keep, b_msg)):
        for z in range(2):
            to = slice(z * stride, (z + 1) * stride)
            for i, dest in enumerate((keep, msg)):
                at = slice((2 * z + i) * stride, (2 * z + i + 1) * stride)
                dest[to, :] = add_low(own[at, :], got[at, :])
    if ride:
        total = add_ride(ride_ref[...], a_got[4 * stride : 4 * stride + RIDE_ROWS, :])
        ride_out[...] = total
        a_msg[2 * stride : 2 * stride + RIDE_ROWS, :] = total
        edge[...] = a_got[4 * stride + RIDE_ROWS :, :]


def fold_first(stride, a_own, a_got, b_own, b_got, ride=None):
    cols = a_own.shape[-1]
    n_ride = 0 if ride is None else RIDE_ROWS
    operands = (a_own, a_got, b_own, b_got) + (() if ride is None else (ride,))
    shapes = [
        out((2 * stride, cols), BF), out((2 * stride + n_ride, cols), BF),
        out((2 * stride, cols), BF), out((2 * stride, cols), BF),
    ] + ([] if ride is None else [out((RIDE_ROWS, cols), BF), out((2 * HALO, cols), BF)])
    runner = call(
        functools.partial(fold_first_kernel, stride=stride, ride=n_ride > 0),
        (1,), [whole(v.shape) for v in operands], [whole(v.shape) for v in shapes], shapes,
        nbytes=24 * stride * cols,
    )
    return runner, operands


def fold_second_kernel(*refs, stride, ride):
    if ride:
        a_own, a_got, b_own, b_got, ride_ref, own, far, msg, ride_out = refs
    else:
        a_own, a_got, b_own, b_got, own, far, msg = refs
    low, high = slice(0, stride), slice(stride, 2 * stride)
    own[...] = add_low(a_own[low, :], a_got[low, :])
    far[...] = add_low(b_own[low, :], b_got[low, :])
    msg[low, :] = add_low(a_own[high, :], a_got[high, :])
    msg[high, :] = add_low(b_own[high, :], b_got[high, :])
    if ride:
        total = add_ride(ride_ref[...], a_got[2 * stride : 2 * stride + RIDE_ROWS, :])
        ride_out[...] = total
        msg[2 * stride : 2 * stride + RIDE_ROWS, :] = total


def fold_second(stride, a_own, a_got, b_own, b_got, ride=None):
    cols = a_own.shape[-1]
    n_ride = 0 if ride is None else RIDE_ROWS
    operands = (a_own, a_got, b_own, b_got) + (() if ride is None else (ride,))
    shapes = [out((stride, cols), BF)] * 2 + [out((2 * stride + n_ride, cols), BF)]
    if ride is not None:
        shapes = shapes + [out((RIDE_ROWS, cols), BF)]
    runner = call(
        functools.partial(fold_second_kernel, stride=stride, ride=n_ride > 0),
        (1,), [whole(v.shape) for v in operands], [whole(v.shape) for v in shapes], shapes,
        nbytes=16 * stride * cols,
    )
    return runner, operands


def fold_third_kernel(*refs, stride, ride):
    if ride:
        own, far, got, ride_ref, keep, msg, ride_out = refs
    else:
        own, far, got, keep, msg = refs
    keep[...] = add_low(own[...], got[0:stride, :])
    msg[0:stride, :] = add_low(far[...], got[stride : 2 * stride, :])
    if ride:
        total = add_ride(ride_ref[...], got[2 * stride : 2 * stride + RIDE_ROWS, :])
        ride_out[...] = total
        msg[stride : stride + RIDE_ROWS, :] = total


def fold_third(stride, own, far, got, ride=None):
    cols = own.shape[-1]
    n_ride = 0 if ride is None else RIDE_ROWS
    operands = (own, far, got) + (() if ride is None else (ride,))
    shapes = [out((stride, cols), BF), out((stride + n_ride, cols), BF)]
    if ride is not None:
        shapes = shapes + [out((RIDE_ROWS, cols), BF)]
    runner = call(
        functools.partial(fold_third_kernel, stride=stride, ride=n_ride > 0),
        (1,), [whole(v.shape) for v in operands], [whole(v.shape) for v in shapes], shapes,
        nbytes=8 * stride * cols,
    )
    return runner, operands


def fold_two_kernel(own, got, first, second):
    slab = first.shape[0]
    for at, dest in ((0, first), (slab, second)):
        dest[...] = own[at : at + slab, :].astype(F32) + got[at : at + slab, :].astype(F32)


def fold_two(own, got):
    rows_all, cols = own.shape
    shapes = [jax.ShapeDtypeStruct((rows_all // 2, cols), F32)] * 2
    runner = call(
        fold_two_kernel, (1,), [whole(own.shape)] * 2, [whole(v.shape) for v in shapes], shapes,
        nbytes=12 * rows_all * cols,
    )
    return runner, (own, got)


def fold_last_kernel(
    where_ref, own, got, ride, wx_ref, cx_ref, gate_ref, heads_ref, dt_ref, swap_ref,
    values, dts, *, slab,
):
    stride = own.shape[0]
    total = own[...].astype(F32) + got[0:stride, :].astype(F32)
    wx_ref[...] = total[0:slab]
    values[...] = join_parts(ride[0:16, :]) + join_parts(got[stride : stride + 16, :])
    dts[...] = ride[16:48, :].astype(F32) + got[stride + 16 : stride + 48, :].astype(F32)
    y, z, x = where_ref[2], where_ref[0], where_ref[1]
    sums = values[...]
    cx_ref[...] = jnp.where(y == 0, sums[0:4], sums[4:8])
    gate_ref[...] = jnp.where(y == 0, sums[8:9], sums[9:10])
    heads_ref[...] = jnp.where(y == 0, sums[14:15], sums[15:16])
    slabs = dts.shape[1] // slab
    picked = jnp.zeros((8, slab), F32)
    for dp in range(2 * slabs):
        at = (dp % slabs) * slab
        block = dts[(dp // slabs) * 16 : (dp // slabs) * 16 + 16, at : at + slab]
        block = jnp.where(y == 0, block[0:8], block[8:16])
        picked = picked + jnp.where(z * 2 + x == dp, block, 0.0)
    dt_ref[...] = jnp.concatenate([picked, jnp.zeros((slab - 8, slab), F32)], axis=0).T[:, 0:8]
    swap_ref[0 : stride - slab, :] = total[slab:stride]
    swap_ref[stride - slab : stride - slab + 8, :] = jnp.concatenate(
        [sums[10:14], sums[14:16], jnp.zeros_like(sums[0:2])], axis=0
    )


def end_kernel(where_ref, mine, theirs, bc_ref, conv_ref, gain_ref, loss_ref):
    n_bc = mine.shape[0] - 8
    bcw = bc_ref.shape[1]
    core = where_ref[3]
    for part, at in ((mine, core), (theirs, 1 - core)):
        for k in range(2):
            row0 = pl.multiple_of((at * 2 + k) * n_bc, n_bc)
            bc_ref[pl.ds(row0, n_bc), :] = part[0:n_bc, k * bcw : (k + 1) * bcw]
    shared = mine[n_bc:, :] + theirs[n_bc:, :]
    for k in range(2):
        gain_ref[:, k * 2 * bcw : (k + 1) * 2 * bcw] = shared[k : k + 1]
    for k in range(4):
        conv_ref[k : k + 1, :] = shared[2 + k // 2 : 3 + k // 2, (k % 2) * bcw : (k % 2 + 1) * bcw]
    loss_ref[...] = shared[4:5, LOSS_LANE : LOSS_LANE + 1] + shared[5:6, LOSS_LANE : LOSS_LANE + 1]


def finish(place, mine, theirs, slab, bcw):
    shapes = [
        jax.ShapeDtypeStruct((slab, bcw), F32), jax.ShapeDtypeStruct((4, bcw), F32),
        jax.ShapeDtypeStruct((1, 4 * bcw), F32), jax.ShapeDtypeStruct((1, 1), F32),
    ]
    runner = call(
        end_kernel, (1,), [whole(mine.shape)] * 2, [whole(v.shape) for v in shapes], shapes,
        prefetch=1, nbytes=4 * slab * bcw,
    )
    return runner, (place, mine, theirs)


def fold_last(place, slab, own, got, ride):
    stride, cols = own.shape
    shapes = [
        jax.ShapeDtypeStruct((slab, cols), F32), jax.ShapeDtypeStruct((4, cols), F32),
        out((1, cols), F32), out((1, cols), F32), jax.ShapeDtypeStruct((slab, 8), F32),
        out((stride - slab + 8, cols), F32),
    ]
    operands = (own, got, ride)
    runner = call(
        functools.partial(fold_last_kernel, slab=slab), (1,),
        [whole(v.shape) for v in operands], [whole(v.shape) for v in shapes], shapes,
        [pltpu.VMEM((RIDE_VALUES, cols), F32), pltpu.VMEM((32, cols), F32)],
        prefetch=1, nbytes=20 * stride * cols,
    )
    return runner, (place, *operands)


def body(
    residual, teacher, valid_mask, gain_in, w_z, w_x, w_bc, w_dt, conv_x, conv_bc, dt_bias, a_log,
    d_skip, gain_gate, w_out,
):
    _, pos_dev, width = residual.shape
    n_tensor = lax.axis_size("tensor")
    n_dp = lax.axis_size("dp")
    moves = Moves(n_dp, n_tensor)
    tokens_all = pos_dev * n_tensor * n_dp
    cols = w_z.shape[1]
    chans = 2 * cols
    own_heads = w_dt.shape[1]
    heads = 2 * own_heads
    inner = cols * n_tensor
    bcw = w_bc.shape[1]
    slab = w_z.shape[0]
    toks = 2 * pos_dev
    core = moves.core
    nb = toks // BLOCK
    by_permutes = n_dp == 8
    res_rows = residual.reshape(pos_dev, width)

    valid = valid_mask.reshape(pos_dev).astype(F32)
    if by_permutes:
        block1 = first_block(moves, w_x, w_bc, w_dt, valid_mask)
        others1 = [moves.swap(block1, z=k) for k in (1, 2, 3)]
        block2 = jnp.concatenate([w_z, w_out], axis=0)

    pack = jnp.concatenate(
        [
            conv_x, gain_gate[None],
            jnp.concatenate(
                [dt_bias, a_log, d_skip, jnp.zeros((cols - 3 * own_heads,), F32)]
            )[None],
            jnp.zeros((2, cols), F32),
            res_rows[pos_dev - HALO // 2 :].astype(F32).reshape(-1, cols),
        ],
        axis=0,
    )
    pack_other = moves.swap(pack, y=1)
    rows_ahead = pack_other[8:].reshape(HALO // 2, width)
    rows_ahead = jnp.where(core == 1, rows_ahead, moves.swap(rows_ahead, c=1))
    conv_x_core = jnp.concatenate([pack[0:4], pack_other[0:4]], axis=1)
    gain_row = jnp.concatenate([pack[4:5], pack_other[4:5]], axis=1)

    def head_param(k):
        at = slice(k * own_heads, (k + 1) * own_heads)
        return jnp.concatenate([pack[5, at], pack_other[5, at]])

    def pad_heads(values):
        return jnp.concatenate([values, jnp.zeros((HEADS_PAD - heads,), F32)])

    bias_col = pad_heads(head_param(0))[:, None]
    rates = pad_heads(-jnp.exp(head_param(1)))
    skip_row = jnp.repeat(head_param(2), HP)[None]
    head_of = (jnp.arange(chans) // HP)[None, :]
    lanes = jnp.arange(HEADS_PAD)[:, None]

    def norm(values):
        factor = lax.rsqrt(jnp.mean(values * values, axis=-1, keepdims=True) + EPSILON)
        return (values * factor * gain_in).astype(BF)

    normed = norm(res_rows.astype(F32))
    normed_other = moves.swap(normed, c=1)
    halo_rows = jnp.where(moves.row == 1, norm(rows_ahead), jnp.zeros((), BF))
    halo_rows = jnp.concatenate([jnp.zeros_like(halo_rows), halo_rows], axis=0)

    ch = Chain()
    halo = ch.hold(halo_rows)
    spread = ch.hold((lanes % (HEADS_PAD // 2) == head_of).astype(BF))
    sum_mat = ch.hold((lanes == head_of).astype(BF).T)
    conv_xs, conv_bcs, bias, rate_col, rate_row, skip, gain, gain_ins, valid_col = ch.hold(
        conv_x_core, conv_bc, bias_col, rates[:, None], rates[None, :], skip_row, gain_row,
        gain_in[None], valid[:, None],
    )
    n = ch.run(join_tokens(moves.place, normed, normed_other))

    def stacked(first, second):
        return ch.drop(ch.run(stack(first, second)))

    if by_permutes:
        a1 = stacked(block1, others1[0])
        a1x = moves.swap(a1, x=1)
        block2_held = ch.hold(block2)
        b1 = stacked(others1[1], others1[2])
        b1y = moves.swap(b1, y=1)
        block2 = ch.drop(block2_held)
        others2 = [moves.swap(block2, z=k) for k in (1, 2, 3)]
        a1, a1x, b1y, others2[0] = lax.optimization_barrier((a1, a1x, b1y, others2[0]))
        a1 = stacked(a1, a1x)
        a1y = moves.swap(a1, y=1)
        b1 = stacked(b1, b1y)
        b1x = moves.swap(b1, x=1)
        wx, wbc, wdt, count, count_msg = ch.run(
            place_first(moves, (a1, a1y, b1, b1x), slab, bcw)
        )
        count_other = moves.swap(ch.drop(count_msg), c=1)
        a2 = stacked(block2, others2[0])
        b2 = stacked(others2[1], others2[2])
        a2x = moves.swap(a2, x=1)
        b2y = moves.swap(b2, y=1)
    else:
        *weights, counted = gather_any(moves, w_x, w_bc, w_dt, w_z, w_out, valid)
        wx, wz, wo, wbc, wdt, count = ch.hold(*weights, counted)
        count_other = jnp.zeros_like(counted)

    def run_front(first, count_, wide, passed):
        carried = ch.drop(*passed, *wide) if first else ()
        results = ch.run(
            front(
                first, count_,
                *now(n, halo, wx, wbc, wdt, conv_xs, conv_bcs, bias, rate_col, spread), carried,
            )
        )
        return results[:8], ch.drop(*results[8:12]), results[12:16], results[16], results[17:]

    front_split = FRONT_SPLIT if by_permutes else nb
    wide, first_part, passed, end, (x_halo, bc_halo) = run_front(0, front_split, (), ())
    last_part = first_part
    if by_permutes:
        a2 = stacked(a2, a2x)
        a2y = moves.swap(a2, y=1)
        b2 = stacked(b2, b2y)
        b2x = moves.swap(b2, x=1)
    if front_split < nb:
        ch.drop(end)
        wide, last_part, passed, end, unused = run_front(
            front_split, nb - front_split, wide, passed
        )
        ch.drop(*unused)
    ch.drop(*passed)
    xc, bcc, dt, a_cols, ahead, a_rows, y, saved = wide
    start_got = moves.up(ch.drop(end))
    if by_permutes:
        wz, wo = ch.run(place_second(moves, (a2, a2y, b2, b2x), slab))
    start = ch.hold(start_got)

    given = (n, y, xc, bcc, a_cols, ahead, start, wz, wo, skip, gain, spread)
    gate, far, far_sq = ch.run(gate_out_proj(True, moves.place, *now(*given)))
    far_got = moves.swap(ch.drop(far), c=1)
    sq_got = moves.swap(ch.drop(far_sq), c=1)
    gate_value = ch.drop(gate)
    gate, near, near_sq = ch.run(
        gate_out_proj(False, moves.place, *now(*given), in_place=(gate_value,))
    )
    mixed, grad_result, gs, gs_msg, q, loss_part = ch.run(
        loss_step(
            ch.drop(near), far_got, ch.drop(near_sq), sq_got, res_rows,
            teacher.reshape(pos_dev, width), ch.drop(valid_col), count.value, count_other, inner,
            tokens_all,
        )
    )
    mixed, grad_result = ch.drop(mixed, grad_result)
    gs_got = moves.swap(ch.drop(gs_msg), c=1)
    q_got = moves.swap(q.value, c=1)
    given = (wo, y, xc, gate, a_cols, ahead, bcc, start, skip, gain, spread, sum_mat)
    q_value = ch.drop(q)
    dz, dy, rowdot, u, dstart, dgate, dskip, dlow = ch.run(
        gate_backward(moves.place, gs.value, q_value, *now(*given))
    )
    ch.drop(dlow)
    in_place = ch.drop(dz, dy, rowdot, u)
    sums = ch.drop(dstart, dgate, dskip)
    operands = now(*given)
    ch.drop(gate, wo, y)
    gs_other = ch.hold(gs_got)
    dz, dy, rowdot, u, dstart, dgate, dskip, dlow = ch.run(
        gate_backward(moves.place, gs_got, q_got, *operands, sums=sums, in_place=in_place)
    )
    ch.drop(dstart)
    dend = moves.down(ch.drop(dlow))

    if by_permutes:
        prepared = two_grads(moves, *now(n, dz, gs, gs_other, u, wz))
        ch.drop(gs, gs_other, u)
        za, za_msg, zb, zb_msg, gain_z = ch.run(prepared)
        za_sent, zb_sent, dend = lax.optimization_barrier((*ch.drop(za_msg, zb_msg), dend))
        za_got = moves.swap(za_sent, y=1)
        zb_got = moves.swap(zb_sent, x=1)
    else:
        grad_z = dot_tn(n.value, dz.value)
        gs_all = jnp.where(
            core == 0,
            jnp.concatenate(now(gs, gs_other), axis=0),
            jnp.concatenate(now(gs_other, gs), axis=0),
        )
        grad_o = dot_tn(gs_all, u.value)
        ch.drop(gs, gs_other, u)

    first_given = (xc, bcc, dt, a_cols, ahead, a_rows, dy, rowdot, saved)
    last_given = (
        x_halo, bc_halo, start, conv_xs, conv_bcs, skip, rate_row, spread, sum_mat, wx, wbc,
    )

    def run_back(top, count_, base, part, whole_out, carried):
        whole_out = ch.drop(*whole_out) if whole_out else ()
        carried = ch.drop(*carried) if carried else ()
        prepared = scan_backward(
            top, count_, base, *now(*first_given), *part, *now(*last_given), dend, carried,
            whole_out,
        )
        if top + 1 == count_:
            ch.drop(*first_given, *last_given[:-4])
        results = ch.run(prepared)
        return results[:3], results[3:6], results[6:]

    back_split = nb - front_split if by_permutes else nb
    whole_out, edges, carried = run_back(nb - 1, back_split, nb - back_split, last_part, (), ())
    if back_split < nb:
        ch.drop(*edges)
        whole_out, edges, carried = run_back(
            nb - 1 - back_split, nb - back_split, 0, first_part, whole_out, carried
        )
    dxin, dbc, ddt = whole_out
    dxh, dbch, halo_out = edges
    dcx, dcbc, dhead = carried[:3]
    ch.drop(*carried[3:])

    if by_permutes:
        za, za_msg, zb, zb_msg = ch.run(
            fold_first(2 * slab, ch.drop(za), za_got, ch.drop(zb), zb_got)
        )
        za_got = moves.swap(ch.drop(za_msg), x=1)
        zb_got = moves.swap(ch.drop(zb_msg), y=1)
        dbc_got = moves.swap(dbc.value, c=1)
        dbch_got = moves.swap(dbch.value, c=1)
        halo_got = moves.swap(halo_out.value, c=1)
        small = ch.drop(gain_z, dcx, dcbc, dgate, dskip, dhead, loss_part)
        small += now(gain_ins, sum_mat)
        prepared = last_grads(
            moves, *now(n, halo, dxin, dxh), (dbc.value, dbc_got, dbch.value, dbch_got),
            (halo_out.value, halo_got), *now(ddt, wx, wbc, wdt), small,
        )
        ch.drop(n, halo, dxh, dbch, halo_out)
        xa, xa_msg, xb, xb_msg, ride = ch.run(prepared)
        xb_got = moves.swap(ch.drop(xb_msg), x=1)
        xa_got = moves.swap(ch.drop(xa_msg), y=1)
        z_own, z_far, z_msg = ch.run(
            fold_second(2 * slab, ch.drop(za), za_got, ch.drop(zb), zb_got)
        )
        z_got = moves.swap(ch.drop(z_msg), z=1)
    else:
        halo_sum = moves.down(add_low(halo_out.value, moves.swap(halo_out.value, c=1)))
        grad_x = dot_tn(n.value, dxin.value) + dot_tn(halo.value, dxh.value)
        grad_bc = dot_tn(n.value, dbc.value.astype(BF)) + dot_tn(halo.value, dbch.value)
        grad_dt = dot_tn(ddt.value, n.value)[0:heads]
        gain_sum = jnp.sum(wz.value.astype(F32) * grad_z, axis=1)
        gain_sum += jnp.sum(wx.value.astype(F32) * grad_x, axis=1)
        gain_sum += jnp.sum(wbc.value.astype(F32) * grad_bc, axis=1)
        gain_sum += jnp.sum(wdt.value[0:heads].astype(F32) * grad_dt, axis=0)

    given = (dz, dxin, dbc, ddt)
    weights = (wz, wx, wbc, wdt)
    far = ch.run(input_grad(True, moves.place, *now(*given), *now(*weights)))
    far_got = moves.swap(ch.drop(far), c=1)
    prepared = input_grad(False, moves.place, *now(*given), *now(*weights))
    ch.drop(*given, *weights)
    near = ch.run(prepared)
    stride = slab + slab // 4
    if by_permutes:
        xa, xa_msg, xb, xb_msg, ride, edge = ch.run(
            fold_first(stride, ch.drop(xa), xa_got, ch.drop(xb), xb_got, ch.drop(ride))
        )
        xa_got = moves.swap(ch.drop(xa_msg), x=1)
        xb_got = moves.swap(ch.drop(xb_msg), y=1)
    else:
        edge = ch.hold(jnp.concatenate([halo_sum[:, :cols], halo_sum[:, cols:]], axis=0))
    grad_residual = ch.drop(
        ch.run(
            norm_backward(
                moves.place, ch.drop(near), far_got, res_rows, gain_ins.value, ch.drop(edge),
                grad_result,
            )
        )
    )
    count_total = count.value[0, 0] + count_other[0, 0]

    if by_permutes:
        z_own, z_msg = ch.run(fold_third(2 * slab, ch.drop(z_own), ch.drop(z_far), z_got))
        z_got = moves.swap(ch.drop(z_msg), z=2)
        x_own, x_far, x_msg, ride = ch.run(
            fold_second(stride, ch.drop(xa), xa_got, ch.drop(xb), xb_got, ch.drop(ride))
        )
        x_got = moves.swap(ch.drop(x_msg), z=1)
        x_own, x_msg, ride = ch.run(
            fold_third(stride, ch.drop(x_own), ch.drop(x_far), x_got, ch.drop(ride))
        )
        grad_w_z, grad_w_out = ch.drop(*ch.run(fold_two(ch.drop(z_own), z_got)))
        x_got = moves.swap(ch.drop(x_msg), z=2)
        grad_w_x, g_conv_x, g_gate, g_heads, g_dt, mine = ch.drop(
            *ch.run(fold_last(moves.place, slab, ch.drop(x_own), x_got, ch.drop(ride)))
        )
        theirs = moves.swap(mine, c=1)
        grad_w_bc, grad_conv_bc, gain_sums, loss_sum = ch.drop(
            *ch.run(finish(moves.place, mine, theirs, slab, bcw))
        )
        grad_gain_in = gain_sums[0]
        loss = loss_sum[0, 0] / (count_total * width)
        g_bias, g_log, g_skip = [
            g_heads[0, at : at + own_heads] for at in (0, HEADS_PAD, 2 * HEADS_PAD)
        ]
        g_gain_gate = g_gate[0]
    else:

        def in_order(values):
            half = values.shape[-1] // 2
            turn = jnp.concatenate([values[..., half:], values[..., :half]], axis=-1)
            return jnp.where(moves.row == 0, values, turn)

        small = [
            in_order(dcx.value.reshape(4, 8, chans).sum(axis=1)),
            in_order(dgate.value.sum(axis=0)),
            in_order(dhead.value[0:8, 0:heads].sum(axis=0)),
            in_order(dhead.value[8:16, 0:heads].sum(axis=0)),
            in_order(dskip.value.sum(axis=0).reshape(heads, HP).sum(axis=1)),
            in_order(grad_dt.T),
        ]
        shared = [
            dcbc.value.reshape(4, 8, bcw).sum(axis=1), loss_part.value.sum(), gain_sum / gain_in,
        ]
        big = jnp.stack([grad_z, grad_o, grad_x])
        big = big[:, :, :cols] + moves.swap(big[:, :, cols:], y=1)
        big = lax.psum_scatter(big, "dp", scatter_dimension=1, tiled=True)
        grad_w_z, grad_w_out, grad_w_x = big[0], big[1], big[2]
        grad_w_bc = lax.psum_scatter(
            lax.psum(grad_bc, "tensor"), "dp", scatter_dimension=0, tiled=True
        )
        sums = lax.psum(jnp.concatenate([v.reshape(-1) for v in small + shared]), "dp")
        sums = sums + moves.swap(sums, y=1)
        done = []
        at = 0
        for value in small:
            part = sums[at : at + value.size].reshape(value.shape)
            half = value.shape[-1] // 2
            done.append(
                lax.dynamic_slice_in_dim(part, moves.row * half, half, value.ndim - 1)
            )
            at += value.size
        g_conv_x, g_gain_gate, g_bias, g_log, g_skip, g_dt = done
        g_dt = lax.dynamic_slice_in_dim(g_dt, moves.dp * slab, slab, 0)
        tail = sums[at:]
        tail = tail + moves.swap(tail, c=1)
        n_conv = 4 * bcw
        grad_conv_bc = tail[:n_conv].reshape(4, bcw)
        loss = tail[n_conv] / (count_total * width)
        grad_gain_in = tail[n_conv + 1 :]
    return (
        mixed[None], loss, grad_residual[None], grad_gain_in, grad_w_z, grad_w_x, grad_w_bc, g_dt,
        g_conv_x, grad_conv_bc, g_bias, g_log, g_skip, g_gain_gate, grad_w_out,
    )


def solution(mesh):
    both = P("dp", "tensor")
    tokens = P("dp", "tensor", None)
    return jax.shard_map(
        body,
        mesh=mesh,
        in_specs=(
            tokens, tokens, both, P(), both, both, P("dp", None), both, P(None, "tensor"), P(),
            P("tensor"), P("tensor"), P("tensor"), P("tensor"), both,
        ),
        out_specs=(
            tokens, P(), tokens, P(), both, both, P("dp", None), both, P(None, "tensor"), P(),
            P("tensor"), P("tensor"), P("tensor"), P("tensor"), both,
        ),
        check_vma=False,
    )
```
